32 devices in a mesh: fsdp: 8 (over y, x, core), sp: 4 (over z).
Axes of the slice: x: 2, y: 2, z: 4, core: 2. Of those that a mesh axis runs over, the one named last changes fastest.
Arguments:
- tokens: bfloat16 [64, 512, 1024], P('fsdp', 'sp'), may hold values from -6 to 6
- validity: int32 [64, 512], P('fsdp'), may hold values from 0 to 1, as said below
- teacher: bfloat16 [64, 512, 1024], P('fsdp', 'sp'), may hold values from -18 to 18
- query_matrix: bfloat16 [1024, 1024], P(('fsdp', 'sp')), may hold values from -0.1875 to 0.1875
- query_offset_bias: bfloat16 [1024], P(('fsdp', 'sp')), may hold values from -2 to 2
- key_matrix: bfloat16 [1024, 1024], P(('fsdp', 'sp')), may hold values from -0.1875 to 0.1875
- value_matrix: bfloat16 [1024, 1024], P(('fsdp', 'sp')), may hold values from -0.1875 to 0.1875
- value_offset_bias: bfloat16 [1024], P(('fsdp', 'sp')), may hold values from -0.29882812 to 0.29882812
- attention_output_weight: bfloat16 [1024, 1024], P(('fsdp', 'sp')), may hold values from -1.5 to 1.5
- attention_output_bias: bfloat16 [1024], P(('fsdp', 'sp')), may hold values from -0.59765625 to 0.59765625
- first_gain: bfloat16 [1024], P(('fsdp', 'sp')), may hold values from 0.5 to 1.5
- first_shift: bfloat16 [1024], P(('fsdp', 'sp')), may hold values from -0.59765625 to 0.59765625
- expand_weight: bfloat16 [1024, 4096], P(('fsdp', 'sp')), may hold values from -0.1875 to 0.1875
- expand_bias: bfloat16 [4096], P(('fsdp', 'sp')), may hold values from -2 to 2
- contract_weight: bfloat16 [4096, 1024], P(('fsdp', 'sp')), may hold values from -0.09375 to 0.09375
- contract_bias: bfloat16 [1024], P(('fsdp', 'sp')), may hold values from -0.59765625 to 0.59765625
- second_gain: bfloat16 [1024], P(('fsdp', 'sp')), may hold values from 0.5 to 1.5
- second_shift: bfloat16 [1024], P(('fsdp', 'sp')), may hold values from -1.5 to 1.5
Outputs:
- output: bfloat16 [64, 512, 1024], P('fsdp', 'sp')
- loss: float32 [], replicated
- grad_tokens: float32 [64, 512, 1024], P('fsdp', 'sp')
- grad_query_weight: float32 [1024, 1024], P(('fsdp', 'sp'))
- grad_query_bias: float32 [1024], P(('fsdp', 'sp'))
- grad_key_weight: float32 [1024, 1024], P(('fsdp', 'sp'))
- grad_value_weight: float32 [1024, 1024], P(('fsdp', 'sp'))
- grad_value_bias: float32 [1024], P(('fsdp', 'sp'))
- grad_output_weight: float32 [1024, 1024], P(('fsdp', 'sp'))
- grad_output_bias: float32 [1024], P(('fsdp', 'sp'))
- grad_first_gain: float32 [1024], P(('fsdp', 'sp'))
- grad_first_shift: float32 [1024], P(('fsdp', 'sp'))
- grad_inner_weight: float32 [1024, 4096], P(('fsdp', 'sp'))
- grad_inner_bias: float32 [4096], P(('fsdp', 'sp'))
- grad_outer_weight: float32 [4096, 1024], P(('fsdp', 'sp'))
- grad_outer_bias: float32 [1024], P(('fsdp', 'sp'))
- grad_second_gain: float32 [1024], P(('fsdp', 'sp'))
- grad_second_shift: float32 [1024], P(('fsdp', 'sp'))
The draws below stay inside these ranges and needn't reach their ends.
Inputs may be any that keep to these rules, and one draw needn't show every extreme that they name: `validity`: each sequence's valid tokens form a prefix of 1 to 512 tokens; of the 8 sequences that start at each multiple of 8, one is valid in all 512 tokens.
All inputs are finite; a program needn't handle non-finite values.
Results may differ from the reference program's by a relative error of at most 0.014.
Values may be sent and summed in bfloat16 or wider, within the bound.
A program may use at most 192 MiB of HBM per device.

```python
import math
import jax
import jax.numpy as jnp
from jax import lax

D = 1024
H = 16
HD = 64
FF = 4096
SEQ_DEV = 8
L = 512
SEQS = 64
TOKENS = 32768


def draw_validity(key, part):
    key = jax.random.fold_in(key, 7)
    jitter_key, pick_key = jax.random.split(key)
    sequence = jnp.arange(SEQS, dtype=jnp.int32)
    base = L // 8 + sequence * (L - L // 8) // max(SEQS - 1, 1)
    jitter = jax.random.randint(jitter_key, (SEQS,), 0, L // 8 + 1)
    length = jnp.clip(base - jitter, 1, L)
    picked = jax.random.randint(pick_key, (SEQS // SEQ_DEV,), 0, SEQ_DEV)
    chosen = sequence % SEQ_DEV == jnp.repeat(picked, SEQ_DEV)
    length = jnp.where(chosen, L, length)
    return (jnp.arange(L, dtype=jnp.int32)[None, :] < length[:, None]).astype(jnp.int32)


def shared_shift(key):
    shift_key = jax.random.fold_in(key, 23)
    shift = jnp.clip(0.3 * jax.random.normal(shift_key, (D,), jnp.float32), -1.5, 1.5)
    return shift.astype(jnp.bfloat16).astype(jnp.float32)


def draw_second_shift(key, part):
    shift = shared_shift(key)
    return shift.astype(jnp.bfloat16)


def draw_teacher(key, part):
    shift = shared_shift(key)
    key = jax.random.fold_in(key, 11)
    noise_key = jax.random.fold_in(key, 0)
    noise = jnp.clip(4.0 * jax.random.normal(noise_key, (SEQS, L, D), jnp.float32), -16.0, 16.0)
    return (shift[None, None, :] + noise).astype(jnp.bfloat16)


def levels(rng, shape, cuts, least, largest):
    level, own = 1.0, jax.random.fold_in(rng, 6)
    for axis_at, blocks in cuts:
        draws = jnp.exp(jax.random.uniform(jax.random.fold_in(own, axis_at), (blocks,), jnp.float32, least / len(cuts), largest / len(cuts)))
        level = level * jnp.repeat(draws, shape[axis_at] // blocks).reshape([-1 if axis == axis_at else 1 for axis in range(len(shape))])
    return level


def bell_draw(key, shape, scale, reach, shards=(), kind=jnp.bfloat16):
    level = levels(key, shape, shards, -0.22, 0.18) if shards else 1.0
    values = jax.random.normal(key, shape, jnp.float32) * scale * level
    return jnp.minimum(jnp.maximum(values, -reach), reach).astype(kind)


def setup_inputs(seed: int = 0) -> dict:
    arg_keys = jax.random.split(jax.random.key(seed), 19)
    return {
        "tokens": bell_draw(arg_keys[0], (SEQS, L, D), 1.0, 6.0, ((0, 8), (1, 4))),
        "validity": draw_validity(jax.random.fold_in(arg_keys[18], 71), 0),
        "teacher": draw_teacher(jax.random.fold_in(arg_keys[18], 71), 0),
        "query_matrix": bell_draw(arg_keys[3], (D, D), D ** -0.5, 0.1875, ((0, 32),)),
        "query_offset_bias": bell_draw(arg_keys[4], (D,), 0.3, 2.0, ((0, 32),)),
        "key_matrix": bell_draw(arg_keys[5], (D, D), D ** -0.5, 0.1875, ((0, 32),)),
        "value_matrix": bell_draw(arg_keys[6], (D, D), D ** -0.5, 0.1875, ((0, 32),)),
        "value_offset_bias": bell_draw(arg_keys[7], (D,), 0.05, 0.29882812, ((0, 32),)),
        "attention_output_weight": bell_draw(arg_keys[8], (D, D), (D // 64) ** -0.5, 1.5, ((0, 32),)),
        "attention_output_bias": bell_draw(arg_keys[9], (D,), 0.1, 0.59765625, ((0, 32),)),
        "first_gain": jnp.clip(1.0 + 0.1 * jax.random.normal(arg_keys[10], (D,), jnp.float32), 0.5, 1.5).astype(jnp.bfloat16),
        "first_shift": bell_draw(arg_keys[11], (D,), 0.1, 0.59765625, ((0, 32),)),
        "expand_weight": bell_draw(arg_keys[12], (D, FF), D ** -0.5, 0.1875, ((0, 32),)),
        "expand_bias": bell_draw(arg_keys[13], (FF,), 0.3, 2.0, ((0, 32),)),
        "contract_weight": bell_draw(arg_keys[14], (FF, D), FF ** -0.5, 0.09375, ((0, 32),)),
        "contract_bias": bell_draw(arg_keys[15], (D,), 0.1, 0.59765625, ((0, 32),)),
        "second_gain": jnp.clip(1.0 + 0.1 * jax.random.normal(arg_keys[16], (D,), jnp.float32), 0.5, 1.5).astype(jnp.bfloat16),
        "second_shift": draw_second_shift(jax.random.fold_in(arg_keys[18], 71), 0),
    }


@jax.custom_vjp
def reduced_rows(v):
    return lax.optimization_barrier(v.astype(jnp.bfloat16)).astype(jnp.float32)

@jax.custom_vjp
def reduced_backward(v):
    return v

def low_keep(v):
    return (reduced_rows(v), None)

def low_pass(kept, grad):
    return (grad,)

def back_keep(v):
    return (v, None)

def back_low(kept, grad):
    return (reduced_rows(grad),)
reduced_rows.defvjp(low_keep, low_pass)
reduced_backward.defvjp(back_keep, back_low)
TOP_PRECISION = lax.Precision.HIGHEST

def norm_layer(hidden, gain, shift):
    average = lax.optimization_barrier(jnp.mean(hidden, axis=-1, keepdims=True))
    centred = hidden - average
    variance = lax.optimization_barrier(jnp.mean(centred * centred, axis=-1, keepdims=True))
    return centred * lax.rsqrt(variance + 1e-12) * gain + shift

def layer_group(params, input_rows, validity):
    query_matrix, query_offset_bias, key_matrix, value_matrix, value_offset_bias, attention_output_weight, attention_output_bias, first_gain, first_shift, expand_weight, expand_bias, contract_weight, contract_bias, second_gain, second_shift = params
    groups = input_rows.shape[0]
    temper = 1.0 / math.sqrt(HD)
    projected_queries = reduced_backward(reduced_rows(jnp.einsum('fpr,ra->fpa', input_rows, query_matrix, precision=TOP_PRECISION) + query_offset_bias))
    projected_keys = reduced_backward(reduced_rows(jnp.einsum('fpr,ra->fpa', input_rows, key_matrix, precision=TOP_PRECISION)))
    projected_values = reduced_backward(reduced_rows(jnp.einsum('fpr,ra->fpa', input_rows, value_matrix, precision=TOP_PRECISION) + value_offset_bias))
    query_heads = projected_queries.reshape(groups, L, H, HD)
    key_heads = projected_keys.reshape(groups, L, H, HD)
    value_heads = projected_values.reshape(groups, L, H, HD)
    scores = reduced_backward(jnp.einsum('sqhd,skhd->shqk', query_heads, key_heads, precision=TOP_PRECISION) * temper)
    masked = jnp.where(validity[:, None, None, :] > 0, scores, -1000000000.0)
    attention = jax.nn.softmax(masked, axis=-1)
    context_rows = reduced_backward(reduced_rows(jnp.einsum('shqk,skhd->sqhd', reduced_rows(attention), value_heads, precision=TOP_PRECISION)))
    context_rows = context_rows.reshape(groups, L, D)
    attended_rows = reduced_backward(jnp.einsum('fpr,ra->fpa', context_rows, attention_output_weight, precision=TOP_PRECISION) + attention_output_bias)
    normalized_rows = norm_layer(input_rows + attended_rows, first_gain, first_shift)
    inner_hidden = reduced_backward(jnp.einsum('jyh,hc->jyc', reduced_rows(normalized_rows), expand_weight, precision=TOP_PRECISION) + expand_bias)
    active_tokens = reduced_rows(jax.nn.gelu(inner_hidden, approximate=False))
    outer_result = reduced_backward(jnp.einsum('ygn,nx->ygx', active_tokens, contract_weight, precision=TOP_PRECISION) + contract_bias)
    return norm_layer(normalized_rows + outer_result, second_gain, second_shift)

def reference(tokens, validity, teacher, query_matrix, query_offset_bias, key_matrix, value_matrix, value_offset_bias, attention_output_weight, attention_output_bias, first_gain, first_shift, expand_weight, expand_bias, contract_weight, contract_bias, second_gain, second_shift):
    params = tuple((weight.astype(jnp.float32) for weight in (query_matrix, query_offset_bias, key_matrix, value_matrix, value_offset_bias, attention_output_weight, attention_output_bias, first_gain, first_shift, expand_weight, expand_bias, contract_weight, contract_bias, second_gain, second_shift)))
    input_rows = tokens.astype(jnp.float32)
    targets = teacher.astype(jnp.float32)
    valid_float = validity.astype(jnp.float32)
    valid_count = jnp.sum(valid_float)
    group_size = math.gcd(SEQS, max(1, 4096 // L))
    batches = SEQS // group_size
    group_fn = jax.checkpoint(layer_group)

    def scaled_loss(params, input_rows):
        stacked = input_rows.reshape(batches, group_size, L, D)

        def advance(running, item):
            block_in, block_valid, block_target = item
            final = group_fn(params, block_in, block_valid)
            error = final - block_target
            return (running + jnp.sum(block_valid[..., None] * error * error), final)
        total_sq, finals = lax.scan(advance, jnp.zeros((), jnp.float32), (stacked, valid_float.reshape(batches, group_size, L), targets.reshape(batches, group_size, L, D)))
        return (total_sq * TOKENS / valid_count, (finals.reshape(SEQS, L, D), total_sq))
    scaled, backward, aux_pair = jax.vjp(scaled_loss, params, input_rows, has_aux=True)
    final, total_sq = aux_pair
    param_grads, grad_tokens = backward(jnp.ones((), jnp.float32))
    loss = total_sq / (D * valid_count)
    grad_query_weight, grad_query_bias, grad_key_weight, grad_value_weight, grad_value_bias, grad_output_weight, grad_output_bias, grad_first_gain, grad_first_shift, grad_inner_weight, grad_inner_bias, grad_outer_weight, grad_outer_bias, grad_second_gain, grad_second_shift = param_grads
    return (final.astype(jnp.bfloat16), loss, grad_tokens, grad_query_weight, grad_query_bias, grad_key_weight, grad_value_weight, grad_value_bias, grad_output_weight, grad_output_bias, grad_first_gain, grad_first_shift, grad_inner_weight, grad_inner_bias, grad_outer_weight, grad_outer_bias, grad_second_gain, grad_second_shift)
```

```python
import functools
import math

import jax
import jax.numpy as jnp
from jax import lax
from jax.experimental import pallas as pl
from jax.experimental.pallas import tpu as pltpu
from jax.sharding import PartitionSpec as P

HD = 64
BF = jnp.bfloat16
F32 = jnp.float32
MESH = pl.DeviceIdType.MESH
AXES = ("fsdp", "sp")
MIB = 1 << 20


def bits_of(n):
    return n.bit_length() - 1


def gather_steps(a, b, color):
    z = [("sp", k) for k in reversed(range(b))]
    f = [("fsdp", k) for k in reversed(range(a))]
    if color and a >= 2:
        f[0], f[1] = f[1], f[0]
    return z + f


class Place:
    def __init__(self, a, b):
        self.a, self.b = a, b
        self.f = lax.axis_index("fsdp")
        self.z = lax.axis_index("sp")

    def dim(self, step):
        axis, k = step
        return self.a - 1 - k if axis == "fsdp" else self.a + self.b - 1 - k

    def bit(self, step):
        axis, k = step
        me = self.f if axis == "fsdp" else self.z
        return lax.rem(me // (1 << k), 2)

    def own(self):
        out = [None] * (self.a + self.b)
        for step in gather_steps(self.a, self.b, 0):
            out[self.dim(step)] = self.bit(step)
        return out

    def partner(self, step):
        axis, k = step
        change = (1 - 2 * self.bit(step)) * (1 << k)
        if axis == "fsdp":
            return (self.f + change, self.z)
        return (self.f, self.z + change)

    def greet(self):
        barrier = pltpu.get_barrier_semaphore()
        s = 1 << self.b
        others = [(self.f, lax.rem(self.z + k, s)) for k in range(1, s)]
        others += [self.partner(("fsdp", k)) for k in range(self.a)]
        for other in others:
            pl.semaphore_signal(barrier, inc=1, device_id=other, device_id_type=MESH)
        pl.semaphore_wait(barrier, len(others))


def exchange_tokens(place, src, dst, send, recv, local):
    s = 1 << place.b
    copies = [pltpu.make_async_copy(src.at[place.z], dst.at[place.z], local)]
    for k in range(1, s):
        to = lax.rem(place.z + k, s)
        copies.append(
            pltpu.make_async_remote_copy(
                src_ref=src.at[to],
                dst_ref=dst.at[place.z],
                send_sem=send.at[k - 1],
                recv_sem=recv.at[k - 1],
                device_id=(place.f, to),
                device_id_type=MESH,
            )
        )
    return copies


def pieces(rows, columns, parts_r, parts_c):
    out = []
    for i in range(parts_r):
        for j in range(parts_c):
            out.append(
                (
                    pl.ds(i * (rows // parts_r), rows // parts_r),
                    pl.ds(j * (columns // parts_c), columns // parts_c),
                )
            )
    return out


def make_units(shapes):
    cuts = []
    for at, (r, c) in enumerate(shapes):
        parts_r = max(1, min(4, r // 32)) if at == 5 else 1
        parts_c = 4 if at == 4 else 1
        cuts.append([(at,) + piece for piece in pieces(r, c, parts_r, parts_c)])
    q, k, v, o, w1, w2 = cuts
    units = [[q[0] + (0,), k[0] + (1,)], [v[0] + (0,), o[0] + (1,)]]
    for i in range(max(len(w1), len(w2))):
        unit = [w1[i] + (0,)] if i < len(w1) else []
        unit += [w2[i] + (1,)] if i < len(w2) else []
        units.append(unit)
    return units


def front_kernel(a, b, units, *refs):
    n_mat = 6
    tokens, vec = refs[0], refs[1]
    shards = refs[2 : 2 + n_mat]
    out_tokens, out_vec = refs[2 + n_mat], refs[3 + n_mat]
    outs = refs[4 + n_mat : 4 + 2 * n_mat]
    send, recv, local, tok_send, tok_recv, tok_local = refs[4 + 2 * n_mat :]
    place = Place(a, b)
    own = place.own()
    chunks = [[(vec, out_vec, (), 0)] + [(shards[at], outs[at], (r, c), color) for at, r, c, color in units[0]]]
    for unit in units[1:]:
        chunks.append([(shards[at], outs[at], (r, c), color) for at, r, c, color in unit])
    flat = [chunk for unit in chunks for chunk in unit]
    number = {}
    for u, unit in enumerate(chunks):
        for i in range(len(unit)):
            number[u, i] = len(number)
    steps = a + b

    def copy_of(m, s):
        src, out, piece, color = flat[m]
        order = gather_steps(a, b, color)
        index = list(own)
        for step in order[:s]:
            index[place.dim(step)] = slice(None)
        there = out.at[tuple(index) + piece]
        here = (src.at[piece] if piece else src) if s == 0 else there
        return pltpu.make_async_remote_copy(
            src_ref=here,
            dst_ref=there,
            send_sem=send.at[m, s],
            recv_sem=recv.at[m, s],
            device_id=place.partner(order[s]),
            device_id_type=MESH,
        )

    def keep_of(m):
        src, out, piece, _ = flat[m]
        return pltpu.make_async_copy(
            src.at[piece] if piece else src, out.at[tuple(own) + piece], local.at[m]
        )

    for m in range(len(flat)):
        keep_of(m).start()
    place.greet()
    moves = exchange_tokens(place, tokens, out_tokens, tok_send, tok_recv, tok_local)
    for t in range(len(chunks) + steps):
        for s in reversed(range(steps + 1)):
            u = t - s
            if not 0 <= u < len(chunks):
                continue
            for i in range(len(chunks[u])):
                m = number[u, i]
                if s == 1:
                    keep_of(m).wait()
                if s > 0:
                    copy_of(m, s - 1).wait_recv()
                if s < steps:
                    copy_of(m, s).start()
        if t == 1:
            for move in moves:
                move.start()
    for m in range(len(flat)):
        for s in range(steps):
            copy_of(m, s).wait_send()
    for move in moves:
        move.wait()


def front(a, b, tokens, vec, shards):
    lead = (2,) * (a + b)
    units = make_units([w.shape for w in shards])
    n_chunks = 1 + sum(len(u) for u in units)
    steps = a + b
    anyspace = pl.BlockSpec(memory_space=pl.ANY)
    outs = [jax.ShapeDtypeStruct(tokens.shape, tokens.dtype), jax.ShapeDtypeStruct(lead + vec.shape, vec.dtype)]
    outs += [jax.ShapeDtypeStruct(lead + w.shape, w.dtype) for w in shards]
    s = 1 << b
    return pl.pallas_call(
        functools.partial(front_kernel, a, b, units),
        out_shape=outs,
        in_specs=[anyspace] * (2 + len(shards)),
        out_specs=[anyspace] * len(outs),
        scratch_shapes=[
            pltpu.SemaphoreType.DMA((n_chunks, steps)),
            pltpu.SemaphoreType.DMA((n_chunks, steps)),
            pltpu.SemaphoreType.DMA((n_chunks,)),
            pltpu.SemaphoreType.DMA((s - 1,)),
            pltpu.SemaphoreType.DMA((s - 1,)),
            pltpu.SemaphoreType.DMA,
        ],
        compiler_params=pltpu.CompilerParams(collective_id=0, has_side_effects=True),
        name="gather_weights",
    )(tokens, vec, *shards)


def back_kernel(a, b, units, *refs):
    n_mat = 6
    tokens, vec = refs[0], refs[1]
    grads = refs[2 : 2 + n_mat]
    out_tokens, out_vec = refs[2 + n_mat], refs[3 + n_mat]
    outs = refs[4 + n_mat : 4 + 2 * n_mat]
    rest = refs[4 + 2 * n_mat :]
    send, recv, local, tok_send, tok_recv, tok_local = rest[:6]
    steps = a + b
    n_chunks = 1 + sum(len(u) for u in units)
    sums = rest[6 : 6 + n_chunks]
    landed = rest[6 + n_chunks :]
    place = Place(a, b)
    own = place.own()
    chunks = [[(vec, out_vec, (), 0)] + [(grads[at], outs[at], (r, c), color) for at, r, c, color in units[0]]]
    for unit in units[1:]:
        chunks.append([(grads[at], outs[at], (r, c), color) for at, r, c, color in unit])
    flat = [chunk for unit in chunks for chunk in unit]
    number = {}
    for u, unit in enumerate(chunks):
        for i in range(len(unit)):
            number[u, i] = len(number)

    def index_at(m, s, flip):
        order = gather_steps(a, b, flat[m][3])[::-1]
        index = [slice(None)] * steps
        for step in order[: s + 1]:
            index[place.dim(step)] = own[place.dim(step)]
        if flip:
            d = place.dim(order[s])
            index[d] = 1 - own[d]
        return order, index

    def without_first(order, index):
        index = list(index)
        del index[place.dim(order[0])]
        return tuple(index)

    def copy_of(m, s):
        src, out, piece, color = flat[m]
        order, index = index_at(m, s, True)
        here = src.at[tuple(index) + piece] if s == 0 else sums[m].at[without_first(order, index)]
        return pltpu.make_async_remote_copy(
            src_ref=here,
            dst_ref=landed[m * steps + s],
            send_sem=send.at[m, s],
            recv_sem=recv.at[m, s],
            device_id=place.partner(order[s]),
            device_id_type=MESH,
        )

    def keep_of(m):
        src, out, piece, _ = flat[m]
        order, index = index_at(m, 0, False)
        return pltpu.make_async_copy(src.at[tuple(index) + piece], sums[m], local.at[m])

    def add(m, s):
        order, index = index_at(m, s, False)
        index = without_first(order, index)
        free = [d for d, v in enumerate(index) if isinstance(v, slice)]

        def one(i, carry):
            at = list(index)
            bits = []
            for j, d in enumerate(free):
                bit = lax.rem(i // (1 << (len(free) - 1 - j)), 2)
                at[d] = bit
                bits.append(bit)
            total = sums[m][tuple(at)].astype(F32) + landed[m * steps + s][tuple(bits)].astype(F32)
            sums[m][tuple(at)] = total.astype(sums[m].dtype)
            return carry

        if s < steps - 1:
            lax.fori_loop(0, 1 << len(free), one, 0)
        else:
            out, piece = flat[m][1], flat[m][2]
            total = sums[m][tuple(index)].astype(F32) + landed[m * steps + s][...].astype(F32)
            if piece:
                out[piece] = total
            else:
                out[...] = total

    place.greet()
    moves = exchange_tokens(place, tokens, out_tokens, tok_send, tok_recv, tok_local)
    for t in range(len(chunks) + steps):
        for s in reversed(range(steps + 1)):
            u = t - s
            if not 0 <= u < len(chunks):
                continue
            for i in range(len(chunks[u])):
                m = number[u, i]
                if s == 0:
                    keep_of(m).start()
                if s == 1:
                    keep_of(m).wait()
                if s > 0:
                    copy_of(m, s - 1).wait_recv()
                    add(m, s - 1)
                if s < steps:
                    copy_of(m, s).start()
        if t == 0:
            for move in moves:
                move.start()
    for m in range(len(flat)):
        for s in range(steps):
            copy_of(m, s).wait_send()
    for move in moves:
        move.wait()


def back(a, b, tokens, vec, grads):
    lead = a + b
    steps = a + b
    shapes = [g.shape[lead:] for g in grads]
    units = make_units(shapes)
    sizes = [vec.shape[lead:]] + [(r.size, c.size) for unit in units for _, r, c, _ in unit]
    types = [vec.dtype] + [grads[at].dtype for unit in units for at, _, _, _ in unit]
    n_chunks = len(sizes)
    anyspace = pl.BlockSpec(memory_space=pl.ANY)
    vmem = pl.BlockSpec(memory_space=pltpu.VMEM)
    outs = [jax.ShapeDtypeStruct(tokens.shape, tokens.dtype), jax.ShapeDtypeStruct(vec.shape[lead:], F32)]
    outs += [jax.ShapeDtypeStruct(shape, F32) for shape in shapes]
    s = 1 << b
    scratch = [
        pltpu.SemaphoreType.DMA((n_chunks, steps)),
        pltpu.SemaphoreType.DMA((n_chunks, steps)),
        pltpu.SemaphoreType.DMA((n_chunks,)),
        pltpu.SemaphoreType.DMA((s - 1,)),
        pltpu.SemaphoreType.DMA((s - 1,)),
        pltpu.SemaphoreType.DMA,
    ]
    scratch += [pltpu.VMEM((2,) * (steps - 1) + size, kind) for size, kind in zip(sizes, types)]
    for size, kind in zip(sizes, types):
        scratch += [pltpu.VMEM((2,) * (steps - 1 - k) + size, kind) for k in range(steps)]
    return pl.pallas_call(
        functools.partial(back_kernel, a, b, units),
        out_shape=outs,
        in_specs=[anyspace] * (2 + len(grads)),
        out_specs=[anyspace] + [vmem] * (len(outs) - 1),
        scratch_shapes=scratch,
        compiler_params=pltpu.CompilerParams(
            collective_id=1, has_side_effects=True, vmem_limit_bytes=56 * MIB
        ),
        name="sum_grads",
    )(tokens, vec, *grads)


def head_mask(head):
    lane = lax.broadcasted_iota(jnp.int32, (1, 2 * HD), 1)
    return (lane // HD == head).astype(F32)


def dot_nt(x, y):
    return lax.dot_general(x, y, (((1,), (1,)), ((), ())), preferred_element_type=F32)


def dot_tn(x, y):
    return lax.dot_general(x, y, (((0,), (0,)), ((), ())), preferred_element_type=F32)


def dot_nn(x, y):
    return lax.dot_general(x, y, (((1,), (0,)), ((), ())), preferred_element_type=F32)


def attend_kernel(temper, bias_ref, q_ref, k_ref, v_ref, ctx_ref, lse_ref):
    length = bias_ref.shape[-1]
    shape = q_ref.shape
    q = q_ref[...].reshape(length, shape[-1])
    k = k_ref[...].reshape(length, shape[-1])
    v = v_ref[...].reshape(length, shape[-1])
    bias = bias_ref[...].reshape(1, length)
    total = jnp.zeros((length, shape[-1]), F32)
    logs = jnp.zeros((length, shape[-1]), F32)
    for head in range(2):
        mask = head_mask(head)
        scores = dot_nt(q, k * (mask * temper).astype(BF)) + bias
        largest = jnp.max(scores, axis=-1, keepdims=True)
        raised = jnp.exp(scores - largest)
        summed = jnp.sum(raised, axis=-1, keepdims=True)
        part = dot_nn(raised.astype(BF), v * mask.astype(BF))
        total = total + part * (1.0 / summed)
        logs = logs + (largest + jnp.log(summed)) * mask
    ctx_ref[...] = total.astype(BF).reshape(shape)
    lse_ref[...] = logs.reshape(shape)


def attend(bias, q, k, v):
    s, n, t, width = q.shape
    rows = pl.BlockSpec((s, 1, t, 2 * HD), lambda i, j: (0, i, 0, j))
    return pl.pallas_call(
        functools.partial(attend_kernel, 1.0 / math.sqrt(HD)),
        grid=(n, width // (2 * HD)),
        out_shape=[
            jax.ShapeDtypeStruct(q.shape, BF),
            jax.ShapeDtypeStruct(q.shape, F32),
        ],
        in_specs=[pl.BlockSpec((1, 1, s * t), lambda i, j: (i, 0, 0)), rows, rows, rows],
        out_specs=[rows, rows],
        compiler_params=pltpu.CompilerParams(vmem_limit_bytes=32 * MIB),
        cost_estimate=pl.CostEstimate(
            flops=4 * n * (s * t) ** 2 * width, bytes_accessed=16 * s * n * t * width, transcendentals=0
        ),
        name="attend",
    )(bias, q, k, v)


def attend_back_kernel(temper, bias_ref, q_ref, k_ref, v_ref, ctx_ref, lse_ref, grad_ref, gq_ref, gk_ref, gv_ref):
    length = bias_ref.shape[-1]
    shape = q_ref.shape

    def whole(ref):
        return ref[...].reshape(length, shape[-1])

    q, k, v, ctx, grad, lse = (whole(r) for r in (q_ref, k_ref, v_ref, ctx_ref, grad_ref, lse_ref))
    key_bias = jnp.transpose(jnp.broadcast_to(bias_ref[...].reshape(1, length), (2 * HD, length)))[:, :1]
    both = grad.astype(F32) * ctx.astype(F32)
    lse_t = jnp.transpose(lse)
    both_t = jnp.transpose(both)
    gq = jnp.zeros((length, shape[-1]), F32)
    gk = jnp.zeros((length, shape[-1]), F32)
    gv = jnp.zeros((length, shape[-1]), F32)
    for head in range(2):
        mask = head_mask(head)
        low = mask.astype(BF)
        k_head = k * (mask * temper).astype(BF)
        grad_head = grad * low
        log_total = lse_t[head * HD : head * HD + 1]
        inner = jnp.sum(both_t[head * HD : (head + 1) * HD], axis=0, keepdims=True)
        scores = dot_nt(k_head, q) + key_bias
        attention = jnp.exp(scores - log_total)
        gv = gv + dot_nn(attention.astype(BF), grad_head)
        grad_attention = dot_nt(v, grad_head)
        grad_scores = (attention * (grad_attention - inner)).astype(BF)
        gk = gk + dot_nn(grad_scores, q * (mask * temper).astype(BF))
        gq = gq + dot_tn(grad_scores, k_head)
    gq_ref[...] = gq.astype(BF).reshape(shape)
    gk_ref[...] = gk.astype(BF).reshape(shape)
    gv_ref[...] = gv.astype(BF).reshape(shape)


def attend_back(bias, q, k, v, ctx, lse, grad):
    s, n, t, width = q.shape
    rows = pl.BlockSpec((s, 1, t, 2 * HD), lambda i, j: (0, i, 0, j))
    return pl.pallas_call(
        functools.partial(attend_back_kernel, 1.0 / math.sqrt(HD)),
        grid=(n, width // (2 * HD)),
        out_shape=[jax.ShapeDtypeStruct(q.shape, BF)] * 3,
        in_specs=[pl.BlockSpec((1, 1, s * t), lambda i, j: (i, 0, 0))] + [rows] * 6,
        out_specs=[rows] * 3,
        compiler_params=pltpu.CompilerParams(vmem_limit_bytes=32 * MIB),
        cost_estimate=pl.CostEstimate(
            flops=10 * n * (s * t) ** 2 * width, bytes_accessed=20 * s * n * t * width, transcendentals=0
        ),
        name="attend_back",
    )(bias, q, k, v, ctx, lse, grad)


def norm_forward(hidden, gain, shift):
    average = jnp.mean(hidden, axis=-1, keepdims=True)
    centred = hidden - average
    scale = lax.rsqrt(jnp.mean(centred * centred, axis=-1, keepdims=True) + 1e-12)
    xhat = centred * scale
    return xhat * gain + shift, xhat, scale


def norm_backward(grad, gain, xhat, scale):
    scaled = grad * gain
    lead = jnp.mean(scaled, axis=-1, keepdims=True)
    slope = jnp.mean(scaled * xhat, axis=-1, keepdims=True)
    return scale * (scaled - lead - xhat * slope)


def gelu_pair(x):
    cdf = 0.5 * (1.0 + lax.erf(x * (1.0 / math.sqrt(2.0))))
    pdf = jnp.exp(-0.5 * x * x) * (1.0 / math.sqrt(2.0 * math.pi))
    return x * cdf, cdf + x * pdf


def body(tokens, validity, teacher, wq, bq, wk, wv, bv, wo, bo, gain1, shift1, w1, b1, w2, b2, gain2, shift2):
    fs, sp = lax.axis_size("fsdp"), lax.axis_size("sp")
    a, b = bits_of(fs), bits_of(sp)
    devices = fs * sp
    seqs, part, width = tokens.shape
    n = seqs // sp
    length = part * sp
    rows = sp * n * part
    total_tokens = rows * devices
    z = lax.axis_index("sp")
    shard_shape = (sp, n, part, width)

    mine = lax.dynamic_slice_in_dim(validity, z * n, n, 0)
    count = jnp.sum(mine)
    vectors = (bq, bv, bo, gain1, shift1, b2, gain2, shift2, b1)
    sizes = [v.shape[0] for v in vectors]
    held = jnp.concatenate(list(vectors) + [jnp.stack([count // 32, count % 32]).astype(BF)])
    vec = jnp.pad(held, (0, 16 * 128 - held.shape[0])).reshape(16, 128)

    shards = (wq, wk, wv, wo, w1, w2)
    got = front(a, b, tokens.reshape(shard_shape), vec, shards)
    moved, vec_all = got[0], got[1].reshape(devices, -1)
    WQ, WK, WV, WO, W1, W2 = (
        g.reshape((devices * w.shape[0],) + w.shape[1:]) for g, w in zip(got[2:], shards)
    )
    full, at = [], 0
    for size in sizes:
        full.append(vec_all[:, at : at + size].reshape(-1).astype(F32))
        at += size
    BQ, BV, BO, G1, S1, B2, G2, S2, B1 = full
    counted = jnp.sum(vec_all[:, at].astype(F32)) * 32.0 + jnp.sum(vec_all[:, at + 1].astype(F32))

    teacher_moved = lax.all_to_all(
        lax.optimization_barrier((teacher, moved))[0].reshape(shard_shape), "sp", split_axis=0, concat_axis=0
    ).reshape(rows, width)

    valid = mine.astype(F32)
    bias = ((valid - 1.0) * 1e9).reshape(n, 1, length)
    mask_rows = jnp.swapaxes(valid.reshape(n, sp, part), 0, 1).reshape(rows, 1)

    x = moved.reshape(rows, width)
    q = (dot_nn(x, WQ) + BQ).astype(BF)
    k = dot_nn(x, WK).astype(BF)
    v = (dot_nn(x, WV) + BV).astype(BF)
    ctx, lse = attend(bias, *(p.reshape(shard_shape) for p in (q, k, v)))
    ctx_rows = ctx.reshape(rows, width)
    first = x.astype(F32) + dot_nn(ctx_rows, WO) + BO
    normed, xhat1, scale1 = norm_forward(first, G1, S1)
    normed_low = normed.astype(BF)
    inner = dot_nn(normed_low, W1) + B1
    active, slope = gelu_pair(inner)
    active_low = active.astype(BF)
    slope = slope.astype(BF)
    second = normed + dot_nn(active_low, W2) + B2
    final, xhat2, scale2 = norm_forward(second, G2, S2)
    error = final - teacher_moved.astype(F32)
    local_loss = jnp.sum(mask_rows * error * error)
    output = lax.all_to_all(final.astype(BF).reshape(shard_shape), "sp", split_axis=0, concat_axis=0)

    grad_final = (2.0 * total_tokens / counted) * mask_rows * error
    grad_second = norm_backward(grad_final, G2, xhat2, scale2)
    grad_outer = grad_second.astype(BF)
    g_w2 = dot_tn(active_low, grad_outer).astype(BF)
    grad_inner = (dot_nt(grad_outer, W2) * slope.astype(F32)).astype(BF)
    g_w1 = dot_tn(normed_low, grad_inner).astype(BF)
    grad_normed = dot_nt(grad_inner, W1) + grad_second
    grad_first = norm_backward(grad_normed, G1, xhat1, scale1)
    grad_attended = grad_first.astype(BF)
    g_wo = dot_tn(ctx_rows, grad_attended).astype(BF)
    grad_ctx = dot_nt(grad_attended, WO).astype(BF)
    gq, gk, gv = attend_back(
        bias, *(p.reshape(shard_shape) for p in (q, k, v)), ctx, lse, grad_ctx.reshape(shard_shape)
    )
    gq, gk, gv = (g.reshape(rows, width) for g in (gq, gk, gv))
    g_wq = dot_tn(x, gq).astype(BF)
    g_wk = dot_tn(x, gk).astype(BF)
    g_wv = dot_tn(x, gv).astype(BF)
    grad_tokens = (dot_nt(gq, WQ) + dot_nt(gk, WK) + dot_nt(gv, WV) + grad_first).astype(BF)

    def column_sum(value):
        return jnp.sum(value.astype(F32), axis=0)

    vector_grads = (
        column_sum(gq),
        column_sum(gv),
        column_sum(grad_attended),
        jnp.sum(grad_normed * xhat1, axis=0),
        column_sum(grad_normed),
        column_sum(grad_outer),
        jnp.sum(grad_final * xhat2, axis=0),
        column_sum(grad_final),
        column_sum(grad_inner),
    )
    parts = [g.reshape(devices, -1) for g in vector_grads]
    parts.append(jnp.broadcast_to(local_loss, (devices, 1)))
    packed = jnp.concatenate(parts, axis=1)
    packed = jnp.pad(packed, ((0, 0), (0, 8 * 128 - packed.shape[1])))
    lead = (2,) * (a + b)
    summed = back(
        a,
        b,
        grad_tokens.reshape(shard_shape),
        packed.reshape(lead + (8, 128)),
        [g.reshape(lead + w.shape) for g, w in zip((g_wq, g_wk, g_wv, g_wo, g_w1, g_w2), shards)],
    )
    home = summed[0].reshape(seqs, part, width).astype(F32)
    own = summed[1].reshape(-1)
    small, at = [], 0
    for size in sizes:
        small.append(own[at : at + size])
        at += size
    loss = own[at] / (width * counted)
    d_bq, d_bv, d_bo, d_g1, d_s1, d_b2, d_g2, d_s2, d_b1 = small
    d_wq, d_wk, d_wv, d_wo, d_w1, d_w2 = summed[2:]
    return (
        output.reshape(seqs, part, width),
        loss,
        home,
        d_wq,
        d_bq,
        d_wk,
        d_wv,
        d_bv,
        d_wo,
        d_bo,
        d_g1,
        d_s1,
        d_w1,
        d_b1,
        d_w2,
        d_b2,
        d_g2,
        d_s2,
    )


def solution(mesh):
    tokens = P("fsdp", "sp", None)
    matrix = P(AXES, None)
    vector = P(AXES)
    return jax.shard_map(
        body,
        mesh=mesh,
        in_specs=(
            tokens,
            P("fsdp", None),
            tokens,
            matrix,
            vector,
            matrix,
            matrix,
            vector,
            matrix,
            vector,
            vector,
            vector,
            matrix,
            vector,
            matrix,
            vector,
            vector,
            vector,
        ),
        out_specs=(
            tokens,
            P(),
            tokens,
            matrix,
            vector,
            matrix,
            matrix,
            vector,
            matrix,
            vector,
            vector,
            vector,
            matrix,
            vector,
            matrix,
            vector,
            vector,
            vector,
        ),
        check_vma=False,
    )
```

```python
import functools
import math

import jax
import jax.numpy as jnp
from jax import lax
from jax.experimental import pallas as pl
from jax.experimental.pallas import tpu as pltpu
from jax.sharding import PartitionSpec as P

HD = 64
BF = jnp.bfloat16
F32 = jnp.float32
MESH = pl.DeviceIdType.MESH
AXES = ("fsdp", "sp")
MIB = 1 << 20
GATHER_PAIRS = ((0, 1, 1), (2, 3, 1), (4, 5, 4))
SUM_PAIRS = ((4, 5, 4), (3, 3, 1), (0, 1, 1), (2, 2, 1))
WAVE_STEPS = (0, 2, 5, 12, 19)


def bits_of(n):
    return n.bit_length() - 1


def gather_steps(a, b, color):
    z = [("sp", k) for k in reversed(range(b))]
    f = [("fsdp", k) for k in reversed(range(a))]
    if color and a >= 2:
        f[0], f[1] = f[1], f[0]
    return z + f


class Place:
    def __init__(self, a, b):
        self.a, self.b = a, b
        self.f = lax.axis_index("fsdp")
        self.z = lax.axis_index("sp")

    def dim(self, step):
        axis, k = step
        return self.a - 1 - k if axis == "fsdp" else self.a + self.b - 1 - k

    def bit(self, step):
        axis, k = step
        me = self.f if axis == "fsdp" else self.z
        return lax.rem(me // (1 << k), 2)

    def own(self):
        out = [None] * (self.a + self.b)
        for step in gather_steps(self.a, self.b, 0):
            out[self.dim(step)] = self.bit(step)
        return out

    def partner(self, step):
        axis, k = step
        change = (1 - 2 * self.bit(step)) * (1 << k)
        if axis == "fsdp":
            return (self.f + change, self.z)
        return (self.f, self.z + change)

    def greet(self):
        barrier = pltpu.get_barrier_semaphore()
        s = 1 << self.b
        others = [(self.f, lax.rem(self.z + k, s)) for k in range(1, s)]
        others += [self.partner(("fsdp", k)) for k in range(self.a)]
        for other in others:
            pl.semaphore_signal(barrier, inc=1, device_id=other, device_id_type=MESH)
        pl.semaphore_wait(barrier, len(others))


def exchange_tokens(place, src, dst, send, recv, local):
    s = 1 << place.b
    copies = [pltpu.make_async_copy(src.at[place.z], dst.at[place.z], local)]
    for k in range(1, s):
        to = lax.rem(place.z + k, s)
        copies.append(
            pltpu.make_async_remote_copy(
                src_ref=src.at[to],
                dst_ref=dst.at[place.z],
                send_sem=send.at[k - 1],
                recv_sem=recv.at[k - 1],
                device_id=(place.f, to),
                device_id_type=MESH,
            )
        )
    return copies


def pieces(rows, columns, parts_r, parts_c):
    out = []
    for i in range(parts_r):
        for j in range(parts_c):
            out.append(
                (
                    pl.ds(i * (rows // parts_r), rows // parts_r),
                    pl.ds(j * (columns // parts_c), columns // parts_c),
                )
            )
    return out


def make_units(shapes, pairs):
    units = []
    for x, y, n in pairs:
        (rx, cx), (ry, cy) = shapes[x], shapes[y]
        if x == y:
            left, right = pieces(rx, cx, 1, 2)
            units.append([(x,) + left + (0,), (y,) + right + (1,)])
            continue
        ny = max(1, min(n, ry // 16)) if ry > rx else 1
        xs = pieces(rx, cx, 1, n)
        ys = pieces(ry, cy, ny, 1)
        for k in range(n):
            unit = [(x,) + xs[k] + (0,)]
            if k < ny:
                unit.append((y,) + ys[k] + (1,))
            units.append(unit)
    return units


def front_kernel(a, b, units, *refs):
    n_mat = 6
    tokens, vec = refs[0], refs[1]
    shards = refs[2 : 2 + n_mat]
    out_tokens, out_vec = refs[2 + n_mat], refs[3 + n_mat]
    outs = refs[4 + n_mat : 4 + 2 * n_mat]
    send, recv, local, tok_send, tok_recv, tok_local = refs[4 + 2 * n_mat :]
    place = Place(a, b)
    own = place.own()
    chunks = [[(vec, out_vec, (), 0)] + [(shards[at], outs[at], (r, c), color) for at, r, c, color in units[0]]]
    for unit in units[1:]:
        chunks.append([(shards[at], outs[at], (r, c), color) for at, r, c, color in unit])
    flat = [chunk for unit in chunks for chunk in unit]
    number = {}
    for u, unit in enumerate(chunks):
        for i in range(len(unit)):
            number[u, i] = len(number)
    steps = a + b

    def copy_of(m, s):
        src, out, piece, color = flat[m]
        order = gather_steps(a, b, color)
        index = list(own)
        for step in order[:s]:
            index[place.dim(step)] = slice(None)
        there = out.at[tuple(index) + piece]
        here = (src.at[piece] if piece else src) if s == 0 else there
        return pltpu.make_async_remote_copy(
            src_ref=here,
            dst_ref=there,
            send_sem=send.at[m, s],
            recv_sem=recv.at[m, s],
            device_id=place.partner(order[s]),
            device_id_type=MESH,
        )

    def keep_of(m):
        src, out, piece, _ = flat[m]
        return pltpu.make_async_copy(
            src.at[piece] if piece else src, out.at[tuple(own) + piece], local.at[m]
        )

    for m in range(len(flat)):
        keep_of(m).start()
    place.greet()
    moves = exchange_tokens(place, tokens, out_tokens, tok_send, tok_recv, tok_local)
    lead = [b + 1, b] + list(range(b - 1, -1, -1)) + list(range(b + 2, steps + 1))
    events = [(u + k, lead.index(k), u, k) for u in range(len(chunks)) for k in range(steps + 1)]
    events.append((len(chunks) + 0.5, 0, -1, -1))
    for _, _, u, k in sorted(events):
        if u < 0:
            for move in moves:
                move.start()
            continue
        for i in range(len(chunks[u])):
            m = number[u, i]
            if k == 1:
                keep_of(m).wait()
            if k > 0:
                copy_of(m, k - 1).wait_recv()
            if k < steps:
                copy_of(m, k).start()
    for m in range(len(flat)):
        for k in range(steps):
            copy_of(m, k).wait_send()
    for move in moves:
        move.wait()


def front(a, b, tokens, vec, shards):
    lead = (2,) * (a + b)
    units = make_units([w.shape for w in shards], GATHER_PAIRS)
    n_chunks = 1 + sum(len(u) for u in units)
    steps = a + b
    anyspace = pl.BlockSpec(memory_space=pl.ANY)
    outs = [jax.ShapeDtypeStruct(tokens.shape, tokens.dtype), jax.ShapeDtypeStruct(lead + vec.shape, vec.dtype)]
    outs += [jax.ShapeDtypeStruct(lead + w.shape, w.dtype) for w in shards]
    s = 1 << b
    return pl.pallas_call(
        functools.partial(front_kernel, a, b, units),
        out_shape=outs,
        in_specs=[anyspace] * (2 + len(shards)),
        out_specs=[anyspace] * len(outs),
        scratch_shapes=[
            pltpu.SemaphoreType.DMA((n_chunks, steps)),
            pltpu.SemaphoreType.DMA((n_chunks, steps)),
            pltpu.SemaphoreType.DMA((n_chunks,)),
            pltpu.SemaphoreType.DMA((s - 1,)),
            pltpu.SemaphoreType.DMA((s - 1,)),
            pltpu.SemaphoreType.DMA,
        ],
        compiler_params=pltpu.CompilerParams(collective_id=0, has_side_effects=True),
        name="gather_weights",
    )(tokens, vec, *shards)


def head_mask(head):
    lane = lax.broadcasted_iota(jnp.int32, (1, 2 * HD), 1)
    return (lane // HD == head).astype(F32)


def dot_nt(x, y):
    return lax.dot_general(x, y, (((1,), (1,)), ((), ())), preferred_element_type=F32)


def dot_tn(x, y):
    return lax.dot_general(x, y, (((0,), (0,)), ((), ())), preferred_element_type=F32)


def dot_nn(x, y):
    return lax.dot_general(x, y, (((1,), (0,)), ((), ())), preferred_element_type=F32)


def attend_kernel(temper, bias_ref, q_ref, k_ref, v_ref, ctx_ref, lse_ref):
    length = bias_ref.shape[-1]
    shape = q_ref.shape
    q = q_ref[...].reshape(length, shape[-1])
    k = k_ref[...].reshape(length, shape[-1])
    v = v_ref[...].reshape(length, shape[-1])
    bias = bias_ref[...].reshape(1, length)
    total = jnp.zeros((length, shape[-1]), F32)
    logs = jnp.zeros((length, shape[-1]), F32)
    for head in range(2):
        mask = head_mask(head)
        scores = dot_nt(q, k * (mask * temper).astype(BF)) + bias
        largest = jnp.max(scores, axis=-1, keepdims=True)
        raised = jnp.exp(scores - largest)
        summed = jnp.sum(raised, axis=-1, keepdims=True)
        part = dot_nn(raised.astype(BF), v * mask.astype(BF))
        total = total + part * (1.0 / summed)
        logs = logs + (largest + jnp.log(summed)) * mask
    ctx_ref[...] = total.astype(BF).reshape(shape)
    turned = jnp.transpose(logs)
    for head in range(2):
        lse_ref[0, 0, head : head + 1] = turned[head * HD : head * HD + 1]


def attend(bias, q, k, v):
    s, n, t, width = q.shape
    rows = pl.BlockSpec((s, 1, t, 2 * HD), lambda i, j: (0, i, 0, j))
    return pl.pallas_call(
        functools.partial(attend_kernel, 1.0 / math.sqrt(HD)),
        grid=(n, width // (2 * HD)),
        out_shape=[
            jax.ShapeDtypeStruct(q.shape, BF),
            jax.ShapeDtypeStruct((n, width // (2 * HD), 8, s * t), F32),
        ],
        in_specs=[pl.BlockSpec((1, 1, s * t), lambda i, j: (i, 0, 0)), rows, rows, rows],
        out_specs=[rows, pl.BlockSpec((1, 1, 8, s * t), lambda i, j: (i, j, 0, 0))],
        compiler_params=pltpu.CompilerParams(vmem_limit_bytes=32 * MIB),
        cost_estimate=pl.CostEstimate(
            flops=4 * n * (s * t) ** 2 * width, bytes_accessed=16 * s * n * t * width, transcendentals=0
        ),
        name="attend",
    )(bias, q, k, v)


def attend_back_pair(temper, bias_ref, q_ref, k_ref, v_ref, ctx_ref, lse_ref, grad_ref):
    length = bias_ref.shape[-1]

    def whole(ref):
        return ref[...].reshape(length, ref.shape[-1])

    q, k, v, ctx, grad = (whole(r) for r in (q_ref, k_ref, v_ref, ctx_ref, grad_ref))
    key_bias = jnp.transpose(jnp.broadcast_to(bias_ref[...].reshape(1, length), (2 * HD, length)))[:, :1]
    both = jnp.transpose(grad.astype(F32) * ctx.astype(F32))
    gq = jnp.zeros(q.shape, F32)
    gk = jnp.zeros(q.shape, F32)
    gv = jnp.zeros(q.shape, F32)
    for head in range(2):
        mask = head_mask(head)
        k_head = k * (mask * temper).astype(BF)
        grad_head = grad * mask.astype(BF)
        log_total = lse_ref[0, 0, head : head + 1]
        inner = jnp.sum(both[head * HD : (head + 1) * HD], axis=0, keepdims=True)
        attention = jnp.exp(dot_nt(k_head, q) + key_bias - log_total)
        gv = gv + dot_nn(attention.astype(BF), grad_head)
        grad_attention = dot_nt(v, grad_head)
        grad_scores = (attention * (grad_attention - inner)).astype(BF)
        gk = gk + dot_nn(grad_scores, q * (mask * temper).astype(BF))
        gq = gq + dot_tn(grad_scores, k_head)
    return gq.astype(BF), gk.astype(BF), gv.astype(BF)


class Sums:
    def __init__(self, a, b, chunks, landed, staged, send, recv, local):
        self.place = Place(a, b)
        self.own = self.place.own()
        self.steps = a + b
        self.chunks, self.landed, self.staged = chunks, landed, staged
        self.send, self.recv, self.local = send, recv, local
        self.orders = [gather_steps(a, b, c[3])[::-1] for c in chunks]

    def index(self, m, s, flip):
        out = [slice(None)] * self.steps
        for step in self.orders[m][: s + 1]:
            out[self.place.dim(step)] = self.own[self.place.dim(step)]
        if flip:
            d = self.place.dim(self.orders[m][s])
            out[d] = 1 - self.own[d]
        return out

    def later(self, m, index):
        out = list(index)
        del out[self.place.dim(self.orders[m][0])]
        return tuple(out)

    def copy(self, m, s):
        src, _, piece, _ = self.chunks[m]
        index = self.index(m, s, True)
        here = src.at[tuple(index) + piece] if s == 0 else self.landed[m][0].at[self.later(m, index)]
        return pltpu.make_async_remote_copy(
            src_ref=here,
            dst_ref=self.landed[m][s],
            send_sem=self.send.at[m, s],
            recv_sem=self.recv.at[m, s],
            device_id=self.place.partner(self.orders[m][s]),
            device_id_type=MESH,
        )

    def keep(self, m):
        src, _, piece, _ = self.chunks[m]
        index = self.index(m, 0, False)
        return pltpu.make_async_copy(src.at[tuple(index) + piece], self.staged[m], self.local.at[m])

    def add(self, m, s):
        total, index = self.landed[m][0], self.later(m, self.index(m, s, False))
        other = self.staged[m] if s == 0 else self.landed[m][s]
        if s == self.steps - 1:
            out, piece = self.chunks[m][1], self.chunks[m][2]
            value = total[index].astype(F32) + other[...].astype(F32)
            out[piece if piece else ...] = value
            return
        free = [d for d, v in enumerate(index) if isinstance(v, slice)]

        def one(i, carry):
            at, bits = list(index), []
            for j, d in enumerate(free):
                at[d] = lax.rem(i // (1 << (len(free) - 1 - j)), 2)
                bits.append(at[d])
            value = total[tuple(at)].astype(F32) + other[tuple(bits)].astype(F32)
            total[tuple(at)] = value.astype(total.dtype)
            return carry

        lax.fori_loop(0, 1 << len(free), one, 0)

    def event(self, unit, s):
        for m in unit:
            if s == 1:
                self.keep(m).start()
        for m in unit:
            if s > 0:
                self.copy(m, s - 1).wait_recv()
                if s == 1:
                    self.keep(m).wait()
                self.add(m, s - 1)
            if s < self.steps:
                self.copy(m, s).start()

    def finish(self):
        for m in range(len(self.chunks)):
            for s in range(self.steps):
                self.copy(m, s).wait_send()


def wave_events(units, steps):
    waves = []
    for t in range(units + steps):
        waves.append([(t - k, k) for k in range(steps, -1, -1) if 0 <= t - k < units])
    return waves


def plan_steps(n, pairs, blocks):
    out = []
    for s in range(n):
        out += [("attend", s, p) for p in range(pairs)]
        if s == n - 1:
            out += [("weights", 0, c) for c in range(blocks)]
        out += [("tokens", s, r) for r in range(blocks)]
    return out


def span(plan, kind, s=None):
    at = [i for i, step in enumerate(plan) if step[0] == kind and s in (None, step[1])]
    return at[0], at[-1] + 1


def back_kernel(a, b, plan, unit_list, wave_steps, slot, temper, *refs):
    bias_ref, q_ref, k_ref, v_ref, ctx_ref, lse_ref, grad_ref = refs[:7]
    x_ref, gf_ref, wq_ref, wk_ref, wv_ref = refs[7:12]
    vec, g_wo, g_w1, g_w2 = refs[12:16]
    out_tokens, out_vec, out_bias = refs[16:19]
    outs = refs[19:25]
    rest = refs[25:]
    gq_s, gk_s, gv_s, sum_q, sum_k, sum_v, bias_s, tok_s = rest[:8]
    send, recv, local, tok_send, tok_recv, tok_local = rest[8:14]
    rest = rest[14:]
    steps = a + b
    sources = {0: sum_q, 1: sum_k, 2: sum_v, 3: g_wo, 4: g_w1, 5: g_w2}
    chunks, units = [(vec, out_vec, (), 0)], []
    for unit in unit_list:
        ids = []
        for at, r, c, color in unit:
            ids.append(len(chunks))
            chunks.append((sources[at], outs[at], (r, c), color))
        units.append(ids)
    units[0] = [0] + units[0]
    units[-1] = units[-1] + [len(chunks)]
    chunks.append((bias_s, out_bias, (), 0))
    landed = [rest[m * steps : (m + 1) * steps] for m in range(len(chunks))]
    staged = rest[len(chunks) * steps :]
    sums = Sums(a, b, chunks, landed, [staged[k] for k in slot], send, recv, local)
    place = sums.place
    i = pl.program_id(0)
    n, length, width = gq_s.shape
    sp = 1 << b

    @pl.when(i == 0)
    def _():
        place.greet()

    def token_moves(s):
        out = [pltpu.make_async_copy(tok_s.at[s, place.z], out_tokens.at[place.z, s], tok_local.at[s])]
        for k in range(1, sp):
            to = lax.rem(place.z + k, sp)
            out.append(
                pltpu.make_async_remote_copy(
                    src_ref=tok_s.at[s, to],
                    dst_ref=out_tokens.at[place.z, s],
                    send_sem=tok_send.at[s, k - 1],
                    recv_sem=tok_recv.at[s, k - 1],
                    device_id=(place.f, to),
                    device_id_type=MESH,
                )
            )
        return out

    for s in range(n):
        lo, hi = span(plan, "attend", s)

        @pl.when(jnp.logical_and(i >= lo, i < hi))
        def _(s=s, lo=lo):
            columns = pl.ds(pl.multiple_of((i - lo) * 2 * HD, 2 * HD), 2 * HD)
            gq, gk, gv = attend_back_pair(temper, bias_ref, q_ref, k_ref, v_ref, ctx_ref, lse_ref, grad_ref)
            gq_s[s, :, columns] = gq
            gk_s[s, :, columns] = gk
            gv_s[s, :, columns] = gv

        lo, hi = span(plan, "tokens", s)

        @pl.when(jnp.logical_and(i >= lo, i < hi))
        def _(s=s, lo=lo, hi=hi):
            wide = wq_ref.shape[0]
            columns = pl.ds(pl.multiple_of((i - lo) * wide, wide), wide)
            total = dot_nt(gq_s[s], wq_ref[...]) + dot_nt(gk_s[s], wk_ref[...]) + dot_nt(gv_s[s], wv_ref[...])
            total = total + gf_ref[...].reshape(length, wide)
            tok_s[s, :, :, columns] = total.astype(BF).reshape(sp, length // sp, wide)

            @pl.when(i == hi - 1)
            def _():
                for move in token_moves(s):
                    move.start()

    lo, hi = span(plan, "weights")

    @pl.when(jnp.logical_and(i >= lo, i < hi))
    def _():
        wide = wq_ref.shape[0]
        columns = pl.ds(pl.multiple_of((i - lo) * wide, wide), wide)
        for held, total in ((gq_s, sum_q), (gk_s, sum_k), (gv_s, sum_v)):
            value = sum(dot_tn(x_ref[:, s].reshape(length, width), held[s, :, columns]) for s in range(n))
            shape = total.shape[:-1] + (wide,)
            total[..., columns] = value.astype(BF).reshape(shape)

        @pl.when(i == hi - 1)
        def _():
            for at, held in enumerate((gq_s, gv_s)):
                row = sum(jnp.sum(held[s].astype(F32), axis=0, keepdims=True) for s in range(n))
                rows = bias_s.shape[-2] // 2
                wide = width // rows
                for r in range(rows):
                    cut = row[:, r * wide : (r + 1) * wide].reshape((1,) * steps + (1, wide))
                    bias_s[..., at * rows + r : at * rows + r + 1, :] = jnp.broadcast_to(cut, (2,) * steps + (1, wide))

    waves = wave_events(len(units), steps)
    for k in sorted(set(wave_steps)):

        @pl.when(i == k)
        def _(k=k):
            for wave, at in zip(waves, wave_steps):
                if at == k:
                    for unit, s in wave:
                        sums.event(units[unit], s)

    @pl.when(i == len(plan) - 1)
    def _():
        sums.finish()
        for s in range(n):
            for move in token_moves(s):
                move.wait()


def staging_plan(sizes, types, units):
    keys, slot = [], [0] * len(sizes)
    for ids in units:
        seen = []
        for m in ids:
            key = (sizes[m], types[m])
            key += (seen.count(key),)
            seen.append(key[:2])
            if key not in keys:
                keys.append(key)
            slot[m] = keys.index(key)
    return slot, keys


def back(a, b, bias, q, k, v, ctx, lse, grad_ctx, x, grad_first, wq, wk, wv, vec, g_wo, g_w1, g_w2):
    lead, steps = (2,) * (a + b), a + b
    s, n, t, width = q.shape
    pairs, blocks = width // (2 * HD), 4
    wide = width // blocks
    length = s * t
    plan = plan_steps(n, pairs, blocks)
    rows = width >> steps
    shapes = [(rows, width)] * 4 + [g_w1.shape[steps:], g_w2.shape[steps:]]
    unit_list = make_units(shapes, SUM_PAIRS)
    n_waves = len(unit_list) + steps
    w_end = span(plan, "weights")[1]
    last = len(plan) - 1
    early = len(unit_list) - 2
    wave_steps = []
    for wave in range(n_waves):
        if wave < early:
            wave_steps.append(min(WAVE_STEPS[wave], w_end - 1) if wave < len(WAVE_STEPS) else w_end - 1)
        else:
            wave_steps.append(max(w_end, min(last, w_end + (wave - early))))
    sizes = [vec.shape[steps:]] + [(r.size, c.size) for unit in unit_list for _, r, c, _ in unit]
    sizes.append((2 * width // 128, 128))
    types = [F32] + [BF] * (len(sizes) - 2) + [F32]

    turn = pairs + blocks

    def at_head(i):
        seq = jnp.minimum(i // turn, n - 1)
        return seq, jnp.minimum(i - seq * turn, pairs - 1)

    def at_tokens(i):
        ends = i >= (n - 1) * turn + pairs + blocks
        seq = jnp.where(ends, n - 1, jnp.clip((i - pairs) // turn, 0, max(n - 2, 0)))
        start = pairs + seq * turn + jnp.where(seq == n - 1, blocks, 0)
        return seq, jnp.clip(i - start, 0, blocks - 1)

    def head_map(i):
        seq, pair = at_head(i)
        return (0, seq, 0, pair)

    def lse_map(i):
        seq, pair = at_head(i)
        return (seq, pair, 0, 0)

    def token_map(i):
        seq, block = at_tokens(i)
        return (0, seq, 0, block)

    def weight_map(i):
        return (at_tokens(i)[1], 0)

    head = pl.BlockSpec((s, 1, t, 2 * HD), head_map)
    weight = pl.BlockSpec((wide, width), weight_map)
    anyspace = pl.BlockSpec(memory_space=pl.ANY)
    in_specs = [pl.BlockSpec((1, 1, length), lambda i: (at_head(i)[0], 0, 0))] + [head] * 4
    in_specs += [pl.BlockSpec((1, 1, 8, length), lse_map), head]
    in_specs += [pl.BlockSpec(x.shape, lambda i: (0, 0, 0, 0), pipeline_mode=pl.Buffered(1))]
    in_specs += [pl.BlockSpec((s, 1, t, wide), token_map)] + [weight] * 3
    in_specs += [anyspace] * 4
    outs = [jax.ShapeDtypeStruct((s, n, t, width), BF)]
    outs += [jax.ShapeDtypeStruct(sizes[0], F32), jax.ShapeDtypeStruct(sizes[-1], F32)]
    outs += [jax.ShapeDtypeStruct(shape, F32) for shape in shapes]
    vmem = pl.BlockSpec(memory_space=pltpu.VMEM)
    n_chunks = len(sizes)
    scratch = [pltpu.VMEM((n, length, width), BF)] * 3
    scratch += [pltpu.VMEM(lead + (rows, width), BF)] * 3
    scratch += [pltpu.VMEM(lead + sizes[-1], F32), pltpu.VMEM((n, s, t, width), BF)]
    scratch += [
        pltpu.SemaphoreType.DMA((n_chunks, steps)),
        pltpu.SemaphoreType.DMA((n_chunks, steps)),
        pltpu.SemaphoreType.DMA((n_chunks,)),
        pltpu.SemaphoreType.DMA((n, s - 1)),
        pltpu.SemaphoreType.DMA((n, s - 1)),
        pltpu.SemaphoreType.DMA((n,)),
    ]
    for size, kind in zip(sizes, types):
        scratch += [pltpu.VMEM((2,) * (steps - 1 - j) + size, kind) for j in range(steps)]
    ids, at = [], 1
    for unit in unit_list:
        ids.append(list(range(at, at + len(unit))))
        at += len(unit)
    ids[0] = [0] + ids[0]
    ids[-1] = ids[-1] + [at]
    slot, keys = staging_plan(sizes, types, ids)
    scratch += [pltpu.VMEM((2,) * (steps - 1) + size, kind) for size, kind, _ in keys]
    return pl.pallas_call(
        functools.partial(back_kernel, a, b, plan, unit_list, wave_steps, slot, 1.0 / math.sqrt(HD)),
        grid=(len(plan),),
        out_shape=outs,
        in_specs=in_specs,
        out_specs=[anyspace] + [vmem] * (len(outs) - 1),
        scratch_shapes=scratch,
        compiler_params=pltpu.CompilerParams(
            collective_id=1, has_side_effects=True, vmem_limit_bytes=60 * MIB
        ),
        name="back_and_sum",
    )(bias, q, k, v, ctx, lse, grad_ctx, x, grad_first, wq, wk, wv, vec, g_wo, g_w1, g_w2)


def norm_forward(hidden, gain, shift):
    average = jnp.mean(hidden, axis=-1, keepdims=True)
    centred = hidden - average
    scale = lax.rsqrt(jnp.mean(centred * centred, axis=-1, keepdims=True) + 1e-12)
    xhat = centred * scale
    return xhat * gain + shift, xhat, scale


def norm_backward(grad, gain, xhat, scale):
    scaled = grad * gain
    lead = jnp.mean(scaled, axis=-1, keepdims=True)
    slope = jnp.mean(scaled * xhat, axis=-1, keepdims=True)
    return scale * (scaled - lead - xhat * slope)


def gelu_pair(x):
    cdf = 0.5 * (1.0 + lax.erf(x * (1.0 / math.sqrt(2.0))))
    pdf = jnp.exp(-0.5 * x * x) * (1.0 / math.sqrt(2.0 * math.pi))
    return x * cdf, cdf + x * pdf


def body(tokens, validity, teacher, wq, bq, wk, wv, bv, wo, bo, gain1, shift1, w1, b1, w2, b2, gain2, shift2):
    fs, sp = lax.axis_size("fsdp"), lax.axis_size("sp")
    a, b = bits_of(fs), bits_of(sp)
    devices = fs * sp
    seqs, part, width = tokens.shape
    n = seqs // sp
    length = part * sp
    rows = sp * n * part
    total_tokens = rows * devices
    z = lax.axis_index("sp")
    shard_shape = (sp, n, part, width)

    mine = lax.dynamic_slice_in_dim(validity, z * n, n, 0)
    count = jnp.sum(mine)
    vectors = (bq, bv, bo, gain1, shift1, b2, gain2, shift2, b1)
    sizes = [v.shape[0] for v in vectors]
    held = jnp.concatenate(list(vectors) + [jnp.stack([count // 32, count % 32]).astype(BF)])
    vec = jnp.pad(held, (0, 16 * 128 - held.shape[0])).reshape(16, 128)

    shards = (wq, wk, wv, wo, w1, w2)
    got = front(a, b, tokens.reshape(shard_shape), vec, shards)
    moved, vec_all = got[0], got[1].reshape(devices, -1)
    WQ, WK, WV, WO, W1, W2 = (
        g.reshape((devices * w.shape[0],) + w.shape[1:]) for g, w in zip(got[2:], shards)
    )
    full, at = [], 0
    for size in sizes:
        full.append(vec_all[:, at : at + size].reshape(-1).astype(F32))
        at += size
    BQ, BV, BO, G1, S1, B2, G2, S2, B1 = full
    counted = jnp.sum(vec_all[:, at].astype(F32)) * 32.0 + jnp.sum(vec_all[:, at + 1].astype(F32))

    teacher_moved = lax.all_to_all(
        lax.optimization_barrier((teacher, moved))[0].reshape(shard_shape), "sp", split_axis=0, concat_axis=0
    ).reshape(rows, width)

    valid = mine.astype(F32)
    bias = ((valid - 1.0) * 1e9).reshape(n, 1, length)
    mask_rows = jnp.swapaxes(valid.reshape(n, sp, part), 0, 1).reshape(rows, 1)

    x = moved.reshape(rows, width)
    q = (dot_nn(x, WQ) + BQ).astype(BF)
    k = dot_nn(x, WK).astype(BF)
    v = (dot_nn(x, WV) + BV).astype(BF)
    ctx, lse = attend(bias, *(p.reshape(shard_shape) for p in (q, k, v)))
    ctx_rows = ctx.reshape(rows, width)
    first = x.astype(F32) + dot_nn(ctx_rows, WO) + BO
    normed, xhat1, scale1 = norm_forward(first, G1, S1)
    normed_low = normed.astype(BF)
    inner = dot_nn(normed_low, W1) + B1
    active, slope = gelu_pair(inner)
    active_low = active.astype(BF)
    slope = slope.astype(BF)
    second = normed + dot_nn(active_low, W2) + B2
    final, xhat2, scale2 = norm_forward(second, G2, S2)
    error = final - teacher_moved.astype(F32)
    local_loss = jnp.sum(mask_rows * error * error)
    output = lax.all_to_all(final.astype(BF).reshape(shard_shape), "sp", split_axis=0, concat_axis=0)

    grad_final = (2.0 * total_tokens / counted) * mask_rows * error
    grad_second = norm_backward(grad_final, G2, xhat2, scale2)
    grad_outer = grad_second.astype(BF)
    g_w2 = dot_tn(active_low, grad_outer).astype(BF)
    grad_inner = (dot_nt(grad_outer, W2) * slope.astype(F32)).astype(BF)
    g_w1 = dot_tn(normed_low, grad_inner).astype(BF)
    grad_normed = dot_nt(grad_inner, W1) + grad_second
    grad_first = norm_backward(grad_normed, G1, xhat1, scale1)
    grad_attended = grad_first.astype(BF)
    g_wo = dot_tn(ctx_rows, grad_attended).astype(BF)
    grad_ctx = dot_nt(grad_attended, WO).astype(BF)

    def column_sum(value):
        return jnp.sum(value.astype(F32), axis=0)

    vector_grads = (
        column_sum(grad_attended),
        jnp.sum(grad_normed * xhat1, axis=0),
        column_sum(grad_normed),
        column_sum(grad_outer),
        jnp.sum(grad_final * xhat2, axis=0),
        column_sum(grad_final),
        column_sum(grad_inner),
    )
    parts = [g.reshape(devices, -1) for g in vector_grads]
    parts.append(jnp.broadcast_to(local_loss, (devices, 1)))
    packed = jnp.concatenate(parts, axis=1)
    packed = jnp.pad(packed, ((0, 0), (0, 8 * 128 - packed.shape[1])))
    lead = (2,) * (a + b)
    summed = back(
        a,
        b,
        bias,
        *(p.reshape(shard_shape) for p in (q, k, v)),
        ctx,
        lse,
        grad_ctx.reshape(shard_shape),
        moved,
        grad_first.reshape(shard_shape),
        WQ,
        WK,
        WV,
        packed.reshape(lead + (8, 128)),
        *(g.reshape(lead + w.shape) for g, w in ((g_wo, wo), (g_w1, w1), (g_w2, w2))),
    )
    home = summed[0].reshape(seqs, part, width).astype(F32)
    own = summed[1].reshape(-1)
    small, at = [], 0
    for g in vector_grads:
        size = g.shape[0] // devices
        small.append(own[at : at + size])
        at += size
    loss = own[at] / (width * counted)
    d_bo, d_g1, d_s1, d_b2, d_g2, d_s2, d_b1 = small
    whole_sums = summed[2].reshape(2, width)
    mine_at = (lax.axis_index("fsdp") * sp + z) * (width // devices)
    d_bq, d_bv = (lax.dynamic_slice_in_dim(w, mine_at, width // devices, 0) for w in whole_sums)
    d_wq, d_wk, d_wv, d_wo, d_w1, d_w2 = summed[3:]
    return (
        output.reshape(seqs, part, width),
        loss,
        home,
        d_wq,
        d_bq,
        d_wk,
        d_wv,
        d_bv,
        d_wo,
        d_bo,
        d_g1,
        d_s1,
        d_w1,
        d_b1,
        d_w2,
        d_b2,
        d_g2,
        d_s2,
    )


def solution(mesh):
    tokens = P("fsdp", "sp", None)
    matrix = P(AXES, None)
    vector = P(AXES)
    return jax.shard_map(
        body,
        mesh=mesh,
        in_specs=(
            tokens,
            P("fsdp", None),
            tokens,
            matrix,
            vector,
            matrix,
            matrix,
            vector,
            matrix,
            vector,
            vector,
            vector,
            matrix,
            vector,
            matrix,
            vector,
            vector,
            vector,
        ),
        out_specs=(
            tokens,
            P(),
            tokens,
            matrix,
            vector,
            matrix,
            matrix,
            vector,
            matrix,
            vector,
            vector,
            vector,
            matrix,
            vector,
            matrix,
            vector,
            vector,
            vector,
        ),
        check_vma=False,
    )
```

```python
import functools
import math

import jax
import jax.numpy as jnp
from jax import lax
from jax.experimental import pallas as pl
from jax.experimental.pallas import tpu as pltpu
from jax.sharding import PartitionSpec as P

HD = 64
BF = jnp.bfloat16
F32 = jnp.float32
MESH = pl.DeviceIdType.MESH
AXES = ("fsdp", "sp")
MIB = 1 << 20
GATHER_PAIRS = ((0, 1, 1), (2, 3, 1), (4, 5, 4))


def bits_of(n):
    return n.bit_length() - 1


def gather_steps(a, b, color):
    z = [("sp", k) for k in reversed(range(b))]
    f = [("fsdp", k) for k in reversed(range(a))]
    if color and a >= 2:
        f[0], f[1] = f[1], f[0]
    return z + f


class Place:
    def __init__(self, a, b):
        self.a, self.b = a, b
        self.f = lax.axis_index("fsdp")
        self.z = lax.axis_index("sp")

    def dim(self, step):
        axis, k = step
        return self.a - 1 - k if axis == "fsdp" else self.a + self.b - 1 - k

    def bit(self, step):
        axis, k = step
        me = self.f if axis == "fsdp" else self.z
        return lax.rem(me // (1 << k), 2)

    def own(self):
        out = [None] * (self.a + self.b)
        for step in gather_steps(self.a, self.b, 0):
            out[self.dim(step)] = self.bit(step)
        return out

    def partner(self, step):
        axis, k = step
        change = (1 - 2 * self.bit(step)) * (1 << k)
        if axis == "fsdp":
            return (self.f + change, self.z)
        return (self.f, self.z + change)

    def greet(self):
        barrier = pltpu.get_barrier_semaphore()
        s = 1 << self.b
        others = [(self.f, lax.rem(self.z + k, s)) for k in range(1, s)]
        others += [self.partner(("fsdp", k)) for k in range(self.a)]
        for other in others:
            pl.semaphore_signal(barrier, inc=1, device_id=other, device_id_type=MESH)
        pl.semaphore_wait(barrier, len(others))


def exchange_tokens(place, src, dst, send, recv, local):
    s = 1 << place.b
    copies = [pltpu.make_async_copy(src.at[place.z], dst.at[place.z], local)]
    for k in range(1, s):
        to = lax.rem(place.z + k, s)
        copies.append(
            pltpu.make_async_remote_copy(
                src_ref=src.at[to],
                dst_ref=dst.at[place.z],
                send_sem=send.at[k - 1],
                recv_sem=recv.at[k - 1],
                device_id=(place.f, to),
                device_id_type=MESH,
            )
        )
    return copies


def pieces(rows, columns, parts_r, parts_c):
    out = []
    for i in range(parts_r):
        for j in range(parts_c):
            out.append(
                (
                    pl.ds(i * (rows // parts_r), rows // parts_r),
                    pl.ds(j * (columns // parts_c), columns // parts_c),
                )
            )
    return out


def make_units(shapes, pairs):
    units = []
    for x, y, n in pairs:
        (rx, cx), (ry, cy) = shapes[x], shapes[y]
        if x == y:
            left, right = pieces(rx, cx, 1, 2)
            units.append([(x,) + left + (0,), (y,) + right + (1,)])
            continue
        ny = max(1, min(n, ry // 16)) if ry > rx else 1
        xs = pieces(rx, cx, 1, n)
        ys = pieces(ry, cy, ny, 1)
        for k in range(n):
            unit = [(x,) + xs[k] + (0,)]
            if k < ny:
                unit.append((y,) + ys[k] + (1,))
            units.append(unit)
    return units


def front_kernel(a, b, units, *refs):
    n_mat = 6
    tokens, vec = refs[0], refs[1]
    shards = refs[2 : 2 + n_mat]
    out_tokens, out_vec = refs[2 + n_mat], refs[3 + n_mat]
    outs = refs[4 + n_mat : 4 + 2 * n_mat]
    send, recv, local, tok_send, tok_recv, tok_local = refs[4 + 2 * n_mat :]
    place = Place(a, b)
    own = place.own()
    chunks = [[(vec, out_vec, (), 0)] + [(shards[at], outs[at], (r, c), color) for at, r, c, color in units[0]]]
    for unit in units[1:]:
        chunks.append([(shards[at], outs[at], (r, c), color) for at, r, c, color in unit])
    flat = [chunk for unit in chunks for chunk in unit]
    number = {}
    for u, unit in enumerate(chunks):
        for i in range(len(unit)):
            number[u, i] = len(number)
    steps = a + b

    def copy_of(m, s):
        src, out, piece, color = flat[m]
        order = gather_steps(a, b, color)
        index = list(own)
        for step in order[:s]:
            index[place.dim(step)] = slice(None)
        there = out.at[tuple(index) + piece]
        here = (src.at[piece] if piece else src) if s == 0 else there
        return pltpu.make_async_remote_copy(
            src_ref=here,
            dst_ref=there,
            send_sem=send.at[m, s],
            recv_sem=recv.at[m, s],
            device_id=place.partner(order[s]),
            device_id_type=MESH,
        )

    def keep_of(m):
        src, out, piece, _ = flat[m]
        return pltpu.make_async_copy(
            src.at[piece] if piece else src, out.at[tuple(own) + piece], local.at[m]
        )

    for m in range(len(flat)):
        keep_of(m).start()
    place.greet()
    moves = exchange_tokens(place, tokens, out_tokens, tok_send, tok_recv, tok_local)
    lead = [b + 1, b] + list(range(b - 1, -1, -1)) + list(range(b + 2, steps + 1))
    events = [(u + k, lead.index(k), u, k) for u in range(len(chunks)) for k in range(steps + 1)]
    events.append((len(chunks) + 0.5, 0, -1, -1))
    for _, _, u, k in sorted(events):
        if u < 0:
            for move in moves:
                move.start()
            continue
        for i in range(len(chunks[u])):
            m = number[u, i]
            if k == 1:
                keep_of(m).wait()
            if k > 0:
                copy_of(m, k - 1).wait_recv()
            if k < steps:
                copy_of(m, k).start()
    for m in range(len(flat)):
        for k in range(steps):
            copy_of(m, k).wait_send()
    for move in moves:
        move.wait()


def front(a, b, tokens, vec, shards):
    lead = (2,) * (a + b)
    units = make_units([w.shape for w in shards], GATHER_PAIRS)
    n_chunks = 1 + sum(len(u) for u in units)
    steps = a + b
    anyspace = pl.BlockSpec(memory_space=pl.ANY)
    outs = [jax.ShapeDtypeStruct(tokens.shape, tokens.dtype), jax.ShapeDtypeStruct(lead + vec.shape, vec.dtype)]
    outs += [jax.ShapeDtypeStruct(lead + w.shape, w.dtype) for w in shards]
    s = 1 << b
    return pl.pallas_call(
        functools.partial(front_kernel, a, b, units),
        out_shape=outs,
        in_specs=[anyspace] * (2 + len(shards)),
        out_specs=[anyspace] * len(outs),
        scratch_shapes=[
            pltpu.SemaphoreType.DMA((n_chunks, steps)),
            pltpu.SemaphoreType.DMA((n_chunks, steps)),
            pltpu.SemaphoreType.DMA((n_chunks,)),
            pltpu.SemaphoreType.DMA((s - 1,)),
            pltpu.SemaphoreType.DMA((s - 1,)),
            pltpu.SemaphoreType.DMA,
        ],
        compiler_params=pltpu.CompilerParams(collective_id=0, has_side_effects=True),
        name="gather_weights",
    )(tokens, vec, *shards)


def head_mask(head):
    lane = lax.broadcasted_iota(jnp.int32, (1, 2 * HD), 1)
    return (lane // HD == head).astype(F32)


def dot_nt(x, y):
    return lax.dot_general(x, y, (((1,), (1,)), ((), ())), preferred_element_type=F32)


def dot_tn(x, y):
    return lax.dot_general(x, y, (((0,), (0,)), ((), ())), preferred_element_type=F32)


def dot_nn(x, y):
    return lax.dot_general(x, y, (((1,), (0,)), ((), ())), preferred_element_type=F32)


def attend_kernel(temper, bias_ref, q_ref, k_ref, v_ref, ctx_ref, lse_ref):
    length = bias_ref.shape[-1]
    shape = q_ref.shape
    q = q_ref[...].reshape(length, shape[-1])
    k = k_ref[...].reshape(length, shape[-1])
    v = v_ref[...].reshape(length, shape[-1])
    bias = bias_ref[...].reshape(1, length)
    total = jnp.zeros((length, shape[-1]), F32)
    logs = jnp.zeros((length, shape[-1]), F32)
    for head in range(2):
        mask = head_mask(head)
        scores = dot_nt(q, k * (mask * temper).astype(BF)) + bias
        largest = jnp.max(scores, axis=-1, keepdims=True)
        raised = jnp.exp(scores - largest)
        summed = jnp.sum(raised, axis=-1, keepdims=True)
        part = dot_nn(raised.astype(BF), v * mask.astype(BF))
        total = total + part * (1.0 / summed)
        logs = logs + (largest + jnp.log(summed)) * mask
    ctx_ref[...] = total.astype(BF).reshape(shape)
    turned = jnp.transpose(logs)
    for head in range(2):
        lse_ref[0, 0, head : head + 1] = turned[head * HD : head * HD + 1]


def attend(bias, q, k, v):
    s, n, t, width = q.shape
    rows = pl.BlockSpec((s, 1, t, 2 * HD), lambda i, j: (0, i, 0, j))
    return pl.pallas_call(
        functools.partial(attend_kernel, 1.0 / math.sqrt(HD)),
        grid=(n, width // (2 * HD)),
        out_shape=[
            jax.ShapeDtypeStruct(q.shape, BF),
            jax.ShapeDtypeStruct((n, width // (2 * HD), 8, s * t), F32),
        ],
        in_specs=[pl.BlockSpec((1, 1, s * t), lambda i, j: (i, 0, 0)), rows, rows, rows],
        out_specs=[rows, pl.BlockSpec((1, 1, 8, s * t), lambda i, j: (i, j, 0, 0))],
        compiler_params=pltpu.CompilerParams(vmem_limit_bytes=32 * MIB),
        cost_estimate=pl.CostEstimate(
            flops=4 * n * (s * t) ** 2 * width, bytes_accessed=16 * s * n * t * width, transcendentals=0
        ),
        name="attend",
    )(bias, q, k, v)


def attend_back_pair(temper, key_bias, q, k, v, ctx, logs, grad):
    both = jnp.transpose(grad.astype(F32) * ctx.astype(F32))
    gq = jnp.zeros(q.shape, F32)
    gk = jnp.zeros(q.shape, F32)
    gv = jnp.zeros(q.shape, F32)
    for head in range(2):
        mask = head_mask(head)
        k_head = k * (mask * temper).astype(BF)
        grad_head = grad * mask.astype(BF)
        log_total = logs[head : head + 1]
        inner = jnp.sum(both[head * HD : (head + 1) * HD], axis=0, keepdims=True)
        attention = jnp.exp(dot_nt(k_head, q) + key_bias - log_total)
        gv = gv + dot_nn(attention.astype(BF), grad_head)
        grad_attention = dot_nt(v, grad_head)
        grad_scores = (attention * (grad_attention - inner)).astype(BF)
        gk = gk + dot_nn(grad_scores, q * (mask * temper).astype(BF))
        gq = gq + dot_tn(grad_scores, k_head)
    return gq.astype(BF), gk.astype(BF), gv.astype(BF)


class Sums:
    def __init__(self, a, b, chunks, landed, staged, send, recv, local):
        self.place = Place(a, b)
        self.own = self.place.own()
        self.steps = a + b
        self.chunks, self.landed, self.staged = chunks, landed, staged
        self.send, self.recv, self.local = send, recv, local
        self.orders = [gather_steps(a, b, c[3])[::-1] for c in chunks]

    def index(self, m, s, flip):
        out = [slice(None)] * self.steps
        for step in self.orders[m][: s + 1]:
            out[self.place.dim(step)] = self.own[self.place.dim(step)]
        if flip:
            d = self.place.dim(self.orders[m][s])
            out[d] = 1 - self.own[d]
        return out

    def later(self, m, index):
        out = list(index)
        del out[self.place.dim(self.orders[m][0])]
        return tuple(out)

    def copy(self, m, s):
        src, _, piece, _ = self.chunks[m]
        index = self.index(m, s, True)
        here = src.at[tuple(index) + piece] if s == 0 else self.landed[m][0].at[self.later(m, index)]
        return pltpu.make_async_remote_copy(
            src_ref=here,
            dst_ref=self.landed[m][s],
            send_sem=self.send.at[m, s],
            recv_sem=self.recv.at[m, s],
            device_id=self.place.partner(self.orders[m][s]),
            device_id_type=MESH,
        )

    def keep(self, m):
        src, _, piece, _ = self.chunks[m]
        index = self.index(m, 0, False)
        return pltpu.make_async_copy(src.at[tuple(index) + piece], self.staged[m], self.local.at[m])

    def add(self, m, s):
        total, index = self.landed[m][0], self.later(m, self.index(m, s, False))
        other = self.landed[m][s]
        if s == 0:
            src, _, piece, _ = self.chunks[m]
            other = self.staged[m]
            if other is None:
                other = src.at[tuple(self.index(m, 0, False)) + piece]
        if s == self.steps - 1:
            out, piece = self.chunks[m][1], self.chunks[m][2]
            value = total[index].astype(F32) + other[...].astype(F32)
            out[piece] = value
            return
        free = [d for d, v in enumerate(index) if isinstance(v, slice)]

        def one(i, carry):
            at = list(index)
            at[free[0]] = i
            total[tuple(at)] = total[tuple(at)] + other[i]
            return carry

        lax.fori_loop(0, 2, one, 0)

    def event(self, unit, s, load):
        for m in unit:
            if s > 0:
                self.copy(m, s - 1).wait_recv()
                if s == 1 and self.staged[m] is not None:
                    self.keep(m).wait()
                self.add(m, s - 1)
            if s < self.steps:
                self.copy(m, s).start()
            else:
                for k in range(self.steps):
                    self.copy(m, k).wait_send()
        for m in load:
            if self.staged[m] is not None:
                self.keep(m).start()


def plan_steps(n, hidden, parts, blocks):
    out = [("hidden", 0, j) for j in range(hidden)]
    out += [("norm", 0, k) for k in range(parts)]
    out += [("project", 0, r) for r in range(blocks)]
    for s in range(n):
        out += [("attend" if s < n - 1 else "last", s, c) for c in range(blocks)]
        out += [("tokens", s, r) for r in range(blocks)]
    return out


def span(plan, kind, s=None):
    at = [i for i, step in enumerate(plan) if step[0] == kind and s in (None, step[1])]
    return at[0], at[-1] + 1


STEP_US = {"hidden": 6.6, "norm": 1.2, "project": 2.2, "attend": 3.4, "last": 4.8, "tokens": 1.9}
LINK_US = 23.0
CORE_US = 3.0
HOP_US = 2.5
SLACK_US = 0.0
LATE_US = -0.5


def plan_events(plan, units, ready, late, a, b):
    steps = a + b
    ends, now = [], 0.0
    for kind, _, _ in plan:
        now += STEP_US[kind]
        ends.append(now)
    free, events = {}, []
    due = [[ends[r], u, 0] for u, r in enumerate(ready)]
    while due:
        due.sort()
        time, u, k = due.pop(0)
        slack = SLACK_US if u < late else LATE_US
        at = min([i for i, end in enumerate(ends) if end >= time + slack] + [len(plan) - 1])
        start = max(time, ends[at])
        events.append((at, start, u, k))
        if k == steps:
            continue
        came_all = start
        for size, color in units[u]:
            where = gather_steps(a, b, color)[::-1][k]
            cost = CORE_US if where == ("fsdp", 0) else LINK_US
            free[where] = max(free.get(where, 0.0), start) + size / (1 << (k + 1)) * cost
            came_all = max(came_all, free[where])
        due.append([came_all + HOP_US, u, k + 1])
    waiting, order, place = sorted(events), [], {}
    while waiting:
        for i, (at, _, u, k) in enumerate(waiting):
            before = [(u, k - 1)] if k else []
            if k == 1 and u:
                before.append((u - 1, 1))
            if late - 1 <= u < len(units) - 1:
                before.append((u + 1 - late, steps))
            if not all(b in place for b in before):
                continue
            if u < late or k == steps:
                break
            freed = place.get((u - late, steps), len(events))
            if any(place.get((w, k), -1) > freed and (w, k + 1) in place for w in range(u)):
                break
        at, _, u, k = waiting.pop(i)
        place[u, k] = len(order)
        order.append((max(at, order[-1][0]) if order else at, u, k))
    loads = [-1] * len(order)
    for u in range(len(units)):
        loads[place[u, 0] if u == 0 else max(place[u, 0], place[u - 1, 1])] = u
    return [event + (load,) for event, load in zip(order, loads)]


def staging_plan(sizes, types, units, loaded):
    keys, slot = [], [None] * len(sizes)
    for ids in units:
        used = {}
        for m in ids:
            if not loaded[m]:
                slot[m] = (-1, 0, 0)
                continue
            (r, c), kind = sizes[m], types[m]
            for k, (rows, columns, had) in enumerate(keys):
                if rows == r and had == kind and used.get(k, 0) + c <= columns:
                    break
            else:
                k = len(keys)
                keys.append((r, c, kind))
            slot[m] = (k, used.get(k, 0), c)
            used[k] = used.get(k, 0) + c
    return slot, keys


def sum_units(shapes, blocks):
    units = []
    r, c = shapes[4]
    parts = pieces(r, c, 1, 8)
    units += [[(4,) + parts[k] + (0,), (4,) + parts[k + 1] + (1,)] for k in range(0, 8, 2)]
    r, c = shapes[5]
    tall = min(4, r // 16)
    parts = pieces(r, c, tall, 8 // tall)
    units += [[(5,) + parts[k] + (0,), (5,) + parts[k + 1] + (1,)] for k in range(0, 8, 2)]
    r, c = shapes[3]
    left, right = pieces(r, c, 1, 2)
    units.append([(3,) + left + (0,), (3,) + right + (1,)])
    r, c = shapes[0]
    for k in range(blocks):
        whole = pieces(r, c, 1, blocks)[k]
        left, right = pieces(r, c, 1, 2 * blocks)[2 * k : 2 * k + 2]
        units.append([(0,) + whole + (0,), (1,) + whole + (1,), (2,) + left + (0,), (2,) + right + (1,)])
    return units


def bits_index(value, count):
    return tuple(lax.rem(value // (1 << (count - 1 - k)), 2) for k in range(count))


def back_kernel(a, b, plan, unit_list, events, slot, lands, temper, *refs):
    bias_ref, q_ref, k_ref, v_ref, ctx_ref, lse_ref = refs[:6]
    active_ref, slope_ref, w2_ref, w1_ref = refs[6:10]
    xhat_ref, scale_ref, gain_ref, wide_ctx_ref, wo_ref = refs[10:15]
    x_ref, wq_ref, wk_ref, wv_ref = refs[15:19]
    vec_ref, grad_outer, normed_low, grad_second = refs[19:23]
    out_tokens, out_bias = refs[23:25]
    outs = refs[25:31]
    g_wo, g_w1, g_w2 = refs[31:34]
    rest = refs[34:]
    gq_s, gk_s, gv_s, sum_q, sum_k, sum_v, bias_s, tok_s, flow, lines, w2_st = rest[:11]
    send, recv, local, tok_send, tok_recv, tok_local, put = rest[11:18]
    rest = rest[18:]
    steps = a + b
    sources = {0: sum_q, 1: sum_k, 2: sum_v, 3: g_wo, 4: g_w1, 5: g_w2}
    chunks, units = [], []
    for unit in unit_list:
        ids = []
        for at, r, c, color in unit:
            ids.append(len(chunks))
            chunks.append((sources[at], outs[at], (r, c), color))
        units.append(ids)
    units[-1] = units[-1] + [len(chunks)]
    chunks.append((bias_s, out_bias, (slice(None), slice(None)), 0))
    landed = []
    for at, start, size in lands:
        refs_of = rest[at * steps : (at + 1) * steps]
        if size != refs_of[0].shape[-1]:
            refs_of = [
                r.at[(slice(None),) * (len(r.shape) - 1) + (pl.ds(start, size),)] for r in refs_of
            ]
        landed.append(refs_of)
    staged = rest[(1 + max(at for at, _, _ in lands)) * steps :]
    views = []
    for m, (k, start, size) in enumerate(slot):
        if k < 0:
            views.append(None)
            continue
        ref = staged[k]
        if size != ref.shape[-1]:
            ref = ref.at[(slice(None),) * steps + (pl.ds(start, size),)]
        views.append(ref)
    sums = Sums(a, b, chunks, landed, views, send, recv, local)
    place = sums.place
    i = pl.program_id(0)
    n, length, width = gq_s.shape
    sp = 1 << b
    part = length // sp
    rows = n * length
    hidden = span(plan, "hidden")[1]
    wide = wq_ref.shape[0]
    h = w1_ref.shape[1]

    loads = [
        pltpu.make_async_copy(grad_outer, gq_s, put.at[0]),
        pltpu.make_async_copy(normed_low, gk_s, put.at[1]),
        pltpu.make_async_copy(grad_second, flow, put.at[2]),
    ]

    @pl.when(i == 0)
    def _():
        for load in loads:
            load.start()
        place.greet()
        for load in loads:
            load.wait()
        lines[...] = jnp.zeros_like(lines)

    def token_moves(s):
        out = [pltpu.make_async_copy(tok_s.at[s, place.z], out_tokens.at[place.z, s], tok_local.at[s])]
        for k in range(1, sp):
            to = lax.rem(place.z + k, sp)
            out.append(
                pltpu.make_async_remote_copy(
                    src_ref=tok_s.at[s, to],
                    dst_ref=out_tokens.at[place.z, s],
                    send_sem=tok_send.at[s, k - 1],
                    recv_sem=tok_recv.at[s, k - 1],
                    device_id=(place.f, to),
                    device_id_type=MESH,
                )
            )
        return out

    def puts(j):
        at = lax.rem(j, 2)
        columns = pl.ds(pl.multiple_of(j * h, h), h)
        held = pl.ds(pl.multiple_of(at * h, h), h)
        to_w1 = g_w1.at[(slice(None),) * (steps + 1) + (columns,)]
        to_w2 = g_w2.at[bits_index(j, bits_of(hidden))]
        return [
            pltpu.make_async_copy(sum_q.at[(slice(None),) * (steps + 1) + (held,)], to_w1, put.at[3 + at]),
            pltpu.make_async_copy(w2_st.at[at], to_w2, put.at[5 + at]),
        ]

    @pl.when(i < hidden)
    def _():
        at = lax.rem(i, 2)
        grad_out = gq_s[...].reshape(rows, width)
        normed = gk_s[...].reshape(rows, width)
        grad_active = dot_nt(grad_out, w2_ref[...])
        grad_inner = (grad_active * slope_ref[...].astype(F32)).astype(BF)
        columns = pl.ds(pl.multiple_of(i * h, h), h)
        lines[0:1, columns] = jnp.sum(grad_inner.astype(F32), axis=0, keepdims=True)
        value = dot_tn(normed, grad_inner).astype(BF)
        sum_q[..., pl.ds(pl.multiple_of(at * h, h), h)] = value.reshape(sum_q.shape[:-1] + (h,))
        value = dot_tn(active_ref[...], grad_out).astype(BF)
        w2_st[at] = value.reshape(w2_st.shape[1:])
        for p in puts(i):
            p.start()
        flow[...] += dot_nt(grad_inner, w1_ref[...]).reshape(flow.shape)

        @pl.when(i > 0)
        def _():
            for p in puts(i - 1):
                p.wait()

    lo, hi = span(plan, "norm")

    @pl.when(i == lo)
    def _():
        for p in puts(hidden - 1):
            p.wait()

    @pl.when(jnp.logical_and(i >= lo, i < hi))
    def _():
        zb = i - lo
        for s in range(n):
            grad = flow[zb, s]
            xhat = xhat_ref[0, s].astype(F32)
            scaled = grad * gain_ref[...]
            mean = jnp.mean(scaled, axis=-1, keepdims=True)
            slope = jnp.mean(scaled * xhat, axis=-1, keepdims=True)
            first = scale_ref[0, s] * (scaled - mean - xhat * slope)
            flow[zb, s] = first
            low = first.astype(BF)
            tok_s[s, zb] = low
            for at, value in ((1, grad * xhat), (2, grad), (3, low.astype(F32))):
                lines[at : at + 1, :width] += jnp.sum(value, axis=0, keepdims=True)

    lo, hi = span(plan, "project")
    first_attend = hi
    put_wo = pltpu.make_async_copy(sum_v, g_wo, put.at[7])

    @pl.when(jnp.logical_and(i >= lo, i < hi))
    def _():
        r = i - lo
        columns = pl.ds(pl.multiple_of(r * wide, wide), wide)
        total = jnp.zeros((wide, width), F32)
        for s in range(n):
            grad = tok_s[s].reshape(length, width)
            gv_s[s, :, columns] = dot_nt(grad, wo_ref[...]).astype(BF)
            total = total + dot_tn(wide_ctx_ref[:, s].reshape(length, wide), grad)
        index = bits_index(r, bits_of(hi - lo))
        sum_v[index] = total.astype(BF).reshape(sum_v.shape[len(index) :])

        @pl.when(i == hi - 1)
        def _():
            put_wo.start()

    @pl.when(i == first_attend)
    def _():
        put_wo.wait()

    def attend_step(s, c):
        bias_rows = jnp.broadcast_to(bias_ref[...].reshape(1, length), (2 * HD, length))
        key_bias = jnp.transpose(bias_rows)[:, :1]
        for pair in range(wide // (2 * HD)):
            cut = slice(pair * 2 * HD, (pair + 1) * 2 * HD)
            columns = pl.ds(pl.multiple_of(c * wide + pair * 2 * HD, 2 * HD), 2 * HD)
            q, k, v, ctx = (r[:, 0, :, cut].reshape(length, 2 * HD) for r in (q_ref, k_ref, v_ref, ctx_ref))
            logs = lse_ref[0, pair, 0:2]
            gq, gk, gv = attend_back_pair(temper, key_bias, q, k, v, ctx, logs, gv_s[s, :, columns])
            gq_s[s, :, columns] = gq
            gk_s[s, :, columns] = gk
            gv_s[s, :, columns] = gv

    def weights_step(c):
        columns = pl.ds(pl.multiple_of(c * wide, wide), wide)
        for at, held, total in ((4, gq_s, sum_q), (None, gk_s, sum_k), (5, gv_s, sum_v)):
            value = sum(dot_tn(x_ref[:, s].reshape(length, width), held[s, :, columns]) for s in range(n))
            total[..., columns] = value.astype(BF).reshape(total.shape[:-1] + (wide,))
            if at is not None:
                row = sum(jnp.sum(held[s, :, columns].astype(F32), axis=0, keepdims=True) for s in range(n))
                lines[at : at + 1, columns] = row

    for s in range(n):
        lo, hi = span(plan, "attend" if s < n - 1 else "last", s)

        @pl.when(jnp.logical_and(i >= lo, i < hi))
        def _(s=s, lo=lo):
            attend_step(s, i - lo)
            if s == n - 1:
                weights_step(i - lo)

        lo, hi = span(plan, "tokens", s)

        @pl.when(jnp.logical_and(i >= lo, i < hi))
        def _(s=s, lo=lo, hi=hi):
            columns = pl.ds(pl.multiple_of((i - lo) * wide, wide), wide)
            total = dot_nt(gq_s[s], wq_ref[...]) + dot_nt(gk_s[s], wk_ref[...]) + dot_nt(gv_s[s], wv_ref[...])
            total = total + flow[:, s, :, columns].reshape(length, wide)
            tok_s[s, :, :, columns] = total.astype(BF).reshape(sp, part, wide)

            @pl.when(i == hi - 1)
            def _():
                for move in token_moves(s):
                    move.start()

    @pl.when(i == span(plan, "last")[1] - 1)
    def _():
        devices = 1 << steps
        for d in range(devices):
            index = tuple((d >> (steps - 1 - k)) & 1 for k in range(steps))
            for at in range(6):
                size = (hidden * h if at == 0 else width) // devices
                tile = d * size // 128
                bias_s[index + (slice(at, at + 1),)] = lines[at : at + 1, tile * 128 : tile * 128 + 128]
            bias_s[index + (slice(6, 7),)] = vec_ref[d : d + 1]

    for k in sorted({event[0] for event in events}):

        @pl.when(i == k)
        def _(k=k):
            for at, unit, s, load in events:
                if at == k:
                    sums.event(units[unit], s, units[load] if load >= 0 else ())

    @pl.when(i == len(plan) - 1)
    def _():
        for s in range(n):
            for move in token_moves(s):
                move.wait()


def back(a, b, bias, heads, lse, active, slope, W2, W1, xhat, scale, gain, WO, x, WQ, WK, WV, grads, vec):
    q, k, v, ctx = heads
    lead, steps = (2,) * (a + b), a + b
    s, n, t, width = q.shape
    devices = 1 << steps
    hidden, blocks = 8, 4
    h, wide, length, rows = W1.shape[1] // hidden, width // blocks, s * t, s * n * t
    plan = plan_steps(n, hidden, s, blocks)
    own_rows = width // devices
    shapes = [(own_rows, width)] * 4 + [(own_rows, W1.shape[1]), (W2.shape[0] // devices, width)]
    unit_list = sum_units(shapes, blocks)
    first, late = span(plan, "attend" if n > 1 else "last")[0], len(unit_list) - blocks
    ready = [2 * k + 2 for k in range(4)] + [hidden] * 4 + [first]
    ready += list(range(*span(plan, "last")))
    megabytes = [[(r.size * c.size * devices * 2 / MIB, color) for _, r, c, color in u] for u in unit_list]
    events = plan_events(plan, megabytes, ready, late, a, b)
    sizes = [(r.size, c.size) for unit in unit_list for _, r, c, _ in unit] + [(8, 128)]
    types = [BF] * (len(sizes) - 1) + [F32]
    loaded = [at > 2 for unit in unit_list for at, _, _, _ in unit] + [False]
    turn, last = 2 * blocks, n - 1

    def count_from(i, starts):
        return sum([(i >= start).astype(jnp.int32) for start in starts], jnp.int32(0))

    def at_kind(i, begin):
        off = i - begin
        seq = count_from(off, [k * turn for k in range(1, n)])
        return seq, jnp.clip(off - seq * turn, 0, blocks - 1)

    def at_head(i):
        return at_kind(i, first)

    def at_tokens(i):
        return at_kind(i, first + blocks)

    def head_map(i):
        seq, pair = at_head(i)
        return (0, seq, 0, pair)

    def lse_map(i):
        seq, pair = at_head(i)
        return (seq, pair, 0, 0)

    def block_of(kind):
        lo, hi = span(plan, kind)
        return lambda i: jnp.clip(i - lo, 0, hi - lo - 1)

    j_of, z_of, r_of = block_of("hidden"), block_of("norm"), block_of("project")
    head = pl.BlockSpec((s, 1, t, wide), head_map)
    weight = pl.BlockSpec((wide, width), lambda i: (at_tokens(i)[1], 0))
    anyspace = pl.BlockSpec(memory_space=pl.ANY)
    vmem = pl.BlockSpec(memory_space=pltpu.VMEM)
    in_specs = [pl.BlockSpec((1, 1, length), lambda i: (at_head(i)[0], 0, 0))] + [head] * 4
    in_specs += [pl.BlockSpec((1, wide // (2 * HD), 8, length), lse_map)]
    in_specs += [pl.BlockSpec((rows, h), lambda i: (0, j_of(i)))] * 2
    in_specs += [pl.BlockSpec((h, width), lambda i: (j_of(i), 0)), pl.BlockSpec((width, h), lambda i: (0, j_of(i)))]
    in_specs += [pl.BlockSpec((1, n, t, width), lambda i: (z_of(i), 0, 0, 0))]
    in_specs += [pl.BlockSpec((1, n, t, 1), lambda i: (z_of(i), 0, 0, 0))]
    in_specs += [pl.BlockSpec((1, width), lambda i: (0, 0))]
    in_specs += [pl.BlockSpec((s, n, t, wide), lambda i: (0, 0, 0, r_of(i)))]
    in_specs += [pl.BlockSpec((wide, width), lambda i: (r_of(i), 0))]
    in_specs += [pl.BlockSpec(x.shape, lambda i: (0, 0, 0, 0), pipeline_mode=pl.Buffered(1))]
    in_specs += [weight] * 3 + [pl.BlockSpec(vec.shape, lambda i: (0, 0))] + [anyspace] * 3
    outs = [jax.ShapeDtypeStruct((s, n, t, width), BF)]
    outs += [jax.ShapeDtypeStruct(sizes[-1], F32)]
    outs += [jax.ShapeDtypeStruct(shape, F32) for shape in shapes]
    outs += [jax.ShapeDtypeStruct(lead + shapes[m], BF) for m in (3, 4, 5)]
    n_chunks = len(sizes)
    scratch = [pltpu.VMEM((n, length, width), BF)] * 3
    scratch += [pltpu.VMEM(lead + (own_rows, width), BF)] * 3
    scratch += [pltpu.VMEM(lead + sizes[-1], F32), pltpu.VMEM((n, s, t, width), BF)]
    scratch += [pltpu.VMEM((s, n, t, width), F32), pltpu.VMEM((8, W1.shape[1]), F32)]
    scratch += [pltpu.VMEM((2,) + (2,) * (steps - bits_of(hidden)) + shapes[5], BF)]
    scratch += [
        pltpu.SemaphoreType.DMA((n_chunks, steps)),
        pltpu.SemaphoreType.DMA((n_chunks, steps)),
        pltpu.SemaphoreType.DMA((n_chunks,)),
        pltpu.SemaphoreType.DMA((n, s - 1)),
        pltpu.SemaphoreType.DMA((n, s - 1)),
        pltpu.SemaphoreType.DMA((n,)),
        pltpu.SemaphoreType.DMA((8,)),
    ]
    ids, at = [], 0
    for unit in unit_list:
        ids.append(list(range(at, at + len(unit))))
        at += len(unit)
    ids[-1] = ids[-1] + [at]
    slot, keys = staging_plan(sizes, types, ids, loaded)
    lands, held = [None] * len(sizes), []
    for u, unit in enumerate(ids):
        used = {}
        for m in unit:
            if u >= late and m < len(sizes) - 1:
                color = [chunk for each in unit_list for chunk in each][m][3]
                lands[m] = (lands[ids[u - late][color]][0], used.get(color, 0), sizes[m][1])
                used[color] = used.get(color, 0) + sizes[m][1]
            else:
                lands[m] = (len(held), 0, sizes[m][1])
                held.append((sizes[m], types[m]))
    for size, kind in held:
        scratch += [pltpu.VMEM((2,) * (steps - 1 - j) + size, kind) for j in range(steps)]
    scratch += [pltpu.VMEM((2,) * (steps - 1) + (r, c), kind) for r, c, kind in keys]
    grad_outer, normed_low, grad_second = grads
    return pl.pallas_call(
        functools.partial(back_kernel, a, b, plan, unit_list, events, slot, lands, 1.0 / math.sqrt(HD)),
        grid=(len(plan),),
        out_shape=outs,
        in_specs=in_specs,
        out_specs=[anyspace] + [vmem] * 7 + [anyspace] * 3,
        scratch_shapes=scratch,
        compiler_params=pltpu.CompilerParams(
            collective_id=1, has_side_effects=True, vmem_limit_bytes=63 * MIB + MIB * 5 // 8
        ),
        name="back_and_sum",
    )(
        bias,
        q,
        k,
        v,
        ctx,
        lse,
        active,
        slope,
        W2,
        W1,
        xhat,
        scale,
        gain,
        ctx,
        WO,
        x,
        WQ,
        WK,
        WV,
        vec,
        grad_outer,
        normed_low,
        grad_second,
    )


def norm_forward(hidden, gain, shift):
    average = jnp.mean(hidden, axis=-1, keepdims=True)
    centred = hidden - average
    scale = lax.rsqrt(jnp.mean(centred * centred, axis=-1, keepdims=True) + 1e-12)
    xhat = centred * scale
    return xhat * gain + shift, xhat, scale


def norm_backward(grad, gain, xhat, scale):
    scaled = grad * gain
    lead = jnp.mean(scaled, axis=-1, keepdims=True)
    slope = jnp.mean(scaled * xhat, axis=-1, keepdims=True)
    return scale * (scaled - lead - xhat * slope)


def gelu_pair(x):
    cdf = 0.5 * (1.0 + lax.erf(x * (1.0 / math.sqrt(2.0))))
    pdf = jnp.exp(-0.5 * x * x) * (1.0 / math.sqrt(2.0 * math.pi))
    return x * cdf, cdf + x * pdf


def body(tokens, validity, teacher, wq, bq, wk, wv, bv, wo, bo, gain1, shift1, w1, b1, w2, b2, gain2, shift2):
    fs, sp = lax.axis_size("fsdp"), lax.axis_size("sp")
    a, b = bits_of(fs), bits_of(sp)
    devices = fs * sp
    seqs, part, width = tokens.shape
    n = seqs // sp
    length = part * sp
    rows = sp * n * part
    total_tokens = rows * devices
    z = lax.axis_index("sp")
    shard_shape = (sp, n, part, width)

    mine = lax.dynamic_slice_in_dim(validity, z * n, n, 0)
    count = jnp.sum(mine)
    vectors = (bq, bv, bo, gain1, shift1, b2, gain2, shift2, b1)
    sizes = [v.shape[0] for v in vectors]
    held = jnp.concatenate(list(vectors) + [jnp.stack([count // 32, count % 32]).astype(BF)])
    vec = jnp.pad(held, (0, 16 * 128 - held.shape[0])).reshape(16, 128)

    shards = (wq, wk, wv, wo, w1, w2)
    got = front(a, b, tokens.reshape(shard_shape), vec, shards)
    moved, vec_all = got[0], got[1].reshape(devices, -1)
    WQ, WK, WV, WO, W1, W2 = (
        g.reshape((devices * w.shape[0],) + w.shape[1:]) for g, w in zip(got[2:], shards)
    )
    full, at = [], 0
    for size in sizes:
        full.append(vec_all[:, at : at + size].reshape(-1).astype(F32))
        at += size
    BQ, BV, BO, G1, S1, B2, G2, S2, B1 = full
    counted = jnp.sum(vec_all[:, at].astype(F32)) * 32.0 + jnp.sum(vec_all[:, at + 1].astype(F32))

    teacher_moved = lax.all_to_all(
        lax.optimization_barrier((teacher, moved))[0].reshape(shard_shape), "sp", split_axis=0, concat_axis=0
    ).reshape(rows, width)

    valid = mine.astype(F32)
    bias = ((valid - 1.0) * 1e9).reshape(n, 1, length)
    mask_rows = jnp.swapaxes(valid.reshape(n, sp, part), 0, 1).reshape(rows, 1)

    x = moved.reshape(rows, width)
    q = (dot_nn(x, WQ) + BQ).astype(BF)
    k = dot_nn(x, WK).astype(BF)
    v = (dot_nn(x, WV) + BV).astype(BF)
    ctx, lse = attend(bias, *(p.reshape(shard_shape) for p in (q, k, v)))
    ctx_rows = ctx.reshape(rows, width)
    first = x.astype(F32) + dot_nn(ctx_rows, WO) + BO
    normed, xhat1, scale1 = norm_forward(first, G1, S1)
    normed_low = normed.astype(BF)
    inner = dot_nn(normed_low, W1) + B1
    active, slope = gelu_pair(inner)
    active_low = active.astype(BF)
    slope = slope.astype(BF)
    second = normed + dot_nn(active_low, W2) + B2
    final, xhat2, scale2 = norm_forward(second, G2, S2)
    error = final - teacher_moved.astype(F32)
    local_loss = jnp.sum(mask_rows * error * error)
    output = lax.all_to_all(final.astype(BF).reshape(shard_shape), "sp", split_axis=0, concat_axis=0)

    grad_final = (2.0 * total_tokens / counted) * mask_rows * error
    grad_second = norm_backward(grad_final, G2, xhat2, scale2)
    grad_outer = grad_second.astype(BF)

    def column_sum(value):
        return jnp.sum(value.astype(F32), axis=0)

    vector_grads = (column_sum(grad_outer), jnp.sum(grad_final * xhat2, axis=0), column_sum(grad_final))
    parts = [g.reshape(devices, -1) for g in vector_grads]
    parts.append(jnp.broadcast_to(local_loss, (devices, 1)))
    packed = jnp.concatenate(parts, axis=1)
    packed = jnp.pad(packed, ((0, 0), (0, 128 - packed.shape[1])))
    by_rows = (n, length, width)
    summed = back(
        a,
        b,
        bias,
        [p.reshape(shard_shape) for p in (q, k, v)] + [ctx],
        lse,
        active_low,
        slope,
        W2,
        W1,
        xhat1.astype(BF).reshape(shard_shape),
        scale1.reshape(sp, n, part, 1),
        G1.reshape(1, width),
        WO,
        moved,
        WQ,
        WK,
        WV,
        [grad_outer.reshape(by_rows), normed_low.reshape(by_rows), grad_second.reshape(shard_shape)],
        packed,
    )
    home = summed[0].reshape(seqs, part, width).astype(F32)
    own = summed[1][6]
    small, at = [], 0
    for g in vector_grads:
        size = g.shape[0] // devices
        small.append(own[at : at + size])
        at += size
    loss = own[at] / (width * counted)
    d_b2, d_g2, d_s2 = small
    me = lax.axis_index("fsdp") * sp + z
    tiles = []
    for at, size in enumerate((sizes[8],) + (width // devices,) * 5):
        tiles.append(lax.dynamic_slice_in_dim(summed[1][at], lax.rem(me * size, 128), size, 0))
    d_b1, d_g1, d_s1, d_bo, d_bq, d_bv = tiles
    d_wq, d_wk, d_wv, d_wo, d_w1, d_w2 = summed[2:8]
    return (
        output.reshape(seqs, part, width),
        loss,
        home,
        d_wq,
        d_bq,
        d_wk,
        d_wv,
        d_bv,
        d_wo,
        d_bo,
        d_g1,
        d_s1,
        d_w1,
        d_b1,
        d_w2,
        d_b2,
        d_g2,
        d_s2,
    )


def solution(mesh):
    tokens = P("fsdp", "sp", None)
    matrix = P(AXES, None)
    vector = P(AXES)
    return jax.shard_map(
        body,
        mesh=mesh,
        in_specs=(
            tokens,
            P("fsdp", None),
            tokens,
            matrix,
            vector,
            matrix,
            matrix,
            vector,
            matrix,
            vector,
            vector,
            vector,
            matrix,
            vector,
            matrix,
            vector,
            vector,
            vector,
        ),
        out_specs=(
            tokens,
            P(),
            tokens,
            matrix,
            vector,
            matrix,
            matrix,
            vector,
            matrix,
            vector,
            vector,
            vector,
            matrix,
            vector,
            matrix,
            vector,
            vector,
            vector,
        ),
        check_vma=False,
    )
```

```python
import functools
import math

import jax
import jax.numpy as jnp
from jax import lax
from jax.experimental import pallas as pl
from jax.experimental.pallas import tpu as pltpu
from jax.sharding import PartitionSpec as P

HD = 64
BF = jnp.bfloat16
F32 = jnp.float32
MESH = pl.DeviceIdType.MESH
AXES = ("fsdp", "sp")
MIB = 1 << 20
ATTEND_PAIRS = 4
GATHER_PAIRS = ((0, 1, 1), (2, 3, 1), (4, 5, 4))


def bits_of(n):
    return n.bit_length() - 1


def gather_steps(a, b, color):
    z = [("sp", k) for k in reversed(range(b))]
    f = [("fsdp", k) for k in reversed(range(a))]
    if color and a >= 2:
        f[0], f[1] = f[1], f[0]
    return z + f


class Place:
    def __init__(self, a, b):
        self.a, self.b = a, b
        self.f = lax.axis_index("fsdp")
        self.z = lax.axis_index("sp")

    def dim(self, step):
        axis, k = step
        return self.a - 1 - k if axis == "fsdp" else self.a + self.b - 1 - k

    def bit(self, step):
        axis, k = step
        me = self.f if axis == "fsdp" else self.z
        return lax.rem(me // (1 << k), 2)

    def own(self):
        out = [None] * (self.a + self.b)
        for step in gather_steps(self.a, self.b, 0):
            out[self.dim(step)] = self.bit(step)
        return out

    def partner(self, step):
        axis, k = step
        change = (1 - 2 * self.bit(step)) * (1 << k)
        if axis == "fsdp":
            return (self.f + change, self.z)
        return (self.f, self.z + change)

    def greet(self):
        barrier = pltpu.get_barrier_semaphore()
        s = 1 << self.b
        others = [(self.f, lax.rem(self.z + k, s)) for k in range(1, s)]
        others += [self.partner(("fsdp", k)) for k in range(self.a)]
        for other in others:
            pl.semaphore_signal(barrier, inc=1, device_id=other, device_id_type=MESH)
        pl.semaphore_wait(barrier, len(others))


def exchange_tokens(place, src, dst, send, recv, local):
    s = 1 << place.b
    copies = [pltpu.make_async_copy(src.at[place.z], dst.at[place.z], local)]
    for k in range(1, s):
        to = lax.rem(place.z + k, s)
        copies.append(
            pltpu.make_async_remote_copy(
                src_ref=src.at[to],
                dst_ref=dst.at[place.z],
                send_sem=send.at[k - 1],
                recv_sem=recv.at[k - 1],
                device_id=(place.f, to),
                device_id_type=MESH,
            )
        )
    return copies


def pieces(rows, columns, parts_r, parts_c):
    out = []
    for i in range(parts_r):
        for j in range(parts_c):
            out.append(
                (
                    pl.ds(i * (rows // parts_r), rows // parts_r),
                    pl.ds(j * (columns // parts_c), columns // parts_c),
                )
            )
    return out


def make_units(shapes, pairs):
    units = []
    for x, y, n in pairs:
        (rx, cx), (ry, cy) = shapes[x], shapes[y]
        if x == y:
            left, right = pieces(rx, cx, 1, 2)
            units.append([(x,) + left + (0,), (y,) + right + (1,)])
            continue
        ny = max(1, min(n, ry // 16)) if ry > rx else 1
        xs = pieces(rx, cx, 1, n)
        ys = pieces(ry, cy, ny, 1)
        for k in range(n):
            unit = [(x,) + xs[k] + (0,)]
            if k < ny:
                unit.append((y,) + ys[k] + (1,))
            units.append(unit)
    return units


def front_kernel(a, b, units, *refs):
    n_mat = 6
    tokens, vec = refs[0], refs[1]
    shards = refs[2 : 2 + n_mat]
    out_tokens, out_vec = refs[2 + n_mat], refs[3 + n_mat]
    outs = refs[4 + n_mat : 4 + 2 * n_mat]
    send, recv, local, tok_send, tok_recv, tok_local = refs[4 + 2 * n_mat :]
    place = Place(a, b)
    own = place.own()
    chunks = [[(vec, out_vec, (), 0)] + [(shards[at], outs[at], (r, c), color) for at, r, c, color in units[0]]]
    for unit in units[1:]:
        chunks.append([(shards[at], outs[at], (r, c), color) for at, r, c, color in unit])
    flat = [chunk for unit in chunks for chunk in unit]
    number = {}
    for u, unit in enumerate(chunks):
        for i in range(len(unit)):
            number[u, i] = len(number)
    steps = a + b

    def copy_of(m, s):
        src, out, piece, color = flat[m]
        order = gather_steps(a, b, color)
        index = list(own)
        for step in order[:s]:
            index[place.dim(step)] = slice(None)
        there = out.at[tuple(index) + piece]
        here = (src.at[piece] if piece else src) if s == 0 else there
        return pltpu.make_async_remote_copy(
            src_ref=here,
            dst_ref=there,
            send_sem=send.at[m, s],
            recv_sem=recv.at[m, s],
            device_id=place.partner(order[s]),
            device_id_type=MESH,
        )

    def keep_of(m):
        src, out, piece, _ = flat[m]
        return pltpu.make_async_copy(
            src.at[piece] if piece else src, out.at[tuple(own) + piece], local.at[m]
        )

    for m in range(len(flat)):
        keep_of(m).start()
    place.greet()
    moves = exchange_tokens(place, tokens, out_tokens, tok_send, tok_recv, tok_local)
    lead = [b + 1, b] + list(range(b - 1, -1, -1)) + list(range(b + 2, steps + 1))
    events = [(u + k, lead.index(k), u, k) for u in range(len(chunks)) for k in range(steps + 1)]
    events.append((len(chunks) + 0.5, 0, -1, -1))
    for _, _, u, k in sorted(events):
        if u < 0:
            for move in moves:
                move.start()
            continue
        for i in range(len(chunks[u])):
            m = number[u, i]
            if k == 1:
                keep_of(m).wait()
            if k > 0:
                copy_of(m, k - 1).wait_recv()
            if k < steps:
                copy_of(m, k).start()
    for m in range(len(flat)):
        for k in range(steps):
            copy_of(m, k).wait_send()
    for move in moves:
        move.wait()


def front(a, b, tokens, vec, shards):
    lead = (2,) * (a + b)
    units = make_units([w.shape for w in shards], GATHER_PAIRS)
    n_chunks = 1 + sum(len(u) for u in units)
    steps = a + b
    anyspace = pl.BlockSpec(memory_space=pl.ANY)
    outs = [jax.ShapeDtypeStruct(tokens.shape, tokens.dtype), jax.ShapeDtypeStruct(lead + vec.shape, vec.dtype)]
    outs += [jax.ShapeDtypeStruct(lead + w.shape, w.dtype) for w in shards]
    s = 1 << b
    return pl.pallas_call(
        functools.partial(front_kernel, a, b, units),
        out_shape=outs,
        in_specs=[anyspace] * (2 + len(shards)),
        out_specs=[anyspace] * len(outs),
        scratch_shapes=[
            pltpu.SemaphoreType.DMA((n_chunks, steps)),
            pltpu.SemaphoreType.DMA((n_chunks, steps)),
            pltpu.SemaphoreType.DMA((n_chunks,)),
            pltpu.SemaphoreType.DMA((s - 1,)),
            pltpu.SemaphoreType.DMA((s - 1,)),
            pltpu.SemaphoreType.DMA,
        ],
        compiler_params=pltpu.CompilerParams(collective_id=0, has_side_effects=True),
        name="gather_weights",
    )(tokens, vec, *shards)


def head_mask(head):
    lane = lax.broadcasted_iota(jnp.int32, (1, 2 * HD), 1)
    return (lane // HD == head).astype(F32)


def dot_nt(x, y):
    return lax.dot_general(x, y, (((1,), (1,)), ((), ())), preferred_element_type=F32)


def dot_tn(x, y):
    return lax.dot_general(x, y, (((0,), (0,)), ((), ())), preferred_element_type=F32)


def dot_nn(x, y):
    return lax.dot_general(x, y, (((1,), (0,)), ((), ())), preferred_element_type=F32)


def attend_kernel(temper, bias_ref, q_ref, k_ref, v_ref, ctx_ref, lse_ref):
    length = bias_ref.shape[-1]
    shape = q_ref.shape
    bias = bias_ref[...].reshape(1, length)
    for pair in range(shape[-1] // (2 * HD)):
        cut = slice(pair * 2 * HD, (pair + 1) * 2 * HD)
        q, k, v = (ref[:, 0, :, cut].reshape(length, 2 * HD) for ref in (q_ref, k_ref, v_ref))
        total = jnp.zeros((length, 2 * HD), F32)
        logs = jnp.zeros((length, 2 * HD), F32)
        for head in range(2):
            mask = head_mask(head)
            scores = dot_nt(q, k * (mask * temper).astype(BF)) + bias
            largest = jnp.max(scores, axis=-1, keepdims=True)
            raised = jnp.exp(scores - largest)
            summed = jnp.sum(raised, axis=-1, keepdims=True)
            part = dot_nn(raised.astype(BF), v * mask.astype(BF))
            total = total + part * (1.0 / summed)
            logs = logs + (largest + jnp.log(summed)) * mask
        ctx_ref[:, 0, :, cut] = total.astype(BF).reshape(shape[0], shape[2], 2 * HD)
        turned = jnp.transpose(logs)
        for head in range(2):
            lse_ref[0, pair, head : head + 1] = turned[head * HD : head * HD + 1]


def attend(bias, q, k, v):
    s, n, t, width = q.shape
    wide = ATTEND_PAIRS * 2 * HD
    rows = pl.BlockSpec((s, 1, t, wide), lambda i, j: (0, i, 0, j))
    return pl.pallas_call(
        functools.partial(attend_kernel, 1.0 / math.sqrt(HD)),
        grid=(n, width // wide),
        out_shape=[
            jax.ShapeDtypeStruct(q.shape, BF),
            jax.ShapeDtypeStruct((n, width // (2 * HD), 8, s * t), F32),
        ],
        in_specs=[pl.BlockSpec((1, 1, s * t), lambda i, j: (i, 0, 0)), rows, rows, rows],
        out_specs=[rows, pl.BlockSpec((1, ATTEND_PAIRS, 8, s * t), lambda i, j: (i, j, 0, 0))],
        compiler_params=pltpu.CompilerParams(vmem_limit_bytes=32 * MIB),
        cost_estimate=pl.CostEstimate(
            flops=4 * n * (s * t) ** 2 * width, bytes_accessed=16 * s * n * t * width, transcendentals=0
        ),
        name="attend",
    )(bias, q, k, v)


def attend_back_pair(temper, key_bias, q, k, v, ctx, logs, grad):
    both = jnp.transpose(grad.astype(F32) * ctx.astype(F32))
    gq = jnp.zeros(q.shape, F32)
    gk = jnp.zeros(q.shape, F32)
    gv = jnp.zeros(q.shape, F32)
    for head in range(2):
        mask = head_mask(head)
        k_head = k * (mask * temper).astype(BF)
        grad_head = grad * mask.astype(BF)
        log_total = logs[head : head + 1]
        inner = jnp.sum(both[head * HD : (head + 1) * HD], axis=0, keepdims=True)
        attention = jnp.exp(dot_nt(k_head, q) + key_bias - log_total)
        gv = gv + dot_nn(attention.astype(BF), grad_head)
        grad_attention = dot_nt(v, grad_head)
        grad_scores = (attention * (grad_attention - inner)).astype(BF)
        gk = gk + dot_nn(grad_scores, q * (mask * temper).astype(BF))
        gq = gq + dot_tn(grad_scores, k_head)
    return gq.astype(BF), gk.astype(BF), gv.astype(BF)


class Sums:
    def __init__(self, a, b, chunks, landed, staged, send, recv, local):
        self.place = Place(a, b)
        self.own = self.place.own()
        self.steps = a + b
        self.chunks, self.landed, self.staged = chunks, landed, staged
        self.send, self.recv, self.local = send, recv, local
        self.orders = [gather_steps(a, b, c[3])[::-1] for c in chunks]

    def index(self, m, s, flip):
        out = [slice(None)] * self.steps
        for step in self.orders[m][: s + 1]:
            out[self.place.dim(step)] = self.own[self.place.dim(step)]
        if flip:
            d = self.place.dim(self.orders[m][s])
            out[d] = 1 - self.own[d]
        return out

    def later(self, m, index):
        out = list(index)
        del out[self.place.dim(self.orders[m][0])]
        return tuple(out)

    def copy(self, m, s):
        src, _, piece, _ = self.chunks[m]
        index = self.index(m, s, True)
        here = src.at[tuple(index) + piece] if s == 0 else self.landed[m][0].at[self.later(m, index)]
        return pltpu.make_async_remote_copy(
            src_ref=here,
            dst_ref=self.landed[m][s],
            send_sem=self.send.at[m, s],
            recv_sem=self.recv.at[m, s],
            device_id=self.place.partner(self.orders[m][s]),
            device_id_type=MESH,
        )

    def keep(self, m):
        src, _, piece, _ = self.chunks[m]
        index = self.index(m, 0, False)
        return pltpu.make_async_copy(src.at[tuple(index) + piece], self.staged[m], self.local.at[m])

    def add(self, m, s):
        total, index = self.landed[m][0], self.later(m, self.index(m, s, False))
        other = self.landed[m][s]
        if s == 0:
            src, _, piece, _ = self.chunks[m]
            other = self.staged[m]
            if other is None:
                other = src.at[tuple(self.index(m, 0, False)) + piece]
        if s == self.steps - 1:
            out, piece = self.chunks[m][1], self.chunks[m][2]
            value = total[index].astype(F32) + other[...].astype(F32)
            out[piece] = value
            return
        free = [d for d, v in enumerate(index) if isinstance(v, slice)]

        def one(i, carry):
            at = list(index)
            at[free[0]] = i
            total[tuple(at)] = total[tuple(at)] + other[i]
            return carry

        lax.fori_loop(0, 2, one, 0)

    def event(self, unit, s, load):
        for m in unit:
            if s > 0:
                self.copy(m, s - 1).wait_recv()
                if s == 1 and self.staged[m] is not None:
                    self.keep(m).wait()
                self.add(m, s - 1)
            if s < self.steps:
                self.copy(m, s).start()
            else:
                for k in range(self.steps):
                    self.copy(m, k).wait_send()
        for m in load:
            if self.staged[m] is not None:
                self.keep(m).start()


def plan_steps(n, hidden, parts, blocks):
    out = [("hidden", 0, j) for j in range(hidden)]
    out += [("norm", 0, k) for k in range(parts)]
    out += [("project", 0, r) for r in range(blocks)]
    for s in range(n):
        out += [("attend" if s < n - 1 else "last", s, c) for c in range(blocks)]
        out += [("tokens", s, r) for r in range(blocks)]
    return out


def span(plan, kind, s=None):
    at = [i for i, step in enumerate(plan) if step[0] == kind and s in (None, step[1])]
    return at[0], at[-1] + 1


STEP_US = {"hidden": 6.6, "norm": 1.2, "project": 2.2, "attend": 3.4, "last": 4.8, "tokens": 1.9}
LINK_US = 23.0
CORE_US = 3.0
HOP_US = 2.5
SLACK_US = 0.0
LATE_US = -0.5


def plan_events(plan, units, ready, late, a, b):
    steps = a + b
    ends, now = [], 0.0
    for kind, _, _ in plan:
        now += STEP_US[kind]
        ends.append(now)
    free, events = {}, []
    due = [[ends[r], u, 0] for u, r in enumerate(ready)]
    while due:
        due.sort()
        time, u, k = due.pop(0)
        slack = SLACK_US if u < late else LATE_US
        at = min([i for i, end in enumerate(ends) if end >= time + slack] + [len(plan) - 1])
        start = max(time, ends[at])
        events.append((at, start, u, k))
        if k == steps:
            continue
        came_all = start
        for size, color in units[u]:
            where = gather_steps(a, b, color)[::-1][k]
            cost = CORE_US if where == ("fsdp", 0) else LINK_US
            free[where] = max(free.get(where, 0.0), start) + size / (1 << (k + 1)) * cost
            came_all = max(came_all, free[where])
        due.append([came_all + HOP_US, u, k + 1])
    waiting, order, place = sorted(events), [], {}
    while waiting:
        for i, (at, _, u, k) in enumerate(waiting):
            before = [(u, k - 1)] if k else []
            if k == 1 and u:
                before.append((u - 1, 1))
            if late - 1 <= u < len(units) - 1:
                before.append((u + 1 - late, steps))
            if not all(b in place for b in before):
                continue
            if u < late or k == steps:
                break
            freed = place.get((u - late, steps), len(events))
            if any(place.get((w, k), -1) > freed and (w, k + 1) in place for w in range(u)):
                break
        at, _, u, k = waiting.pop(i)
        place[u, k] = len(order)
        order.append((max(at, order[-1][0]) if order else at, u, k))
    loads = [-1] * len(order)
    for u in range(len(units)):
        loads[place[u, 0] if u == 0 else max(place[u, 0], place[u - 1, 1])] = u
    return [event + (load,) for event, load in zip(order, loads)]


def staging_plan(sizes, types, units, loaded):
    keys, slot = [], [None] * len(sizes)
    for ids in units:
        used = {}
        for m in ids:
            if not loaded[m]:
                slot[m] = (-1, 0, 0)
                continue
            (r, c), kind = sizes[m], types[m]
            for k, (rows, columns, had) in enumerate(keys):
                if rows == r and had == kind and used.get(k, 0) + c <= columns:
                    break
            else:
                k = len(keys)
                keys.append((r, c, kind))
            slot[m] = (k, used.get(k, 0), c)
            used[k] = used.get(k, 0) + c
    return slot, keys


def sum_units(shapes, blocks):
    units = []
    r, c = shapes[4]
    parts = pieces(r, c, 1, 8)
    units += [[(4,) + parts[k] + (0,), (4,) + parts[k + 1] + (1,)] for k in range(0, 8, 2)]
    r, c = shapes[5]
    tall = min(4, r // 16)
    parts = pieces(r, c, tall, 8 // tall)
    units += [[(5,) + parts[k] + (0,), (5,) + parts[k + 1] + (1,)] for k in range(0, 8, 2)]
    r, c = shapes[3]
    left, right = pieces(r, c, 1, 2)
    units.append([(3,) + left + (0,), (3,) + right + (1,)])
    r, c = shapes[0]
    for k in range(blocks):
        whole = pieces(r, c, 1, blocks)[k]
        left, right = pieces(r, c, 1, 2 * blocks)[2 * k : 2 * k + 2]
        units.append([(0,) + whole + (0,), (1,) + whole + (1,), (2,) + left + (0,), (2,) + right + (1,)])
    return units


def bits_index(value, count):
    return tuple(lax.rem(value // (1 << (count - 1 - k)), 2) for k in range(count))


def back_kernel(a, b, plan, unit_list, events, slot, lands, temper, *refs):
    bias_ref, q_ref, k_ref, v_ref, ctx_ref, lse_ref = refs[:6]
    active_ref, slope_ref, w2_ref, w1_ref = refs[6:10]
    xhat_ref, scale_ref, gain_ref, wide_ctx_ref, wo_ref = refs[10:15]
    x_ref, wq_ref, wk_ref, wv_ref = refs[15:19]
    vec_ref, grad_outer, normed_low, grad_second = refs[19:23]
    out_tokens, out_bias = refs[23:25]
    outs = refs[25:31]
    g_wo, g_w1, g_w2 = refs[31:34]
    rest = refs[34:]
    gq_s, gk_s, gv_s, sum_q, sum_k, sum_v, bias_s, tok_s, flow, lines, w2_st = rest[:11]
    send, recv, local, tok_send, tok_recv, tok_local, put = rest[11:18]
    rest = rest[18:]
    steps = a + b
    sources = {0: sum_q, 1: sum_k, 2: sum_v, 3: g_wo, 4: g_w1, 5: g_w2}
    chunks, units = [], []
    for unit in unit_list:
        ids = []
        for at, r, c, color in unit:
            ids.append(len(chunks))
            chunks.append((sources[at], outs[at], (r, c), color))
        units.append(ids)
    units[-1] = units[-1] + [len(chunks)]
    chunks.append((bias_s, out_bias, (slice(None), slice(None)), 0))
    landed = []
    for at, start, size in lands:
        refs_of = rest[at * steps : (at + 1) * steps]
        if size != refs_of[0].shape[-1]:
            refs_of = [
                r.at[(slice(None),) * (len(r.shape) - 1) + (pl.ds(start, size),)] for r in refs_of
            ]
        landed.append(refs_of)
    staged = rest[(1 + max(at for at, _, _ in lands)) * steps :]
    views = []
    for m, (k, start, size) in enumerate(slot):
        if k < 0:
            views.append(None)
            continue
        ref = staged[k]
        if size != ref.shape[-1]:
            ref = ref.at[(slice(None),) * steps + (pl.ds(start, size),)]
        views.append(ref)
    sums = Sums(a, b, chunks, landed, views, send, recv, local)
    place = sums.place
    i = pl.program_id(0)
    n, length, width = gq_s.shape
    sp = 1 << b
    part = length // sp
    rows = n * length
    hidden = span(plan, "hidden")[1]
    wide = wq_ref.shape[0]
    h = w1_ref.shape[1]

    loads = [
        pltpu.make_async_copy(grad_outer, gq_s, put.at[0]),
        pltpu.make_async_copy(normed_low, gk_s, put.at[1]),
        pltpu.make_async_copy(grad_second, flow, put.at[2]),
    ]

    @pl.when(i == 0)
    def _():
        for load in loads:
            load.start()
        place.greet()
        for load in loads:
            load.wait()
        lines[...] = jnp.zeros_like(lines)

    def token_moves(s):
        out = [pltpu.make_async_copy(tok_s.at[s, place.z], out_tokens.at[place.z, s], tok_local.at[s])]
        for k in range(1, sp):
            to = lax.rem(place.z + k, sp)
            out.append(
                pltpu.make_async_remote_copy(
                    src_ref=tok_s.at[s, to],
                    dst_ref=out_tokens.at[place.z, s],
                    send_sem=tok_send.at[s, k - 1],
                    recv_sem=tok_recv.at[s, k - 1],
                    device_id=(place.f, to),
                    device_id_type=MESH,
                )
            )
        return out

    def puts(j):
        at = lax.rem(j, 2)
        columns = pl.ds(pl.multiple_of(j * h, h), h)
        held = pl.ds(pl.multiple_of(at * h, h), h)
        to_w1 = g_w1.at[(slice(None),) * (steps + 1) + (columns,)]
        to_w2 = g_w2.at[bits_index(j, bits_of(hidden))]
        return [
            pltpu.make_async_copy(sum_q.at[(slice(None),) * (steps + 1) + (held,)], to_w1, put.at[3 + at]),
            pltpu.make_async_copy(w2_st.at[at], to_w2, put.at[5 + at]),
        ]

    @pl.when(i < hidden)
    def _():
        at = lax.rem(i, 2)
        grad_out = gq_s[...].reshape(rows, width)
        normed = gk_s[...].reshape(rows, width)
        grad_active = dot_nt(grad_out, w2_ref[...])
        grad_inner = (grad_active * slope_ref[...].astype(F32)).astype(BF)
        columns = pl.ds(pl.multiple_of(i * h, h), h)
        lines[0:1, columns] = jnp.sum(grad_inner.astype(F32), axis=0, keepdims=True)
        value = dot_tn(normed, grad_inner).astype(BF)
        sum_q[..., pl.ds(pl.multiple_of(at * h, h), h)] = value.reshape(sum_q.shape[:-1] + (h,))
        value = dot_tn(active_ref[...], grad_out).astype(BF)
        w2_st[at] = value.reshape(w2_st.shape[1:])
        for p in puts(i):
            p.start()
        flow[...] += dot_nt(grad_inner, w1_ref[...]).reshape(flow.shape)

        @pl.when(i > 0)
        def _():
            for p in puts(i - 1):
                p.wait()

    lo, hi = span(plan, "norm")

    @pl.when(i == lo)
    def _():
        for p in puts(hidden - 1):
            p.wait()

    @pl.when(jnp.logical_and(i >= lo, i < hi))
    def _():
        zb = i - lo
        for s in range(n):
            grad = flow[zb, s]
            xhat = xhat_ref[0, s].astype(F32)
            scaled = grad * gain_ref[...]
            mean = jnp.mean(scaled, axis=-1, keepdims=True)
            slope = jnp.mean(scaled * xhat, axis=-1, keepdims=True)
            first = scale_ref[0, s] * (scaled - mean - xhat * slope)
            flow[zb, s] = first
            low = first.astype(BF)
            tok_s[s, zb] = low
            for at, value in ((1, grad * xhat), (2, grad), (3, low.astype(F32))):
                lines[at : at + 1, :width] += jnp.sum(value, axis=0, keepdims=True)

    lo, hi = span(plan, "project")
    first_attend = hi
    put_wo = pltpu.make_async_copy(sum_v, g_wo, put.at[7])

    @pl.when(jnp.logical_and(i >= lo, i < hi))
    def _():
        r = i - lo
        columns = pl.ds(pl.multiple_of(r * wide, wide), wide)
        total = jnp.zeros((wide, width), F32)
        for s in range(n):
            grad = tok_s[s].reshape(length, width)
            gv_s[s, :, columns] = dot_nt(grad, wo_ref[...]).astype(BF)
            total = total + dot_tn(wide_ctx_ref[:, s].reshape(length, wide), grad)
        index = bits_index(r, bits_of(hi - lo))
        sum_v[index] = total.astype(BF).reshape(sum_v.shape[len(index) :])

        @pl.when(i == hi - 1)
        def _():
            put_wo.start()

    @pl.when(i == first_attend)
    def _():
        put_wo.wait()

    def attend_step(s, c):
        bias_rows = jnp.broadcast_to(bias_ref[...].reshape(1, length), (2 * HD, length))
        key_bias = jnp.transpose(bias_rows)[:, :1]
        for pair in range(wide // (2 * HD)):
            cut = slice(pair * 2 * HD, (pair + 1) * 2 * HD)
            columns = pl.ds(pl.multiple_of(c * wide + pair * 2 * HD, 2 * HD), 2 * HD)
            q, k, v, ctx = (r[:, 0, :, cut].reshape(length, 2 * HD) for r in (q_ref, k_ref, v_ref, ctx_ref))
            logs = lse_ref[0, pair, 0:2]
            gq, gk, gv = attend_back_pair(temper, key_bias, q, k, v, ctx, logs, gv_s[s, :, columns])
            gq_s[s, :, columns] = gq
            gk_s[s, :, columns] = gk
            gv_s[s, :, columns] = gv

    def weights_step(c):
        columns = pl.ds(pl.multiple_of(c * wide, wide), wide)
        for at, held, total in ((4, gq_s, sum_q), (None, gk_s, sum_k), (5, gv_s, sum_v)):
            value = sum(dot_tn(x_ref[:, s].reshape(length, width), held[s, :, columns]) for s in range(n))
            total[..., columns] = value.astype(BF).reshape(total.shape[:-1] + (wide,))
            if at is not None:
                row = sum(jnp.sum(held[s, :, columns].astype(F32), axis=0, keepdims=True) for s in range(n))
                lines[at : at + 1, columns] = row

    for s in range(n):
        lo, hi = span(plan, "attend" if s < n - 1 else "last", s)

        @pl.when(jnp.logical_and(i >= lo, i < hi))
        def _(s=s, lo=lo):
            attend_step(s, i - lo)
            if s == n - 1:
                weights_step(i - lo)

        lo, hi = span(plan, "tokens", s)

        @pl.when(jnp.logical_and(i >= lo, i < hi))
        def _(s=s, lo=lo, hi=hi):
            columns = pl.ds(pl.multiple_of((i - lo) * wide, wide), wide)
            total = dot_nt(gq_s[s], wq_ref[...]) + dot_nt(gk_s[s], wk_ref[...]) + dot_nt(gv_s[s], wv_ref[...])
            total = total + flow[:, s, :, columns].reshape(length, wide)
            tok_s[s, :, :, columns] = total.astype(BF).reshape(sp, part, wide)

            @pl.when(i == hi - 1)
            def _():
                for move in token_moves(s):
                    move.start()

    @pl.when(i == span(plan, "last")[1] - 1)
    def _():
        devices = 1 << steps
        for d in range(devices):
            index = tuple((d >> (steps - 1 - k)) & 1 for k in range(steps))
            for at in range(6):
                size = (hidden * h if at == 0 else width) // devices
                tile = d * size // 128
                bias_s[index + (slice(at, at + 1),)] = lines[at : at + 1, tile * 128 : tile * 128 + 128]
            bias_s[index + (slice(6, 7),)] = vec_ref[d : d + 1]

    for k in sorted({event[0] for event in events}):

        @pl.when(i == k)
        def _(k=k):
            for at, unit, s, load in events:
                if at == k:
                    sums.event(units[unit], s, units[load] if load >= 0 else ())

    @pl.when(i == len(plan) - 1)
    def _():
        for s in range(n):
            for move in token_moves(s):
                move.wait()


def back(a, b, bias, heads, lse, active, slope, W2, W1, xhat, scale, gain, WO, x, WQ, WK, WV, grads, vec):
    q, k, v, ctx = heads
    lead, steps = (2,) * (a + b), a + b
    s, n, t, width = q.shape
    devices = 1 << steps
    hidden, blocks = 8, 4
    h, wide, length, rows = W1.shape[1] // hidden, width // blocks, s * t, s * n * t
    plan = plan_steps(n, hidden, s, blocks)
    own_rows = width // devices
    shapes = [(own_rows, width)] * 4 + [(own_rows, W1.shape[1]), (W2.shape[0] // devices, width)]
    unit_list = sum_units(shapes, blocks)
    first, late = span(plan, "attend" if n > 1 else "last")[0], len(unit_list) - blocks
    ready = [2 * k + 2 for k in range(4)] + [hidden] * 4 + [first]
    ready += list(range(*span(plan, "last")))
    megabytes = [[(r.size * c.size * devices * 2 / MIB, color) for _, r, c, color in u] for u in unit_list]
    events = plan_events(plan, megabytes, ready, late, a, b)
    sizes = [(r.size, c.size) for unit in unit_list for _, r, c, _ in unit] + [(8, 128)]
    types = [BF] * (len(sizes) - 1) + [F32]
    loaded = [at > 2 for unit in unit_list for at, _, _, _ in unit] + [False]
    turn, last = 2 * blocks, n - 1

    def count_from(i, starts):
        return sum([(i >= start).astype(jnp.int32) for start in starts], jnp.int32(0))

    def at_kind(i, begin):
        off = i - begin
        seq = count_from(off, [k * turn for k in range(1, n)])
        return seq, jnp.clip(off - seq * turn, 0, blocks - 1)

    def at_head(i):
        return at_kind(i, first)

    def at_tokens(i):
        return at_kind(i, first + blocks)

    def head_map(i):
        seq, pair = at_head(i)
        return (0, seq, 0, pair)

    def lse_map(i):
        seq, pair = at_head(i)
        return (seq, pair, 0, 0)

    def block_of(kind):
        lo, hi = span(plan, kind)
        return lambda i: jnp.clip(i - lo, 0, hi - lo - 1)

    j_of, z_of, r_of = block_of("hidden"), block_of("norm"), block_of("project")
    head = pl.BlockSpec((s, 1, t, wide), head_map)
    weight = pl.BlockSpec((wide, width), lambda i: (at_tokens(i)[1], 0))
    anyspace = pl.BlockSpec(memory_space=pl.ANY)
    vmem = pl.BlockSpec(memory_space=pltpu.VMEM)
    in_specs = [pl.BlockSpec((1, 1, length), lambda i: (at_head(i)[0], 0, 0))] + [head] * 4
    in_specs += [pl.BlockSpec((1, wide // (2 * HD), 8, length), lse_map)]
    in_specs += [pl.BlockSpec((rows, h), lambda i: (0, j_of(i)))] * 2
    in_specs += [pl.BlockSpec((h, width), lambda i: (j_of(i), 0)), pl.BlockSpec((width, h), lambda i: (0, j_of(i)))]
    in_specs += [pl.BlockSpec((1, n, t, width), lambda i: (z_of(i), 0, 0, 0))]
    in_specs += [pl.BlockSpec((1, n, t, 1), lambda i: (z_of(i), 0, 0, 0))]
    in_specs += [pl.BlockSpec((1, width), lambda i: (0, 0))]
    in_specs += [pl.BlockSpec((s, n, t, wide), lambda i: (0, 0, 0, r_of(i)))]
    in_specs += [pl.BlockSpec((wide, width), lambda i: (r_of(i), 0))]
    in_specs += [pl.BlockSpec(x.shape, lambda i: (0, 0, 0, 0), pipeline_mode=pl.Buffered(1))]
    in_specs += [weight] * 3 + [pl.BlockSpec(vec.shape, lambda i: (0, 0))] + [anyspace] * 3
    outs = [jax.ShapeDtypeStruct((s, n, t, width), BF)]
    outs += [jax.ShapeDtypeStruct(sizes[-1], F32)]
    outs += [jax.ShapeDtypeStruct(shape, F32) for shape in shapes]
    outs += [jax.ShapeDtypeStruct(lead + shapes[m], BF) for m in (3, 4, 5)]
    n_chunks = len(sizes)
    scratch = [pltpu.VMEM((n, length, width), BF)] * 3
    scratch += [pltpu.VMEM(lead + (own_rows, width), BF)] * 3
    scratch += [pltpu.VMEM(lead + sizes[-1], F32), pltpu.VMEM((n, s, t, width), BF)]
    scratch += [pltpu.VMEM((s, n, t, width), F32), pltpu.VMEM((8, W1.shape[1]), F32)]
    scratch += [pltpu.VMEM((2,) + (2,) * (steps - bits_of(hidden)) + shapes[5], BF)]
    scratch += [
        pltpu.SemaphoreType.DMA((n_chunks, steps)),
        pltpu.SemaphoreType.DMA((n_chunks, steps)),
        pltpu.SemaphoreType.DMA((n_chunks,)),
        pltpu.SemaphoreType.DMA((n, s - 1)),
        pltpu.SemaphoreType.DMA((n, s - 1)),
        pltpu.SemaphoreType.DMA((n,)),
        pltpu.SemaphoreType.DMA((8,)),
    ]
    ids, at = [], 0
    for unit in unit_list:
        ids.append(list(range(at, at + len(unit))))
        at += len(unit)
    ids[-1] = ids[-1] + [at]
    slot, keys = staging_plan(sizes, types, ids, loaded)
    lands, held = [None] * len(sizes), []
    for u, unit in enumerate(ids):
        used = {}
        for m in unit:
            if u >= late and m < len(sizes) - 1:
                color = [chunk for each in unit_list for chunk in each][m][3]
                lands[m] = (lands[ids[u - late][color]][0], used.get(color, 0), sizes[m][1])
                used[color] = used.get(color, 0) + sizes[m][1]
            else:
                lands[m] = (len(held), 0, sizes[m][1])
                held.append((sizes[m], types[m]))
    for size, kind in held:
        scratch += [pltpu.VMEM((2,) * (steps - 1 - j) + size, kind) for j in range(steps)]
    scratch += [pltpu.VMEM((2,) * (steps - 1) + (r, c), kind) for r, c, kind in keys]
    grad_outer, normed_low, grad_second = grads
    return pl.pallas_call(
        functools.partial(back_kernel, a, b, plan, unit_list, events, slot, lands, 1.0 / math.sqrt(HD)),
        grid=(len(plan),),
        out_shape=outs,
        in_specs=in_specs,
        out_specs=[anyspace] + [vmem] * 7 + [anyspace] * 3,
        scratch_shapes=scratch,
        compiler_params=pltpu.CompilerParams(
            collective_id=1, has_side_effects=True, vmem_limit_bytes=63 * MIB + MIB * 5 // 8
        ),
        name="back_and_sum",
    )(
        bias,
        q,
        k,
        v,
        ctx,
        lse,
        active,
        slope,
        W2,
        W1,
        xhat,
        scale,
        gain,
        ctx,
        WO,
        x,
        WQ,
        WK,
        WV,
        vec,
        grad_outer,
        normed_low,
        grad_second,
    )


def norm_forward(hidden, gain, shift):
    average = jnp.mean(hidden, axis=-1, keepdims=True)
    centred = hidden - average
    scale = lax.rsqrt(jnp.mean(centred * centred, axis=-1, keepdims=True) + 1e-12)
    xhat = centred * scale
    return xhat * gain + shift, xhat, scale


def norm_backward(grad, gain, xhat, scale):
    scaled = grad * gain
    lead = jnp.mean(scaled, axis=-1, keepdims=True)
    slope = jnp.mean(scaled * xhat, axis=-1, keepdims=True)
    return scale * (scaled - lead - xhat * slope)


def gelu_pair(x):
    cdf = 0.5 * (1.0 + lax.erf(x * (1.0 / math.sqrt(2.0))))
    pdf = jnp.exp(-0.5 * x * x) * (1.0 / math.sqrt(2.0 * math.pi))
    return x * cdf, cdf + x * pdf


def body(tokens, validity, teacher, wq, bq, wk, wv, bv, wo, bo, gain1, shift1, w1, b1, w2, b2, gain2, shift2):
    fs, sp = lax.axis_size("fsdp"), lax.axis_size("sp")
    a, b = bits_of(fs), bits_of(sp)
    devices = fs * sp
    seqs, part, width = tokens.shape
    n = seqs // sp
    length = part * sp
    rows = sp * n * part
    total_tokens = rows * devices
    z = lax.axis_index("sp")
    shard_shape = (sp, n, part, width)

    mine = lax.dynamic_slice_in_dim(validity, z * n, n, 0)
    count = jnp.sum(mine)
    vectors = (bq, bv, bo, gain1, shift1, b2, gain2, shift2, b1)
    sizes = [v.shape[0] for v in vectors]
    lines = [jnp.pad(v.reshape(1, -1), ((0, 0), (0, 128 - v.shape[0]))) for v in vectors]
    lane = lax.broadcasted_iota(jnp.int32, (1, 128), 1)
    lines.append(jnp.where(lane == 0, count // 32, count % 32).astype(BF))
    row = lax.broadcasted_iota(jnp.int32, (16, 128), 0)
    vec = jnp.zeros((16, 128), BF)
    for at, line in enumerate(lines):
        vec = jnp.where(row == at, line, vec)

    shards = (wq, wk, wv, wo, w1, w2)
    got = front(a, b, tokens.reshape(shard_shape), vec, shards)
    moved, vec_all = got[0], got[1].reshape(devices, 16, 128)
    WQ, WK, WV, WO, W1, W2 = (
        g.reshape((devices * w.shape[0],) + w.shape[1:]) for g, w in zip(got[2:], shards)
    )
    full = [vec_all[:, at, :size].reshape(-1).astype(F32) for at, size in enumerate(sizes)]
    BQ, BV, BO, G1, S1, B2, G2, S2, B1 = full
    counts = vec_all[:, len(sizes), :2].astype(F32)
    counted = jnp.sum(counts[:, 0]) * 32.0 + jnp.sum(counts[:, 1])

    teacher_moved = lax.all_to_all(
        lax.optimization_barrier((teacher, moved))[0].reshape(shard_shape), "sp", split_axis=0, concat_axis=0
    ).reshape(rows, width)

    valid = mine.astype(F32)
    bias = ((valid - 1.0) * 1e9).reshape(n, 1, length)
    mask_rows = jnp.swapaxes(valid.reshape(n, sp, part), 0, 1).reshape(rows, 1)

    x = moved.reshape(rows, width)
    q = (dot_nn(x, WQ) + BQ).astype(BF)
    k = dot_nn(x, WK).astype(BF)
    v = (dot_nn(x, WV) + BV).astype(BF)
    ctx, lse = attend(bias, *(p.reshape(shard_shape) for p in (q, k, v)))
    ctx_rows = ctx.reshape(rows, width)
    first = x.astype(F32) + dot_nn(ctx_rows, WO) + BO
    normed, xhat1, scale1 = norm_forward(first, G1, S1)
    normed_low = normed.astype(BF)
    inner = dot_nn(normed_low, W1) + B1
    active, slope = gelu_pair(inner)
    active_low = active.astype(BF)
    slope = slope.astype(BF)
    second = normed + dot_nn(active_low, W2) + B2
    final, xhat2, scale2 = norm_forward(second, G2, S2)
    error = final - teacher_moved.astype(F32)
    local_loss = jnp.sum(mask_rows * error * error)
    output = lax.all_to_all(final.astype(BF).reshape(shard_shape), "sp", split_axis=0, concat_axis=0)

    grad_final = (2.0 * total_tokens / counted) * mask_rows * error
    grad_second = norm_backward(grad_final, G2, xhat2, scale2)
    grad_outer = grad_second.astype(BF)

    def column_sum(value):
        return jnp.sum(value.astype(F32), axis=0)

    vector_grads = (column_sum(grad_outer), jnp.sum(grad_final * xhat2, axis=0), column_sum(grad_final))
    parts = [g.reshape(devices, -1) for g in vector_grads]
    parts.append(jnp.broadcast_to(local_loss, (devices, 1)))
    packed = jnp.concatenate(parts, axis=1)
    packed = jnp.pad(packed, ((0, 0), (0, 128 - packed.shape[1])))
    by_rows = (n, length, width)
    summed = back(
        a,
        b,
        bias,
        [p.reshape(shard_shape) for p in (q, k, v)] + [ctx],
        lse,
        active_low,
        slope,
        W2,
        W1,
        xhat1.astype(BF).reshape(shard_shape),
        scale1.reshape(sp, n, part, 1),
        G1.reshape(1, width),
        WO,
        moved,
        WQ,
        WK,
        WV,
        [grad_outer.reshape(by_rows), normed_low.reshape(by_rows), grad_second.reshape(shard_shape)],
        packed,
    )
    home = summed[0].reshape(seqs, part, width).astype(F32)
    own = summed[1][6]
    small, at = [], 0
    for g in vector_grads:
        size = g.shape[0] // devices
        small.append(own[at : at + size])
        at += size
    loss = own[at] / (width * counted)
    d_b2, d_g2, d_s2 = small
    me = lax.axis_index("fsdp") * sp + z
    tiles = []
    for at, size in enumerate((sizes[8],) + (width // devices,) * 5):
        tiles.append(lax.dynamic_slice_in_dim(summed[1][at], lax.rem(me * size, 128), size, 0))
    d_b1, d_g1, d_s1, d_bo, d_bq, d_bv = tiles
    d_wq, d_wk, d_wv, d_wo, d_w1, d_w2 = summed[2:8]
    return (
        output.reshape(seqs, part, width),
        loss,
        home,
        d_wq,
        d_bq,
        d_wk,
        d_wv,
        d_bv,
        d_wo,
        d_bo,
        d_g1,
        d_s1,
        d_w1,
        d_b1,
        d_w2,
        d_b2,
        d_g2,
        d_s2,
    )


def solution(mesh):
    tokens = P("fsdp", "sp", None)
    matrix = P(AXES, None)
    vector = P(AXES)
    return jax.shard_map(
        body,
        mesh=mesh,
        in_specs=(
            tokens,
            P("fsdp", None),
            tokens,
            matrix,
            vector,
            matrix,
            matrix,
            vector,
            matrix,
            vector,
            vector,
            vector,
            matrix,
            vector,
            matrix,
            vector,
            vector,
            vector,
        ),
        out_specs=(
            tokens,
            P(),
            tokens,
            matrix,
            vector,
            matrix,
            matrix,
            vector,
            matrix,
            vector,
            vector,
            vector,
            matrix,
            vector,
            matrix,
            vector,
            vector,
            vector,
        ),
        check_vma=False,
    )
```

```python
import functools
import math

import jax
import jax.numpy as jnp
from jax import lax
from jax.experimental import pallas as pl
from jax.experimental.pallas import tpu as pltpu
from jax.sharding import PartitionSpec as P

HD = 64
BF = jnp.bfloat16
F32 = jnp.float32
MESH = pl.DeviceIdType.MESH
AXES = ("fsdp", "sp")
MIB = 1 << 20
ATTEND_PAIRS = 8
GATHER_PAIRS = ((0, 1, 1), (2, 3, 1), (4, 5, 4))


def bits_of(n):
    return n.bit_length() - 1


def gather_steps(a, b, color):
    z = [("sp", k) for k in reversed(range(b))]
    f = [("fsdp", k) for k in reversed(range(a))]
    if color and a >= 2:
        f[0], f[1] = f[1], f[0]
    return z + f


class Place:
    def __init__(self, a, b):
        self.a, self.b = a, b
        self.f = lax.axis_index("fsdp")
        self.z = lax.axis_index("sp")

    def dim(self, step):
        axis, k = step
        return self.a - 1 - k if axis == "fsdp" else self.a + self.b - 1 - k

    def bit(self, step):
        axis, k = step
        me = self.f if axis == "fsdp" else self.z
        return lax.rem(me // (1 << k), 2)

    def own(self):
        out = [None] * (self.a + self.b)
        for step in gather_steps(self.a, self.b, 0):
            out[self.dim(step)] = self.bit(step)
        return out

    def partner(self, step):
        axis, k = step
        change = (1 - 2 * self.bit(step)) * (1 << k)
        if axis == "fsdp":
            return (self.f + change, self.z)
        return (self.f, self.z + change)

    def greet(self):
        barrier = pltpu.get_barrier_semaphore()
        s = 1 << self.b
        others = [(self.f, lax.rem(self.z + k, s)) for k in range(1, s)]
        others += [self.partner(("fsdp", k)) for k in range(self.a)]
        for other in others:
            pl.semaphore_signal(barrier, inc=1, device_id=other, device_id_type=MESH)
        pl.semaphore_wait(barrier, len(others))


def exchange_tokens(place, src, dst, send, recv, local):
    s = 1 << place.b
    copies = [pltpu.make_async_copy(src.at[place.z], dst.at[place.z], local)]
    for k in range(1, s):
        to = lax.rem(place.z + k, s)
        copies.append(
            pltpu.make_async_remote_copy(
                src_ref=src.at[to],
                dst_ref=dst.at[place.z],
                send_sem=send.at[k - 1],
                recv_sem=recv.at[k - 1],
                device_id=(place.f, to),
                device_id_type=MESH,
            )
        )
    return copies


def pieces(rows, columns, parts_r, parts_c):
    out = []
    for i in range(parts_r):
        for j in range(parts_c):
            out.append(
                (
                    pl.ds(i * (rows // parts_r), rows // parts_r),
                    pl.ds(j * (columns // parts_c), columns // parts_c),
                )
            )
    return out


def make_units(shapes, pairs):
    units = []
    for x, y, n in pairs:
        (rx, cx), (ry, cy) = shapes[x], shapes[y]
        if x == y:
            left, right = pieces(rx, cx, 1, 2)
            units.append([(x,) + left + (0,), (y,) + right + (1,)])
            continue
        ny = max(1, min(n, ry // 16)) if ry > rx else 1
        xs = pieces(rx, cx, 1, n)
        ys = pieces(ry, cy, ny, 1)
        for k in range(n):
            unit = [(x,) + xs[k] + (0,)]
            if k < ny:
                unit.append((y,) + ys[k] + (1,))
            units.append(unit)
    return units


def front_kernel(a, b, units, *refs):
    n_mat = 6
    tokens, vec = refs[0], refs[1]
    shards = refs[2 : 2 + n_mat]
    out_tokens, out_vec = refs[2 + n_mat], refs[3 + n_mat]
    outs = refs[4 + n_mat : 4 + 2 * n_mat]
    send, recv, local, tok_send, tok_recv, tok_local = refs[4 + 2 * n_mat :]
    place = Place(a, b)
    own = place.own()
    chunks = [[(vec, out_vec, (), 0)] + [(shards[at], outs[at], (r, c), color) for at, r, c, color in units[0]]]
    for unit in units[1:]:
        chunks.append([(shards[at], outs[at], (r, c), color) for at, r, c, color in unit])
    flat = [chunk for unit in chunks for chunk in unit]
    number = {}
    for u, unit in enumerate(chunks):
        for i in range(len(unit)):
            number[u, i] = len(number)
    steps = a + b

    def copy_of(m, s):
        src, out, piece, color = flat[m]
        order = gather_steps(a, b, color)
        index = list(own)
        for step in order[:s]:
            index[place.dim(step)] = slice(None)
        there = out.at[tuple(index) + piece]
        here = (src.at[piece] if piece else src) if s == 0 else there
        return pltpu.make_async_remote_copy(
            src_ref=here,
            dst_ref=there,
            send_sem=send.at[m, s],
            recv_sem=recv.at[m, s],
            device_id=place.partner(order[s]),
            device_id_type=MESH,
        )

    def keep_of(m):
        src, out, piece, _ = flat[m]
        return pltpu.make_async_copy(
            src.at[piece] if piece else src, out.at[tuple(own) + piece], local.at[m]
        )

    for m in range(len(flat)):
        keep_of(m).start()
    place.greet()
    moves = exchange_tokens(place, tokens, out_tokens, tok_send, tok_recv, tok_local)
    lead = [b + 1, b] + list(range(b - 1, -1, -1)) + list(range(b + 2, steps + 1))
    events = [(u + k, lead.index(k), u, k) for u in range(len(chunks)) for k in range(steps + 1)]
    events.append((len(chunks) + 0.5, 0, -1, -1))
    for _, _, u, k in sorted(events):
        if u < 0:
            for move in moves:
                move.start()
            continue
        for i in range(len(chunks[u])):
            m = number[u, i]
            if k == 1:
                keep_of(m).wait()
            if k > 0:
                copy_of(m, k - 1).wait_recv()
            if k < steps:
                copy_of(m, k).start()
    for m in range(len(flat)):
        for k in range(steps):
            copy_of(m, k).wait_send()
    for move in moves:
        move.wait()


def front(a, b, tokens, vec, shards):
    lead = (2,) * (a + b)
    units = make_units([w.shape for w in shards], GATHER_PAIRS)
    n_chunks = 1 + sum(len(u) for u in units)
    steps = a + b
    anyspace = pl.BlockSpec(memory_space=pl.ANY)
    outs = [jax.ShapeDtypeStruct(tokens.shape, tokens.dtype), jax.ShapeDtypeStruct(lead + vec.shape, vec.dtype)]
    outs += [jax.ShapeDtypeStruct(lead + w.shape, w.dtype) for w in shards]
    s = 1 << b
    return pl.pallas_call(
        functools.partial(front_kernel, a, b, units),
        out_shape=outs,
        in_specs=[anyspace] * (2 + len(shards)),
        out_specs=[anyspace] * len(outs),
        scratch_shapes=[
            pltpu.SemaphoreType.DMA((n_chunks, steps)),
            pltpu.SemaphoreType.DMA((n_chunks, steps)),
            pltpu.SemaphoreType.DMA((n_chunks,)),
            pltpu.SemaphoreType.DMA((s - 1,)),
            pltpu.SemaphoreType.DMA((s - 1,)),
            pltpu.SemaphoreType.DMA,
        ],
        compiler_params=pltpu.CompilerParams(collective_id=0, has_side_effects=True),
        name="gather_weights",
    )(tokens, vec, *shards)


def head_mask(head):
    lane = lax.broadcasted_iota(jnp.int32, (1, 2 * HD), 1)
    return (lane // HD == head).astype(F32)


def dot_nt(x, y):
    return lax.dot_general(x, y, (((1,), (1,)), ((), ())), preferred_element_type=F32)


def dot_tn(x, y):
    return lax.dot_general(x, y, (((0,), (0,)), ((), ())), preferred_element_type=F32)


def dot_nn(x, y):
    return lax.dot_general(x, y, (((1,), (0,)), ((), ())), preferred_element_type=F32)


def attend_kernel(temper, bias_ref, q_ref, k_ref, v_ref, ctx_ref, lse_ref):
    length = bias_ref.shape[-1]
    shape = q_ref.shape
    bias = bias_ref[...].reshape(1, length)
    for pair in range(shape[-1] // (2 * HD)):
        cut = slice(pair * 2 * HD, (pair + 1) * 2 * HD)
        q, k, v = (ref[:, 0, :, cut].reshape(length, 2 * HD) for ref in (q_ref, k_ref, v_ref))
        total = jnp.zeros((length, 2 * HD), F32)
        logs = jnp.zeros((length, 2 * HD), F32)
        for head in range(2):
            mask = head_mask(head)
            scores = dot_nt(q, k * (mask * temper).astype(BF)) + bias
            largest = jnp.max(scores, axis=-1, keepdims=True)
            raised = jnp.exp(scores - largest)
            summed = jnp.sum(raised, axis=-1, keepdims=True)
            part = dot_nn(raised.astype(BF), v * mask.astype(BF))
            total = total + part * (1.0 / summed)
            logs = logs + (largest + jnp.log(summed)) * mask
        ctx_ref[:, 0, :, cut] = total.astype(BF).reshape(shape[0], shape[2], 2 * HD)
        turned = jnp.transpose(logs)
        for head in range(2):
            lse_ref[0, pair, head : head + 1] = turned[head * HD : head * HD + 1]


def attend(bias, q, k, v):
    s, n, t, width = q.shape
    wide = ATTEND_PAIRS * 2 * HD
    rows = pl.BlockSpec((s, 1, t, wide), lambda i, j: (0, i, 0, j))
    return pl.pallas_call(
        functools.partial(attend_kernel, 1.0 / math.sqrt(HD)),
        grid=(n, width // wide),
        out_shape=[
            jax.ShapeDtypeStruct(q.shape, BF),
            jax.ShapeDtypeStruct((n, width // (2 * HD), 8, s * t), F32),
        ],
        in_specs=[pl.BlockSpec((1, 1, s * t), lambda i, j: (i, 0, 0)), rows, rows, rows],
        out_specs=[rows, pl.BlockSpec((1, ATTEND_PAIRS, 8, s * t), lambda i, j: (i, j, 0, 0))],
        compiler_params=pltpu.CompilerParams(vmem_limit_bytes=32 * MIB),
        cost_estimate=pl.CostEstimate(
            flops=4 * n * (s * t) ** 2 * width, bytes_accessed=16 * s * n * t * width, transcendentals=0
        ),
        name="attend",
    )(bias, q, k, v)


def attend_back_pair(temper, key_bias, q, k, v, ctx, logs, grad):
    both = jnp.transpose(grad.astype(F32) * ctx.astype(F32))
    gq = jnp.zeros(q.shape, F32)
    gk = jnp.zeros(q.shape, F32)
    gv = jnp.zeros(q.shape, F32)
    for head in range(2):
        mask = head_mask(head)
        k_head = k * (mask * temper).astype(BF)
        grad_head = grad * mask.astype(BF)
        log_total = logs[head : head + 1]
        inner = jnp.sum(both[head * HD : (head + 1) * HD], axis=0, keepdims=True)
        attention = jnp.exp(dot_nt(k_head, q) + key_bias - log_total)
        gv = gv + dot_nn(attention.astype(BF), grad_head)
        grad_attention = dot_nt(v, grad_head)
        grad_scores = (attention * (grad_attention - inner)).astype(BF)
        gk = gk + dot_nn(grad_scores, q * (mask * temper).astype(BF))
        gq = gq + dot_tn(grad_scores, k_head)
    return gq.astype(BF), gk.astype(BF), gv.astype(BF)


class Sums:
    def __init__(self, a, b, chunks, landed, staged, send, recv, local):
        self.place = Place(a, b)
        self.own = self.place.own()
        self.steps = a + b
        self.chunks, self.landed, self.staged = chunks, landed, staged
        self.send, self.recv, self.local = send, recv, local
        self.orders = [gather_steps(a, b, c[3])[::-1] for c in chunks]

    def index(self, m, s, flip):
        out = [slice(None)] * self.steps
        for step in self.orders[m][: s + 1]:
            out[self.place.dim(step)] = self.own[self.place.dim(step)]
        if flip:
            d = self.place.dim(self.orders[m][s])
            out[d] = 1 - self.own[d]
        return out

    def later(self, m, index):
        out = list(index)
        del out[self.place.dim(self.orders[m][0])]
        return tuple(out)

    def copy(self, m, s):
        src, _, piece, _ = self.chunks[m]
        index = self.index(m, s, True)
        here = src.at[tuple(index) + piece] if s == 0 else self.landed[m][0].at[self.later(m, index)]
        return pltpu.make_async_remote_copy(
            src_ref=here,
            dst_ref=self.landed[m][s],
            send_sem=self.send.at[m, s],
            recv_sem=self.recv.at[m, s],
            device_id=self.place.partner(self.orders[m][s]),
            device_id_type=MESH,
        )

    def keep(self, m):
        src, _, piece, _ = self.chunks[m]
        index = self.index(m, 0, False)
        return pltpu.make_async_copy(src.at[tuple(index) + piece], self.staged[m], self.local.at[m])

    def add(self, m, s):
        total, index = self.landed[m][0], self.later(m, self.index(m, s, False))
        other = self.landed[m][s]
        if s == 0:
            src, _, piece, _ = self.chunks[m]
            other = self.staged[m]
            if other is None:
                other = src.at[tuple(self.index(m, 0, False)) + piece]
        if s == self.steps - 1:
            out, piece = self.chunks[m][1], self.chunks[m][2]
            value = total[index].astype(F32) + other[...].astype(F32)
            out[piece] = value
            return
        free = [d for d, v in enumerate(index) if isinstance(v, slice)]

        def one(i, carry):
            at = list(index)
            at[free[0]] = i
            total[tuple(at)] = total[tuple(at)] + other[i]
            return carry

        lax.fori_loop(0, 2, one, 0)

    def event(self, unit, s, load):
        for m in unit:
            if s > 0:
                self.copy(m, s - 1).wait_recv()
                if s == 1 and self.staged[m] is not None:
                    self.keep(m).wait()
                self.add(m, s - 1)
            if s < self.steps:
                self.copy(m, s).start()
            else:
                for k in range(self.steps):
                    self.copy(m, k).wait_send()
        for m in load:
            if self.staged[m] is not None:
                self.keep(m).start()


def plan_steps(n, hidden, parts, blocks):
    out = [("hidden", 0, j) for j in range(hidden)]
    out += [("norm", 0, k) for k in range(parts)]
    out += [("project", 0, r) for r in range(blocks)]
    for s in range(n):
        out += [("attend" if s < n - 1 else "last", s, c) for c in range(blocks)]
        out += [("tokens", s, r) for r in range(blocks)]
    return out


def span(plan, kind, s=None):
    at = [i for i, step in enumerate(plan) if step[0] == kind and s in (None, step[1])]
    return at[0], at[-1] + 1


STEP_US = {"hidden": 6.6, "norm": 1.2, "project": 2.2, "attend": 3.4, "last": 4.8, "tokens": 1.9}
LINK_US = 23.0
CORE_US = 3.0
HOP_US = 2.5
SLACK_US = 0.0
LATE_US = -0.5


def plan_events(plan, units, ready, late, a, b):
    steps = a + b
    ends, now = [], 0.0
    for kind, _, _ in plan:
        now += STEP_US[kind]
        ends.append(now)
    free, events = {}, []
    due = [[ends[r], u, 0] for u, r in enumerate(ready)]
    while due:
        due.sort()
        time, u, k = due.pop(0)
        slack = SLACK_US if u < late else LATE_US
        at = min([i for i, end in enumerate(ends) if end >= time + slack] + [len(plan) - 1])
        start = max(time, ends[at])
        events.append((at, start, u, k))
        if k == steps:
            continue
        came_all = start
        for size, color in units[u]:
            where = gather_steps(a, b, color)[::-1][k]
            cost = CORE_US if where == ("fsdp", 0) else LINK_US
            free[where] = max(free.get(where, 0.0), start) + size / (1 << (k + 1)) * cost
            came_all = max(came_all, free[where])
        due.append([came_all + HOP_US, u, k + 1])
    waiting, order, place = sorted(events), [], {}
    while waiting:
        for i, (at, _, u, k) in enumerate(waiting):
            before = [(u, k - 1)] if k else []
            if k == 1 and u:
                before.append((u - 1, 1))
            if late - 1 <= u < len(units) - 1:
                before.append((u + 1 - late, steps))
            if not all(b in place for b in before):
                continue
            if u < late or k == steps:
                break
            freed = place.get((u - late, steps), len(events))
            if any(place.get((w, k), -1) > freed and (w, k + 1) in place for w in range(u)):
                break
        at, _, u, k = waiting.pop(i)
        place[u, k] = len(order)
        order.append((max(at, order[-1][0]) if order else at, u, k))
    loads = [-1] * len(order)
    for u in range(len(units)):
        loads[place[u, 0] if u == 0 else max(place[u, 0], place[u - 1, 1])] = u
    return [event + (load,) for event, load in zip(order, loads)]


def staging_plan(sizes, types, units, loaded):
    keys, slot = [], [None] * len(sizes)
    for ids in units:
        used = {}
        for m in ids:
            if not loaded[m]:
                slot[m] = (-1, 0, 0)
                continue
            (r, c), kind = sizes[m], types[m]
            for k, (rows, columns, had) in enumerate(keys):
                if rows == r and had == kind and used.get(k, 0) + c <= columns:
                    break
            else:
                k = len(keys)
                keys.append((r, c, kind))
            slot[m] = (k, used.get(k, 0), c)
            used[k] = used.get(k, 0) + c
    return slot, keys


def sum_units(shapes, blocks):
    units = []
    r, c = shapes[4]
    parts = pieces(r, c, 1, 8)
    units += [[(4,) + parts[k] + (0,), (4,) + parts[k + 1] + (1,)] for k in range(0, 8, 2)]
    r, c = shapes[5]
    tall = min(4, r // 16)
    parts = pieces(r, c, tall, 8 // tall)
    units += [[(5,) + parts[k] + (0,), (5,) + parts[k + 1] + (1,)] for k in range(0, 8, 2)]
    r, c = shapes[3]
    left, right = pieces(r, c, 1, 2)
    units.append([(3,) + left + (0,), (3,) + right + (1,)])
    r, c = shapes[0]
    for k in range(blocks):
        whole = pieces(r, c, 1, blocks)[k]
        left, right = pieces(r, c, 1, 2 * blocks)[2 * k : 2 * k + 2]
        units.append([(0,) + whole + (0,), (1,) + whole + (1,), (2,) + left + (0,), (2,) + right + (1,)])
    return units


def bits_index(value, count):
    return tuple(lax.rem(value // (1 << (count - 1 - k)), 2) for k in range(count))


def back_kernel(a, b, plan, unit_list, events, slot, lands, temper, *refs):
    bias_ref, q_ref, k_ref, v_ref, ctx_ref, lse_ref = refs[:6]
    active_ref, slope_ref, w2_ref, w1_ref = refs[6:10]
    xhat_ref, scale_ref, gain_ref, wide_ctx_ref, wo_ref = refs[10:15]
    x_ref, wq_ref, wk_ref, wv_ref = refs[15:19]
    vec_ref, grad_outer, normed_low, grad_second = refs[19:23]
    out_tokens, out_bias = refs[23:25]
    outs = refs[25:31]
    g_wo, g_w1, g_w2 = refs[31:34]
    rest = refs[34:]
    gq_s, gk_s, gv_s, sum_q, sum_k, sum_v, bias_s, tok_s, flow, lines, w2_st = rest[:11]
    send, recv, local, tok_send, tok_recv, tok_local, put = rest[11:18]
    rest = rest[18:]
    steps = a + b
    sources = {0: sum_q, 1: sum_k, 2: sum_v, 3: g_wo, 4: g_w1, 5: g_w2}
    chunks, units = [], []
    for unit in unit_list:
        ids = []
        for at, r, c, color in unit:
            ids.append(len(chunks))
            chunks.append((sources[at], outs[at], (r, c), color))
        units.append(ids)
    units[-1] = units[-1] + [len(chunks)]
    chunks.append((bias_s, out_bias, (slice(None), slice(None)), 0))
    landed = []
    for at, start, size in lands:
        refs_of = rest[at * steps : (at + 1) * steps]
        if size != refs_of[0].shape[-1]:
            refs_of = [
                r.at[(slice(None),) * (len(r.shape) - 1) + (pl.ds(start, size),)] for r in refs_of
            ]
        landed.append(refs_of)
    staged = rest[(1 + max(at for at, _, _ in lands)) * steps :]
    views = []
    for m, (k, start, size) in enumerate(slot):
        if k < 0:
            views.append(None)
            continue
        ref = staged[k]
        if size != ref.shape[-1]:
            ref = ref.at[(slice(None),) * steps + (pl.ds(start, size),)]
        views.append(ref)
    sums = Sums(a, b, chunks, landed, views, send, recv, local)
    place = sums.place
    i = pl.program_id(0)
    n, length, width = gq_s.shape
    sp = 1 << b
    part = length // sp
    rows = n * length
    hidden = span(plan, "hidden")[1]
    wide = wq_ref.shape[0]
    h = w1_ref.shape[1]

    loads = [
        pltpu.make_async_copy(grad_outer, gq_s, put.at[0]),
        pltpu.make_async_copy(normed_low, gk_s, put.at[1]),
        pltpu.make_async_copy(grad_second, flow, put.at[2]),
    ]

    @pl.when(i == 0)
    def _():
        for load in loads:
            load.start()
        place.greet()
        for load in loads:
            load.wait()
        lines[...] = jnp.zeros_like(lines)

    def token_moves(s):
        out = [pltpu.make_async_copy(tok_s.at[s, place.z], out_tokens.at[place.z, s], tok_local.at[s])]
        for k in range(1, sp):
            to = lax.rem(place.z + k, sp)
            out.append(
                pltpu.make_async_remote_copy(
                    src_ref=tok_s.at[s, to],
                    dst_ref=out_tokens.at[place.z, s],
                    send_sem=tok_send.at[s, k - 1],
                    recv_sem=tok_recv.at[s, k - 1],
                    device_id=(place.f, to),
                    device_id_type=MESH,
                )
            )
        return out

    def puts(j):
        at = lax.rem(j, 2)
        columns = pl.ds(pl.multiple_of(j * h, h), h)
        held = pl.ds(pl.multiple_of(at * h, h), h)
        to_w1 = g_w1.at[(slice(None),) * (steps + 1) + (columns,)]
        to_w2 = g_w2.at[bits_index(j, bits_of(hidden))]
        return [
            pltpu.make_async_copy(sum_q.at[(slice(None),) * (steps + 1) + (held,)], to_w1, put.at[3 + at]),
            pltpu.make_async_copy(w2_st.at[at], to_w2, put.at[5 + at]),
        ]

    @pl.when(i < hidden)
    def _():
        at = lax.rem(i, 2)
        grad_out = gq_s[...].reshape(rows, width)
        normed = gk_s[...].reshape(rows, width)
        grad_active = dot_nt(grad_out, w2_ref[...])
        grad_inner = (grad_active * slope_ref[...].astype(F32)).astype(BF)
        columns = pl.ds(pl.multiple_of(i * h, h), h)
        lines[0:1, columns] = jnp.sum(grad_inner.astype(F32), axis=0, keepdims=True)
        value = dot_tn(normed, grad_inner).astype(BF)
        sum_q[..., pl.ds(pl.multiple_of(at * h, h), h)] = value.reshape(sum_q.shape[:-1] + (h,))
        value = dot_tn(active_ref[...], grad_out).astype(BF)
        w2_st[at] = value.reshape(w2_st.shape[1:])
        for p in puts(i):
            p.start()
        flow[...] += dot_nt(grad_inner, w1_ref[...]).reshape(flow.shape)

        @pl.when(i > 0)
        def _():
            for p in puts(i - 1):
                p.wait()

    lo, hi = span(plan, "norm")

    @pl.when(i == lo)
    def _():
        for p in puts(hidden - 1):
            p.wait()

    @pl.when(jnp.logical_and(i >= lo, i < hi))
    def _():
        zb = i - lo
        for s in range(n):
            grad = flow[zb, s]
            xhat = xhat_ref[0, s].astype(F32)
            scaled = grad * gain_ref[...]
            mean = jnp.mean(scaled, axis=-1, keepdims=True)
            slope = jnp.mean(scaled * xhat, axis=-1, keepdims=True)
            first = scale_ref[0, s] * (scaled - mean - xhat * slope)
            flow[zb, s] = first
            low = first.astype(BF)
            tok_s[s, zb] = low
            for at, value in ((1, grad * xhat), (2, grad), (3, low.astype(F32))):
                lines[at : at + 1, :width] += jnp.sum(value, axis=0, keepdims=True)

    lo, hi = span(plan, "project")
    first_attend = hi
    put_wo = pltpu.make_async_copy(sum_v, g_wo, put.at[7])

    @pl.when(jnp.logical_and(i >= lo, i < hi))
    def _():
        r = i - lo
        columns = pl.ds(pl.multiple_of(r * wide, wide), wide)
        total = jnp.zeros((wide, width), F32)
        for s in range(n):
            grad = tok_s[s].reshape(length, width)
            gv_s[s, :, columns] = dot_nt(grad, wo_ref[...]).astype(BF)
            total = total + dot_tn(wide_ctx_ref[:, s].reshape(length, wide), grad)
        index = bits_index(r, bits_of(hi - lo))
        sum_v[index] = total.astype(BF).reshape(sum_v.shape[len(index) :])

        @pl.when(i == hi - 1)
        def _():
            put_wo.start()

    @pl.when(i == first_attend)
    def _():
        put_wo.wait()

    def attend_step(s, c):
        bias_rows = jnp.broadcast_to(bias_ref[...].reshape(1, length), (2 * HD, length))
        key_bias = jnp.transpose(bias_rows)[:, :1]
        for pair in range(wide // (2 * HD)):
            cut = slice(pair * 2 * HD, (pair + 1) * 2 * HD)
            columns = pl.ds(pl.multiple_of(c * wide + pair * 2 * HD, 2 * HD), 2 * HD)
            q, k, v, ctx = (r[:, 0, :, cut].reshape(length, 2 * HD) for r in (q_ref, k_ref, v_ref, ctx_ref))
            logs = lse_ref[0, pair, 0:2]
            gq, gk, gv = attend_back_pair(temper, key_bias, q, k, v, ctx, logs, gv_s[s, :, columns])
            gq_s[s, :, columns] = gq
            gk_s[s, :, columns] = gk
            gv_s[s, :, columns] = gv

    def weights_step(c):
        columns = pl.ds(pl.multiple_of(c * wide, wide), wide)
        for at, held, total in ((4, gq_s, sum_q), (None, gk_s, sum_k), (5, gv_s, sum_v)):
            value = sum(dot_tn(x_ref[:, s].reshape(length, width), held[s, :, columns]) for s in range(n))
            total[..., columns] = value.astype(BF).reshape(total.shape[:-1] + (wide,))
            if at is not None:
                row = sum(jnp.sum(held[s, :, columns].astype(F32), axis=0, keepdims=True) for s in range(n))
                lines[at : at + 1, columns] = row

    for s in range(n):
        lo, hi = span(plan, "attend" if s < n - 1 else "last", s)

        @pl.when(jnp.logical_and(i >= lo, i < hi))
        def _(s=s, lo=lo):
            attend_step(s, i - lo)
            if s == n - 1:
                weights_step(i - lo)

        lo, hi = span(plan, "tokens", s)

        @pl.when(jnp.logical_and(i >= lo, i < hi))
        def _(s=s, lo=lo, hi=hi):
            columns = pl.ds(pl.multiple_of((i - lo) * wide, wide), wide)
            total = dot_nt(gq_s[s], wq_ref[...]) + dot_nt(gk_s[s], wk_ref[...]) + dot_nt(gv_s[s], wv_ref[...])
            total = total + flow[:, s, :, columns].reshape(length, wide)
            tok_s[s, :, :, columns] = total.astype(BF).reshape(sp, part, wide)

            @pl.when(i == hi - 1)
            def _():
                for move in token_moves(s):
                    move.start()

    @pl.when(i == span(plan, "last")[1] - 1)
    def _():
        devices = 1 << steps
        for d in range(devices):
            index = tuple((d >> (steps - 1 - k)) & 1 for k in range(steps))
            for at in range(6):
                size = (hidden * h if at == 0 else width) // devices
                tile = d * size // 128
                bias_s[index + (slice(at, at + 1),)] = lines[at : at + 1, tile * 128 : tile * 128 + 128]
            bias_s[index + (slice(6, 7),)] = vec_ref[d : d + 1]

    for k in sorted({event[0] for event in events}):

        @pl.when(i == k)
        def _(k=k):
            for at, unit, s, load in events:
                if at == k:
                    sums.event(units[unit], s, units[load] if load >= 0 else ())

    @pl.when(i == len(plan) - 1)
    def _():
        for s in range(n):
            for move in token_moves(s):
                move.wait()


def back(a, b, bias, heads, lse, active, slope, W2, W1, xhat, scale, gain, WO, x, WQ, WK, WV, grads, vec):
    q, k, v, ctx = heads
    lead, steps = (2,) * (a + b), a + b
    s, n, t, width = q.shape
    devices = 1 << steps
    hidden, blocks = 8, 4
    h, wide, length, rows = W1.shape[1] // hidden, width // blocks, s * t, s * n * t
    plan = plan_steps(n, hidden, s, blocks)
    own_rows = width // devices
    shapes = [(own_rows, width)] * 4 + [(own_rows, W1.shape[1]), (W2.shape[0] // devices, width)]
    unit_list = sum_units(shapes, blocks)
    first, late = span(plan, "attend" if n > 1 else "last")[0], len(unit_list) - blocks
    ready = [2 * k + 2 for k in range(4)] + [hidden] * 4 + [first]
    ready += list(range(*span(plan, "last")))
    megabytes = [[(r.size * c.size * devices * 2 / MIB, color) for _, r, c, color in u] for u in unit_list]
    events = plan_events(plan, megabytes, ready, late, a, b)
    sizes = [(r.size, c.size) for unit in unit_list for _, r, c, _ in unit] + [(8, 128)]
    types = [BF] * (len(sizes) - 1) + [F32]
    loaded = [at > 2 for unit in unit_list for at, _, _, _ in unit] + [False]
    turn, last = 2 * blocks, n - 1

    def count_from(i, starts):
        return sum([(i >= start).astype(jnp.int32) for start in starts], jnp.int32(0))

    def at_kind(i, begin):
        off = i - begin
        seq = count_from(off, [k * turn for k in range(1, n)])
        return seq, jnp.clip(off - seq * turn, 0, blocks - 1)

    def at_head(i):
        return at_kind(i, first)

    def at_tokens(i):
        return at_kind(i, first + blocks)

    def head_map(i):
        seq, pair = at_head(i)
        return (0, seq, 0, pair)

    def lse_map(i):
        seq, pair = at_head(i)
        return (seq, pair, 0, 0)

    def block_of(kind):
        lo, hi = span(plan, kind)
        return lambda i: jnp.clip(i - lo, 0, hi - lo - 1)

    j_of, z_of, r_of = block_of("hidden"), block_of("norm"), block_of("project")
    head = pl.BlockSpec((s, 1, t, wide), head_map)
    weight = pl.BlockSpec((wide, width), lambda i: (at_tokens(i)[1], 0))
    anyspace = pl.BlockSpec(memory_space=pl.ANY)
    vmem = pl.BlockSpec(memory_space=pltpu.VMEM)
    in_specs = [pl.BlockSpec((1, 1, length), lambda i: (at_head(i)[0], 0, 0))] + [head] * 4
    in_specs += [pl.BlockSpec((1, wide // (2 * HD), 8, length), lse_map)]
    in_specs += [pl.BlockSpec((rows, h), lambda i: (0, j_of(i)))] * 2
    in_specs += [pl.BlockSpec((h, width), lambda i: (j_of(i), 0)), pl.BlockSpec((width, h), lambda i: (0, j_of(i)))]
    in_specs += [pl.BlockSpec((1, n, t, width), lambda i: (z_of(i), 0, 0, 0))]
    in_specs += [pl.BlockSpec((1, n, t, 1), lambda i: (z_of(i), 0, 0, 0))]
    in_specs += [pl.BlockSpec((1, width), lambda i: (0, 0))]
    in_specs += [pl.BlockSpec((s, n, t, wide), lambda i: (0, 0, 0, r_of(i)))]
    in_specs += [pl.BlockSpec((wide, width), lambda i: (r_of(i), 0))]
    in_specs += [pl.BlockSpec(x.shape, lambda i: (0, 0, 0, 0), pipeline_mode=pl.Buffered(1))]
    in_specs += [weight] * 3 + [pl.BlockSpec(vec.shape, lambda i: (0, 0))] + [anyspace] * 3
    outs = [jax.ShapeDtypeStruct((s, n, t, width), BF)]
    outs += [jax.ShapeDtypeStruct(sizes[-1], F32)]
    outs += [jax.ShapeDtypeStruct(shape, F32) for shape in shapes]
    outs += [jax.ShapeDtypeStruct(lead + shapes[m], BF) for m in (3, 4, 5)]
    n_chunks = len(sizes)
    scratch = [pltpu.VMEM((n, length, width), BF)] * 3
    scratch += [pltpu.VMEM(lead + (own_rows, width), BF)] * 3
    scratch += [pltpu.VMEM(lead + sizes[-1], F32), pltpu.VMEM((n, s, t, width), BF)]
    scratch += [pltpu.VMEM((s, n, t, width), F32), pltpu.VMEM((8, W1.shape[1]), F32)]
    scratch += [pltpu.VMEM((2,) + (2,) * (steps - bits_of(hidden)) + shapes[5], BF)]
    scratch += [
        pltpu.SemaphoreType.DMA((n_chunks, steps)),
        pltpu.SemaphoreType.DMA((n_chunks, steps)),
        pltpu.SemaphoreType.DMA((n_chunks,)),
        pltpu.SemaphoreType.DMA((n, s - 1)),
        pltpu.SemaphoreType.DMA((n, s - 1)),
        pltpu.SemaphoreType.DMA((n,)),
        pltpu.SemaphoreType.DMA((8,)),
    ]
    ids, at = [], 0
    for unit in unit_list:
        ids.append(list(range(at, at + len(unit))))
        at += len(unit)
    ids[-1] = ids[-1] + [at]
    slot, keys = staging_plan(sizes, types, ids, loaded)
    lands, held = [None] * len(sizes), []
    for u, unit in enumerate(ids):
        used = {}
        for m in unit:
            if u >= late and m < len(sizes) - 1:
                color = [chunk for each in unit_list for chunk in each][m][3]
                lands[m] = (lands[ids[u - late][color]][0], used.get(color, 0), sizes[m][1])
                used[color] = used.get(color, 0) + sizes[m][1]
            else:
                lands[m] = (len(held), 0, sizes[m][1])
                held.append((sizes[m], types[m]))
    for size, kind in held:
        scratch += [pltpu.VMEM((2,) * (steps - 1 - j) + size, kind) for j in range(steps)]
    scratch += [pltpu.VMEM((2,) * (steps - 1) + (r, c), kind) for r, c, kind in keys]
    grad_outer, normed_low, grad_second = grads
    return pl.pallas_call(
        functools.partial(back_kernel, a, b, plan, unit_list, events, slot, lands, 1.0 / math.sqrt(HD)),
        grid=(len(plan),),
        out_shape=outs,
        in_specs=in_specs,
        out_specs=[anyspace] + [vmem] * 7 + [anyspace] * 3,
        scratch_shapes=scratch,
        compiler_params=pltpu.CompilerParams(
            collective_id=1, has_side_effects=True, vmem_limit_bytes=63 * MIB + MIB * 5 // 8
        ),
        name="back_and_sum",
    )(
        bias,
        q,
        k,
        v,
        ctx,
        lse,
        active,
        slope,
        W2,
        W1,
        xhat,
        scale,
        gain,
        ctx,
        WO,
        x,
        WQ,
        WK,
        WV,
        vec,
        grad_outer,
        normed_low,
        grad_second,
    )


def norm_forward(hidden, gain, shift):
    average = jnp.mean(hidden, axis=-1, keepdims=True)
    centred = hidden - average
    scale = lax.rsqrt(jnp.mean(centred * centred, axis=-1, keepdims=True) + 1e-12)
    xhat = centred * scale
    return xhat * gain + shift, xhat, scale


def norm_backward(grad, gain, xhat, scale):
    scaled = grad * gain
    lead = jnp.mean(scaled, axis=-1, keepdims=True)
    slope = jnp.mean(scaled * xhat, axis=-1, keepdims=True)
    return scale * (scaled - lead - xhat * slope)


def gelu_pair(x):
    cdf = 0.5 * (1.0 + lax.erf(x * (1.0 / math.sqrt(2.0))))
    pdf = jnp.exp(-0.5 * x * x) * (1.0 / math.sqrt(2.0 * math.pi))
    return x * cdf, cdf + x * pdf


def body(tokens, validity, teacher, wq, bq, wk, wv, bv, wo, bo, gain1, shift1, w1, b1, w2, b2, gain2, shift2):
    fs, sp = lax.axis_size("fsdp"), lax.axis_size("sp")
    a, b = bits_of(fs), bits_of(sp)
    devices = fs * sp
    seqs, part, width = tokens.shape
    n = seqs // sp
    length = part * sp
    rows = sp * n * part
    total_tokens = rows * devices
    z = lax.axis_index("sp")
    shard_shape = (sp, n, part, width)

    mine = lax.dynamic_slice_in_dim(validity, z * n, n, 0)
    count = jnp.sum(mine)
    vectors = (bq, bv, bo, gain1, shift1, b2, gain2, shift2, b1)
    sizes = [v.shape[0] for v in vectors]
    lines = [jnp.pad(v.reshape(1, -1), ((0, 0), (0, 128 - v.shape[0]))) for v in vectors]
    lane = lax.broadcasted_iota(jnp.int32, (1, 128), 1)
    lines.append(jnp.where(lane == 0, count // 32, count % 32).astype(BF))
    row = lax.broadcasted_iota(jnp.int32, (16, 128), 0)
    vec = jnp.zeros((16, 128), BF)
    for at, line in enumerate(lines):
        vec = jnp.where(row == at, line, vec)

    shards = (wq, wk, wv, wo, w1, w2)
    got = front(a, b, tokens.reshape(shard_shape), vec, shards)
    moved, vec_all = got[0], got[1].reshape(devices, 16, 128)
    WQ, WK, WV, WO, W1, W2 = (
        g.reshape((devices * w.shape[0],) + w.shape[1:]) for g, w in zip(got[2:], shards)
    )
    full = [vec_all[:, at, :size].reshape(-1).astype(F32) for at, size in enumerate(sizes)]
    BQ, BV, BO, G1, S1, B2, G2, S2, B1 = full
    counts = vec_all[:, len(sizes), :2].astype(F32)
    counted = jnp.sum(counts[:, 0]) * 32.0 + jnp.sum(counts[:, 1])

    teacher_moved = lax.all_to_all(
        lax.optimization_barrier((teacher, moved))[0].reshape(shard_shape), "sp", split_axis=0, concat_axis=0
    ).reshape(rows, width)

    valid = mine.astype(F32)
    bias = ((valid - 1.0) * 1e9).reshape(n, 1, length)
    mask_rows = jnp.swapaxes(valid.reshape(n, sp, part), 0, 1).reshape(rows, 1)

    x = moved.reshape(rows, width)
    q = (dot_nn(x, WQ) + BQ).astype(BF)
    k = dot_nn(x, WK).astype(BF)
    v = (dot_nn(x, WV) + BV).astype(BF)
    ctx, lse = attend(bias, *(p.reshape(shard_shape) for p in (q, k, v)))
    ctx_rows = ctx.reshape(rows, width)
    first = x.astype(F32) + dot_nn(ctx_rows, WO) + BO
    normed, xhat1, scale1 = norm_forward(first, G1, S1)
    normed_low = normed.astype(BF)
    inner = dot_nn(normed_low, W1) + B1
    active, slope = gelu_pair(inner)
    active_low = active.astype(BF)
    slope = slope.astype(BF)
    second = normed + dot_nn(active_low, W2) + B2
    final, xhat2, scale2 = norm_forward(second, G2, S2)
    error = final - teacher_moved.astype(F32)
    local_loss = jnp.sum(mask_rows * error * error)
    output = lax.all_to_all(final.astype(BF).reshape(shard_shape), "sp", split_axis=0, concat_axis=0)

    grad_final = (2.0 * total_tokens / counted) * mask_rows * error
    grad_second = norm_backward(grad_final, G2, xhat2, scale2)
    grad_outer = grad_second.astype(BF)

    def column_sum(value):
        return jnp.sum(value.astype(F32), axis=0)

    vector_grads = (column_sum(grad_outer), jnp.sum(grad_final * xhat2, axis=0), column_sum(grad_final))
    parts = [g.reshape(devices, -1) for g in vector_grads]
    parts.append(jnp.broadcast_to(local_loss, (devices, 1)))
    packed = jnp.concatenate(parts, axis=1)
    packed = jnp.pad(packed, ((0, 0), (0, 128 - packed.shape[1])))
    by_rows = (n, length, width)
    summed = back(
        a,
        b,
        bias,
        [p.reshape(shard_shape) for p in (q, k, v)] + [ctx],
        lse,
        active_low,
        slope,
        W2,
        W1,
        xhat1.astype(BF).reshape(shard_shape),
        scale1.reshape(sp, n, part, 1),
        G1.reshape(1, width),
        WO,
        moved,
        WQ,
        WK,
        WV,
        [grad_outer.reshape(by_rows), normed_low.reshape(by_rows), grad_second.reshape(shard_shape)],
        packed,
    )
    home = summed[0].reshape(seqs, part, width).astype(F32)
    own = summed[1][6]
    small, at = [], 0
    for g in vector_grads:
        size = g.shape[0] // devices
        small.append(own[at : at + size])
        at += size
    loss = own[at] / (width * counted)
    d_b2, d_g2, d_s2 = small
    me = lax.axis_index("fsdp") * sp + z
    tiles = []
    for at, size in enumerate((sizes[8],) + (width // devices,) * 5):
        tiles.append(lax.dynamic_slice_in_dim(summed[1][at], lax.rem(me * size, 128), size, 0))
    d_b1, d_g1, d_s1, d_bo, d_bq, d_bv = tiles
    d_wq, d_wk, d_wv, d_wo, d_w1, d_w2 = summed[2:8]
    return (
        output.reshape(seqs, part, width),
        loss,
        home,
        d_wq,
        d_bq,
        d_wk,
        d_wv,
        d_bv,
        d_wo,
        d_bo,
        d_g1,
        d_s1,
        d_w1,
        d_b1,
        d_w2,
        d_b2,
        d_g2,
        d_s2,
    )


def solution(mesh):
    tokens = P("fsdp", "sp", None)
    matrix = P(AXES, None)
    vector = P(AXES)
    return jax.shard_map(
        body,
        mesh=mesh,
        in_specs=(
            tokens,
            P("fsdp", None),
            tokens,
            matrix,
            vector,
            matrix,
            matrix,
            vector,
            matrix,
            vector,
            vector,
            vector,
            matrix,
            vector,
            matrix,
            vector,
            vector,
            vector,
        ),
        out_specs=(
            tokens,
            P(),
            tokens,
            matrix,
            vector,
            matrix,
            matrix,
            vector,
            matrix,
            vector,
            vector,
            vector,
            matrix,
            vector,
            matrix,
            vector,
            vector,
            vector,
        ),
        check_vma=False,
    )
```
